32 devices in a mesh: grp: 2 (over x), seq: 16 (over z, y, core).
Axes of the slice: x: 2, y: 2, z: 4, core: 2. Of those that a mesh axis runs over, the one named last changes fastest.
Arguments:
- inputs: bfloat16 [4096, 4096], P(('grp', 'seq')), parts along dimension 0, may hold values from -6 to 6
- in_weight: bfloat16 [4096, 768], replicated, may hold values from -0.09375 to 0.09375
- filter_taps: float32 [2048, 256], P('seq'), may hold values from -6 to 6
- grad_out: bfloat16 [4096, 256], P(('grp', 'seq')), parts along dimension 0, may hold values from -6 to 6
Outputs:
- grad_inputs: bfloat16 [4096, 4096], P(('grp', 'seq')), parts along dimension 0
- grad_weight: float32 [8192, 768], P(('grp', 'seq')), parts along dimension 0
- grad_taps: float32 [4096, 256], P(('grp', 'seq')), parts along dimension 0
The draws below stay inside these ranges and needn't reach their ends.
There are 2 independent parts, one for each index of `grp`. The reference program is written for one: setup_inputs(seed, part) draws one part's arguments, and reference() takes and returns one part's arrays. A program takes and returns all parts, laid end to end along the dimension named above; an argument that names none is the same for every part. Nothing has to cross between parts.
All inputs are finite; a program needn't handle non-finite values.
Results may differ from the reference program's by a relative error of at most 0.0064.
Values sent between devices are 32-bit elements; how exact they have to be, the bound alone decides.
No kernel may reach another device: no remote copies, remote signals or barrier semaphores. Data moves between devices by JAX's collectives and lax.ppermute only.
A program may use at most 128 MiB of HBM per device.

```python
import math
import jax
import jax.numpy as jnp
from jax import lax

D = 4096
CH = 256
SEQ = 2048


def raised(result, stream_key, source, target, parts, factor):
    def block_of(axis_at):
        return (jnp.arange(result.shape[axis_at]) // (result.shape[axis_at] // parts)).reshape((-1,) + (1,) * (result.ndim - 1 - axis_at))

    first = jax.random.permutation(stream_key, parts)[block_of(target)]
    second = (block_of(target) + parts // 2) % parts
    return jnp.where((block_of(source) == first) | (block_of(source) == second), factor * result, result)


def shard_levels(stream_key, dims, cuts, smallest, high):
    gain = 1.0
    for position, parts in cuts:
        steps = jax.random.uniform(jax.random.fold_in(jax.random.fold_in(stream_key, 6), position), (parts,), jnp.float32, smallest / len(cuts), high / len(cuts))
        gain = gain * jnp.repeat(jnp.exp(steps), dims[position] // parts).reshape((-1,) + (1,) * (len(dims) - 1 - position))
    return gain


def normal_values(own_key, shape, width, limit, split=(), kind=jnp.bfloat16):
    level = shard_levels(own_key, shape, split, -0.22, 0.18) if split else 1.0
    drawn = jax.random.normal(own_key, shape, jnp.float32) * width * level
    return jnp.minimum(jnp.maximum(drawn, -limit), limit).astype(kind)


def heavy_noise(own_key, shape, spread, bound, split, heavy, kind=jnp.bfloat16):
    drawn = spread * jax.random.normal(own_key, shape, jnp.float32)
    if split:
        drawn = drawn * shard_levels(own_key, shape, split, -0.22, 0.18)
    return jnp.clip(raised(drawn, jax.random.fold_in(own_key, 3), *heavy), -bound, bound).astype(kind)


def setup_inputs(seed: int = 0, part: int = 0) -> dict:
    seeds = jax.random.split(jax.random.key(seed), 5)
    part_keys = jax.random.split(jax.random.fold_in(seeds[4], part), 5)
    inputs = heavy_noise(part_keys[0], (SEQ, D), 1.0, 6.0, ((0, 16),), (0, 1, 16, 2.0))
    in_weight = normal_values(seeds[1], (D, 3 * CH), D ** -0.5, 0.09375)
    filter_taps = normal_values(seeds[2], (SEQ, CH), 1.0, 6.0, ((0, 16),), jnp.float32)
    grad_out = normal_values(part_keys[3], (SEQ, CH), 1.0, 6.0, ((0, 16),))
    return {"inputs": inputs, "in_weight": in_weight, "filter_taps": filter_taps, "grad_out": grad_out}


def reference(inputs, in_weight, filter_taps, grad_out):
    seqlen = inputs.shape[0]
    channels = filter_taps.shape[1]
    scaling = 1.0 / math.sqrt(seqlen)
    projected = jnp.dot(inputs, in_weight, preferred_element_type=jnp.float32).astype(jnp.bfloat16)
    query_rows = projected[:, :channels].astype(jnp.float32)
    key_rows = projected[:, channels:2 * channels].astype(jnp.float32)
    value_rows = projected[:, 2 * channels:].astype(jnp.float32)
    gated_input = key_rows * value_rows
    kernel = filter_taps * scaling
    back_grad = grad_out.astype(jnp.float32) * query_rows
    fft_length = 2 * seqlen
    kernel_spec = jnp.fft.rfft(kernel, n=fft_length, axis=0)
    gated_spec = jnp.fft.rfft(gated_input, n=fft_length, axis=0)
    back_spec = jnp.fft.rfft(back_grad, n=fft_length, axis=0)
    mixed_rows = jnp.fft.irfft(kernel_spec * gated_spec, n=fft_length, axis=0)[:seqlen]
    back_conv = jnp.fft.irfft(jnp.conj(kernel_spec) * back_spec, n=fft_length, axis=0)[:seqlen]
    grad_taps = jnp.fft.irfft(back_spec * jnp.conj(gated_spec), n=fft_length, axis=0)[:seqlen] * scaling
    grad_proj = jnp.concatenate([grad_out.astype(jnp.float32) * mixed_rows, back_conv * value_rows, back_conv * key_rows], axis=1).astype(jnp.bfloat16)
    grad_inputs = lax.dot_general(grad_proj, in_weight, (((1,), (1,)), ((), ())), preferred_element_type=jnp.float32).astype(jnp.bfloat16)
    grad_weight = lax.dot_general(inputs, grad_proj, (((0,), (0,)), ((), ())), preferred_element_type=jnp.float32) * scaling
    return (grad_inputs, grad_weight, grad_taps.astype(jnp.float32))
```

```python
import functools
import math

import jax
import jax.numpy as jnp
import numpy as np
from jax import lax
from jax.experimental import pallas as pl
from jax.experimental.pallas import tpu as pltpu
from jax.sharding import PartitionSpec as P

VMEM_LIMIT = 48 * 1024 * 1024


def split_pair(table):
    high = table.astype(np.float32).astype(jnp.bfloat16)
    low = (table - high.astype(np.float64)).astype(np.float32).astype(jnp.bfloat16)
    return high, low


def transform_tables(blocks, width, rows):
    length = 2 * blocks * rows
    kept = blocks + 1
    padded = -(-kept * width // 16) * 16
    k1 = np.arange(kept)
    block = np.arange(blocks)
    angle = 2.0 * np.pi * ((k1[:, None] * block[None, :]) % (2 * blocks)) / (2 * blocks)
    eye = np.eye(width)

    def spread(matrix):
        wide = np.kron(matrix, eye)
        return np.pad(wide, ((0, padded - wide.shape[0]), (0, 0)))

    mix = np.concatenate([spread(np.cos(angle)), spread(-np.sin(angle))], axis=0)
    weight = np.where((k1 == 0) | (k1 == blocks), 1.0, 2.0)[:, None] / length
    unmix = np.concatenate(
        [spread(weight * np.cos(angle)), spread(-weight * np.sin(angle))], axis=0
    ).T
    row = np.arange(rows)
    turn = 2.0 * np.pi * ((k1[:, None] * row[None, :]) % length) / length
    turn = np.pad(np.repeat(turn, width, axis=0), ((0, padded - kept * width), (0, 0)))
    inner = 2.0 * np.pi * ((row[:, None] * row[None, :]) % rows) / rows
    cos, sin = np.cos(inner), np.sin(inner)
    forward = np.block([[cos, -sin], [sin, cos]])
    inverse = np.block([[cos, sin], [-sin, cos]])
    tables = split_pair(mix) + (np.cos(turn).astype(np.float32), np.sin(turn).astype(np.float32))
    return tables + split_pair(forward) + split_pair(inverse) + split_pair(unmix)


def halves(value):
    high = value.astype(jnp.bfloat16)
    return high, (value - high.astype(jnp.float32)).astype(jnp.bfloat16)


def dot32(left, right):
    (lh, ll), (rh, rl) = left, right
    dot = functools.partial(jnp.dot, preferred_element_type=jnp.float32)
    return dot(lh, rh) + (dot(lh, rl) + dot(ll, rh))


def project_kernel(scaling, x_ref, w_ref, taps_ref, go_ref, moved_ref, sig_ref, kv_ref, acc):
    step = pl.program_id(0)
    block = x_ref[...]
    product = jnp.dot(block, w_ref[...], preferred_element_type=jnp.float32)

    @pl.when(step == 0)
    def _():
        acc[...] = product

    @pl.when(step > 0)
    def _():
        acc[...] += product

    owners = moved_ref.shape[0]
    part = moved_ref.shape[2]
    for owner in range(owners):
        moved_ref[owner] = block[:, owner * part : (owner + 1) * part].astype(jnp.float32)

    @pl.when(step == pl.num_programs(0) - 1)
    def _():
        count, _, width, _ = sig_ref.shape
        channels = count * width
        projected = acc[...].astype(jnp.bfloat16).astype(jnp.float32).T
        query = projected[:channels]
        key = projected[channels : 2 * channels]
        value = projected[2 * channels :]
        go = go_ref[...].astype(jnp.float32).T
        signals = ((taps_ref[...] * scaling).T, key * value, go * query)
        for which, signal in enumerate(signals):
            for owner in range(count):
                sig_ref[owner, which] = signal[owner * width : (owner + 1) * width]
        kv_ref[0] = go
        kv_ref[1] = value
        kv_ref[2] = key


def conv_kernel(
    x_ref, m_h, m_l, t_re, t_im, f_h, f_l, i_h, i_l, u_h, u_l, y_ref, flat
):
    blocks, _, width, rows = x_ref.shape
    for p in range(blocks):
        for s in range(3):
            flat[p * width : (p + 1) * width, s * rows : (s + 1) * rows] = x_ref[p, s]
    turn_re, turn_im = t_re[...], t_im[...]
    count = turn_re.shape[0]
    mixed = dot32((m_h[...], m_l[...]), halves(flat[...]))
    turned = []
    for s in range(3):
        re = mixed[:count, s * rows : (s + 1) * rows]
        im = mixed[count:, s * rows : (s + 1) * rows]
        turned.append(
            jnp.concatenate([re * turn_re + im * turn_im, im * turn_re - re * turn_im], axis=1)
        )
    spectrum = dot32(halves(jnp.concatenate(turned, axis=0)), (f_h[...], f_l[...]))
    (k_re, k_im), (g_re, g_im), (b_re, b_im) = [
        (spectrum[s * count : (s + 1) * count, :rows], spectrum[s * count : (s + 1) * count, rows:])
        for s in range(3)
    ]
    products = jnp.concatenate(
        [
            jnp.concatenate([k_re * g_re - k_im * g_im, k_re * g_im + k_im * g_re], axis=1),
            jnp.concatenate([k_re * b_re + k_im * b_im, k_re * b_im - k_im * b_re], axis=1),
            jnp.concatenate([b_re * g_re + b_im * g_im, b_im * g_re - b_re * g_im], axis=1),
        ],
        axis=0,
    )
    back = dot32(halves(products), (i_h[...], i_l[...]))
    parts_re, parts_im = [], []
    for s in range(3):
        re = back[s * count : (s + 1) * count, :rows]
        im = back[s * count : (s + 1) * count, rows:]
        parts_re.append(re * turn_re - im * turn_im)
        parts_im.append(im * turn_re + re * turn_im)
    stacked = jnp.concatenate(
        [jnp.concatenate(parts_re, axis=1), jnp.concatenate(parts_im, axis=1)], axis=0
    )
    result = dot32((u_h[...], u_l[...]), halves(stacked))
    for p in range(blocks):
        for s in range(3):
            y_ref[p, s] = result[p * width : (p + 1) * width, s * rows : (s + 1) * rows]


def gate_kernel(scaling, y_ref, kv_ref, gp_ref, sent_ref, taps_ref, flat):
    count, _, width, _ = y_ref.shape
    channels = count * width
    for s in range(3):
        for owner in range(count):
            flat[s, owner * width : (owner + 1) * width] = y_ref[owner, s]
    back = flat[1]
    for index, value in enumerate((kv_ref[0] * flat[0], kv_ref[1] * back, kv_ref[2] * back)):
        rounded = value.T.astype(jnp.bfloat16)
        gp_ref[:, index * channels : (index + 1) * channels] = rounded
        sent_ref[:, index * channels : (index + 1) * channels] = rounded.astype(jnp.float32)
    taps_ref[...] = flat[2].T * scaling


def weight_kernel(scaling, x_ref, gp_ref, out_ref, acc):
    step = pl.program_id(0)
    product = lax.dot_general(
        x_ref[0].astype(jnp.bfloat16),
        gp_ref[0].astype(jnp.bfloat16),
        (((0,), (0,)), ((), ())),
        preferred_element_type=jnp.float32,
    )

    @pl.when(step == 0)
    def _():
        acc[...] = product

    @pl.when(step > 0)
    def _():
        acc[...] += product

    @pl.when(step == pl.num_programs(0) - 1)
    def _():
        out_ref[...] = acc[...] * scaling


def per_device(inputs, in_weight, filter_taps, grad_out):
    rows, depth = inputs.shape
    channels = filter_taps.shape[1]
    columns = in_weight.shape[1]
    blocks = lax.axis_size("seq")
    width = channels // blocks
    part = depth // blocks
    scaling = 1.0 / math.sqrt(rows * blocks)
    f32 = jnp.float32
    params = pltpu.CompilerParams(vmem_limit_bytes=VMEM_LIMIT)
    steps = 8
    chunk = depth // steps
    owners = blocks // steps
    moved, signals, gates = pl.pallas_call(
        functools.partial(project_kernel, scaling),
        grid=(steps,),
        in_specs=[
            pl.BlockSpec((rows, chunk), lambda i: (0, i)),
            pl.BlockSpec((chunk, columns), lambda i: (i, 0)),
            pl.BlockSpec((rows, channels), lambda i: (0, 0)),
            pl.BlockSpec((rows, channels), lambda i: (0, 0)),
        ],
        out_specs=[
            pl.BlockSpec((owners, rows, part), lambda i: (i, 0, 0)),
            pl.BlockSpec((blocks, 3, width, rows), lambda i: (0, 0, 0, 0)),
            pl.BlockSpec((3, channels, rows), lambda i: (0, 0, 0)),
        ],
        out_shape=[
            jax.ShapeDtypeStruct((blocks, rows, part), f32),
            jax.ShapeDtypeStruct((blocks, 3, width, rows), f32),
            jax.ShapeDtypeStruct((3, channels, rows), f32),
        ],
        scratch_shapes=[pltpu.VMEM((rows, columns), f32)],
        compiler_params=params,
    )(inputs, in_weight, filter_taps, grad_out)

    signals = lax.all_to_all(signals, "seq", split_axis=0, concat_axis=0, tiled=True)
    held = lax.all_to_all(moved, "seq", split_axis=0, concat_axis=0, tiled=True)
    tables = [jnp.asarray(table) for table in transform_tables(blocks, width, rows)]
    results = pl.pallas_call(
        conv_kernel,
        out_shape=jax.ShapeDtypeStruct((blocks, 3, width, rows), f32),
        scratch_shapes=[pltpu.VMEM((blocks * width, 3 * rows), f32)],
        compiler_params=params,
    )(signals, *tables)
    results = lax.all_to_all(results, "seq", split_axis=0, concat_axis=0, tiled=True)
    grad_proj, sent, grad_taps = pl.pallas_call(
        functools.partial(gate_kernel, scaling),
        out_shape=[
            jax.ShapeDtypeStruct((rows, columns), jnp.bfloat16),
            jax.ShapeDtypeStruct((rows, columns), f32),
            jax.ShapeDtypeStruct((rows, channels), f32),
        ],
        scratch_shapes=[pltpu.VMEM((3, channels, rows), f32)],
        compiler_params=params,
    )(results, gates)
    everyone = lax.all_gather(sent, "seq", axis=0)
    grad_inputs = lax.dot_general(
        grad_proj, in_weight, (((1,), (1,)), ((), ())), preferred_element_type=f32
    ).astype(jnp.bfloat16)
    grad_weight = pl.pallas_call(
        functools.partial(weight_kernel, scaling),
        grid=(blocks,),
        in_specs=[
            pl.BlockSpec((1, rows, part), lambda i: (i, 0, 0)),
            pl.BlockSpec((1, rows, columns), lambda i: (i, 0, 0)),
        ],
        out_specs=pl.BlockSpec((part, columns), lambda i: (0, 0)),
        out_shape=jax.ShapeDtypeStruct((part, columns), f32),
        scratch_shapes=[pltpu.VMEM((part, columns), f32)],
        compiler_params=params,
    )(held, everyone)
    return grad_inputs, grad_weight, grad_taps


def solution(mesh):
    in_specs = (P(("grp", "seq"), None), P(), P("seq", None), P(("grp", "seq"), None))
    out_specs = (P(("grp", "seq"), None), P(("grp", "seq"), None), P(("grp", "seq"), None))
    return jax.shard_map(
        per_device, mesh=mesh, in_specs=in_specs, out_specs=out_specs, check_vma=False
    )
```

```python
import functools
import math

import jax
import jax.numpy as jnp
import numpy as np
from jax import lax
from jax.experimental import pallas as pl
from jax.experimental.pallas import tpu as pltpu
from jax.sharding import PartitionSpec as P

VMEM_LIMIT = 48 * 1024 * 1024
SIDE = 4


def split_pair(table):
    high = table.astype(np.float32).astype(jnp.bfloat16)
    low = (table - high.astype(np.float64)).astype(np.float32).astype(jnp.bfloat16)
    return high, low


def transform_tables(blocks, width, rows):
    length = 2 * blocks * rows
    kept = blocks + 1
    padded = -(-kept * width // 16) * 16
    k1 = np.arange(kept)
    block = np.arange(blocks)
    angle = 2.0 * np.pi * ((k1[:, None] * block[None, :]) % (2 * blocks)) / (2 * blocks)
    eye = np.eye(width)

    def spread(matrix):
        wide = np.kron(matrix, eye)
        return np.pad(wide, ((0, padded - wide.shape[0]), (0, 0)))

    mix = np.concatenate([spread(np.cos(angle)), spread(-np.sin(angle))], axis=0)
    weight = np.where((k1 == 0) | (k1 == blocks), 1.0, 2.0)[:, None] / length
    unmix = np.concatenate(
        [spread(weight * np.cos(angle)), spread(-weight * np.sin(angle))], axis=0
    ).T
    row = np.arange(rows)
    turn = 2.0 * np.pi * ((k1[:, None] * row[None, :]) % length) / length
    turn = np.pad(np.repeat(turn, width, axis=0), ((0, padded - kept * width), (0, 0)))
    inner = 2.0 * np.pi * ((row[:, None] * row[None, :]) % rows) / rows
    cos, sin = np.cos(inner), np.sin(inner)
    forward = np.block([[cos, -sin], [sin, cos]])
    inverse = np.block([[cos, sin], [-sin, cos]])
    tables = split_pair(mix) + (np.cos(turn).astype(np.float32), np.sin(turn).astype(np.float32))
    return tables + split_pair(forward) + split_pair(inverse) + split_pair(unmix)


def halves(value):
    high = value.astype(jnp.bfloat16)
    return high, (value - high.astype(jnp.float32)).astype(jnp.bfloat16)


def dot32(left, right):
    (lh, ll), (rh, rl) = left, right
    dot = functools.partial(jnp.dot, preferred_element_type=jnp.float32)
    return dot(lh, rh) + (dot(lh, rl) + dot(ll, rh))


def project_kernel(scaling, place_ref, x_ref, w_ref, taps_ref, go_ref, *refs):
    moved_refs, (sig_ref, kv_ref, acc) = refs[:SIDE], refs[SIDE:]
    step = pl.program_id(0)
    block = x_ref[...]
    product = jnp.dot(block, w_ref[...], preferred_element_type=jnp.float32)

    @pl.when(step == 0)
    def _():
        acc[...] = product

    @pl.when(step > 0)
    def _():
        acc[...] += product

    part = moved_refs[0].shape[3]
    core = place_ref[2]
    units = block.shape[1] // (2 * part)
    for unit in range(units):
        chip = step * units + unit
        far = (chip // SIDE) ^ place_ref[0]
        near = (chip % SIDE) ^ place_ref[1]
        for which, moved_ref in enumerate(moved_refs):

            @pl.when(near == which)
            def _():
                for c in range(2):
                    first = (2 * unit + c) * part
                    moved_ref[far, core ^ c] = block[:, first : first + part].astype(jnp.float32)

    @pl.when(step == pl.num_programs(0) - 1)
    def _():
        count, _, width, _ = sig_ref.shape
        channels = count * width
        projected = acc[...].astype(jnp.bfloat16).astype(jnp.float32).T
        query = projected[:channels]
        key = projected[channels : 2 * channels]
        value = projected[2 * channels :]
        go = go_ref[...].astype(jnp.float32).T
        signals = ((taps_ref[...] * scaling).T, key * value, go * query)
        for which, signal in enumerate(signals):
            for owner in range(count):
                sig_ref[owner, which] = signal[owner * width : (owner + 1) * width]
        kv_ref[0] = go
        kv_ref[1] = value
        kv_ref[2] = key


def conv_kernel(
    x_ref, m_h, m_l, t_re, t_im, f_h, f_l, i_h, i_l, u_h, u_l, y_ref, flat
):
    blocks, _, width, rows = x_ref.shape
    for p in range(blocks):
        for s in range(3):
            flat[p * width : (p + 1) * width, s * rows : (s + 1) * rows] = x_ref[p, s]
    turn_re, turn_im = t_re[...], t_im[...]
    count = turn_re.shape[0]
    mixed = dot32((m_h[...], m_l[...]), halves(flat[...]))
    turned = []
    for s in range(3):
        re = mixed[:count, s * rows : (s + 1) * rows]
        im = mixed[count:, s * rows : (s + 1) * rows]
        turned.append(
            jnp.concatenate([re * turn_re + im * turn_im, im * turn_re - re * turn_im], axis=1)
        )
    spectrum = dot32(halves(jnp.concatenate(turned, axis=0)), (f_h[...], f_l[...]))
    (k_re, k_im), (g_re, g_im), (b_re, b_im) = [
        (spectrum[s * count : (s + 1) * count, :rows], spectrum[s * count : (s + 1) * count, rows:])
        for s in range(3)
    ]
    products = jnp.concatenate(
        [
            jnp.concatenate([k_re * g_re - k_im * g_im, k_re * g_im + k_im * g_re], axis=1),
            jnp.concatenate([k_re * b_re + k_im * b_im, k_re * b_im - k_im * b_re], axis=1),
            jnp.concatenate([b_re * g_re + b_im * g_im, b_im * g_re - b_re * g_im], axis=1),
        ],
        axis=0,
    )
    back = dot32(halves(products), (i_h[...], i_l[...]))
    parts_re, parts_im = [], []
    for s in range(3):
        re = back[s * count : (s + 1) * count, :rows]
        im = back[s * count : (s + 1) * count, rows:]
        parts_re.append(re * turn_re - im * turn_im)
        parts_im.append(im * turn_re + re * turn_im)
    stacked = jnp.concatenate(
        [jnp.concatenate(parts_re, axis=1), jnp.concatenate(parts_im, axis=1)], axis=0
    )
    result = dot32((u_h[...], u_l[...]), halves(stacked))
    for p in range(blocks):
        for s in range(3):
            y_ref[p, s] = result[p * width : (p + 1) * width, s * rows : (s + 1) * rows]


def gate_kernel(scaling, y_ref, kv_ref, gp_ref, sent_ref, taps_ref, flat):
    count, _, width, _ = y_ref.shape
    channels = count * width
    for s in range(3):
        for owner in range(count):
            flat[s, owner * width : (owner + 1) * width] = y_ref[owner, s]
    back = flat[1]
    for index, value in enumerate((kv_ref[0] * flat[0], kv_ref[1] * back, kv_ref[2] * back)):
        rounded = value.T.astype(jnp.bfloat16)
        gp_ref[:, index * channels : (index + 1) * channels] = rounded
        sent_ref[:, index * channels : (index + 1) * channels] = rounded.astype(jnp.float32)
    taps_ref[...] = flat[2].T * scaling


def turn_kernel(*refs):
    x_refs, out_refs = refs[:SIDE], refs[SIDE:]
    far, _, rows, part = x_refs[0].shape
    for which, x_ref in enumerate(x_refs):
        for core, out_ref in enumerate(out_refs):
            for f in range(far):
                out_ref[f * part : (f + 1) * part, which * rows : (which + 1) * rows] = (
                    x_ref[f, core].T.astype(jnp.bfloat16)
                )


def weight_kernel(x_ref, *refs):
    gp_refs, out_ref = refs[:SIDE], refs[SIDE]
    gp = jnp.concatenate([gp_ref[...].astype(jnp.bfloat16) for gp_ref in gp_refs], axis=0)
    out_ref[...] = jnp.dot(x_ref[...], gp, preferred_element_type=jnp.float32)


def per_device(inputs, in_weight, filter_taps, grad_out):
    rows, depth = inputs.shape
    channels = filter_taps.shape[1]
    columns = in_weight.shape[1]
    blocks = lax.axis_size("seq")
    width = channels // blocks
    part = depth // blocks
    far = blocks // (2 * SIDE)
    chunk = max(2 * part, 512)
    steps = depth // chunk
    scaling = 1.0 / math.sqrt(rows * blocks)
    f32, bf16 = jnp.float32, jnp.bfloat16
    params = pltpu.CompilerParams(vmem_limit_bytes=VMEM_LIMIT)

    def shaped(*shape, dtype=f32):
        return jax.ShapeDtypeStruct(shape, dtype)

    def exchange(value, flip):
        return lax.ppermute(value, "seq", [(i, i ^ flip) for i in range(blocks)])

    device = lax.axis_index("seq")
    place = jnp.stack([device // (2 * SIDE), (device // 2) % SIDE, device % 2]).astype(jnp.int32)
    whole = lambda *shape: pl.BlockSpec(shape, lambda i, place: (0,) * len(shape))
    *moved, signals, gates = pl.pallas_call(
        functools.partial(project_kernel, scaling),
        grid_spec=pltpu.PrefetchScalarGridSpec(
            num_scalar_prefetch=1,
            grid=(steps,),
            in_specs=[
                pl.BlockSpec((rows, chunk), lambda i, place: (0, i)),
                pl.BlockSpec((chunk, columns), lambda i, place: (i, 0)),
                whole(rows, channels),
                whole(rows, channels),
            ],
            out_specs=[whole(far, 2, rows, part)] * SIDE
            + [whole(blocks, 3, width, rows), whole(3, channels, rows)],
            scratch_shapes=[pltpu.VMEM((rows, columns), f32)],
        ),
        out_shape=[shaped(far, 2, rows, part)] * SIDE
        + [shaped(blocks, 3, width, rows), shaped(3, channels, rows)],
        compiler_params=params,
    )(place, inputs, in_weight, filter_taps, grad_out)

    signals = lax.all_to_all(signals, "seq", split_axis=0, concat_axis=0, tiled=True)
    held = [moved[0]] + [exchange(moved[k], 2 * k) for k in range(1, SIDE)]
    tables = [jnp.asarray(table) for table in transform_tables(blocks, width, rows)]
    results = pl.pallas_call(
        conv_kernel,
        out_shape=shaped(blocks, 3, width, rows),
        scratch_shapes=[pltpu.VMEM((blocks * width, 3 * rows), f32)],
        compiler_params=params,
    )(signals, *tables)
    results = lax.all_to_all(results, "seq", split_axis=0, concat_axis=0, tiled=True)
    grad_proj, sent, grad_taps = pl.pallas_call(
        functools.partial(gate_kernel, scaling),
        out_shape=[
            shaped(rows, columns, dtype=bf16),
            shaped(rows, columns),
            shaped(rows, channels),
        ],
        scratch_shapes=[pltpu.VMEM((3, channels, rows), f32)],
        compiler_params=params,
    )(results, gates)
    gathered = [grad_proj] + [exchange(sent, 2 * k) for k in range(1, SIDE)]
    turned = pl.pallas_call(
        turn_kernel,
        out_shape=[shaped(far * part, SIDE * rows, dtype=bf16)] * 2,
        compiler_params=params,
        cost_estimate=pl.CostEstimate(
            flops=0, bytes_accessed=10 * SIDE * far * rows * part, transcendentals=0
        ),
    )(*held)
    grad_inputs = lax.dot_general(
        grad_proj, in_weight, (((1,), (1,)), ((), ())), preferred_element_type=f32
    ).astype(bf16)

    def weight_part(sides):
        return pl.pallas_call(
            weight_kernel,
            grid=(far,),
            in_specs=[pl.BlockSpec((part, SIDE * rows), lambda i: (i, 0))]
            + [pl.BlockSpec((rows, columns), lambda i: (0, 0))] * SIDE,
            out_specs=pl.BlockSpec((part, columns), lambda i: (i, 0)),
            out_shape=shaped(far * part, columns),
            compiler_params=params,
            cost_estimate=pl.CostEstimate(
                flops=2 * far * part * SIDE * rows * columns,
                bytes_accessed=4 * far * part * columns,
                transcendentals=0,
            ),
        )(sides, *gathered)

    from_core = exchange(weight_part(turned[1]), 1)
    summed = (weight_part(turned[0]) + from_core).reshape(far, part, columns)
    grad_weight = summed[0]
    for k in range(1, far):
        grad_weight = grad_weight + exchange(summed[k], 2 * SIDE * k)
    return grad_inputs, grad_weight * scaling, grad_taps


def solution(mesh):
    in_specs = (P(("grp", "seq"), None), P(), P("seq", None), P(("grp", "seq"), None))
    out_specs = (P(("grp", "seq"), None), P(("grp", "seq"), None), P(("grp", "seq"), None))
    return jax.shard_map(
        per_device, mesh=mesh, in_specs=in_specs, out_specs=out_specs, check_vma=False
    )
```

```python
import functools
import math

import jax
import jax.numpy as jnp
import numpy as np
from jax import lax
from jax.experimental import pallas as pl
from jax.experimental.pallas import tpu as pltpu
from jax.sharding import PartitionSpec as P

VMEM_LIMIT = 48 * 1024 * 1024
SIDE = 4


def split_pair(table):
    high = table.astype(np.float32).astype(jnp.bfloat16)
    low = (table - high.astype(np.float64)).astype(np.float32).astype(jnp.bfloat16)
    return high, low


def transform_tables(blocks, width, rows):
    length = 2 * blocks * rows
    kept = blocks + 1
    padded = -(-kept * width // 16) * 16
    k1 = np.arange(kept)
    block = np.arange(blocks)
    angle = 2.0 * np.pi * ((k1[:, None] * block[None, :]) % (2 * blocks)) / (2 * blocks)
    eye = np.eye(width)

    def spread(matrix):
        wide = np.kron(matrix, eye)
        return np.pad(wide, ((0, padded - wide.shape[0]), (0, 0)))

    mix = np.concatenate([spread(np.cos(angle)), spread(-np.sin(angle))], axis=0)
    weight = np.where((k1 == 0) | (k1 == blocks), 1.0, 2.0)[:, None] / length
    unmix = np.concatenate(
        [spread(weight * np.cos(angle)), spread(-weight * np.sin(angle))], axis=0
    ).T
    row = np.arange(rows)
    turn = 2.0 * np.pi * ((k1[:, None] * row[None, :]) % length) / length
    turn = np.pad(np.repeat(turn, width, axis=0), ((0, padded - kept * width), (0, 0)))
    inner = 2.0 * np.pi * ((row[:, None] * row[None, :]) % rows) / rows
    cos, sin = np.cos(inner), np.sin(inner)
    forward = np.block([[cos, -sin], [sin, cos]])
    inverse = np.block([[cos, sin], [-sin, cos]])
    tables = split_pair(mix) + (np.cos(turn).astype(np.float32), np.sin(turn).astype(np.float32))
    return tables + split_pair(forward) + split_pair(inverse) + split_pair(unmix)


def halves(value):
    high = value.astype(jnp.bfloat16)
    return high, (value - high.astype(jnp.float32)).astype(jnp.bfloat16)


def dot32(left, right):
    (lh, ll), (rh, rl) = left, right
    dot = functools.partial(jnp.dot, preferred_element_type=jnp.float32)
    return dot(lh, rh) + (dot(lh, rl) + dot(ll, rh))


def project_kernel(scaling, place_ref, x_ref, w_ref, taps_ref, go_ref, *refs):
    moved_refs, (sig_ref, kv_ref, acc) = refs[:SIDE], refs[SIDE:]
    step = pl.program_id(0)
    block = x_ref[...]
    product = jnp.dot(block, w_ref[...], preferred_element_type=jnp.float32)

    @pl.when(step == 0)
    def _():
        acc[...] = product

    @pl.when(step > 0)
    def _():
        acc[...] += product

    part = moved_refs[0].shape[3]
    core = place_ref[2]
    units = block.shape[1] // (2 * part)
    for unit in range(units):
        chip = step * units + unit
        far = (chip // SIDE) ^ place_ref[0]
        near = (chip % SIDE) ^ place_ref[1]
        for which, moved_ref in enumerate(moved_refs):

            @pl.when(near == which)
            def _():
                for c in range(2):
                    first = (2 * unit + c) * part
                    moved_ref[far, core ^ c] = block[:, first : first + part].astype(jnp.float32)

    @pl.when(step == pl.num_programs(0) - 1)
    def _():
        count, _, width, _ = sig_ref.shape
        channels = count * width
        projected = acc[...].astype(jnp.bfloat16).astype(jnp.float32).T
        query = projected[:channels]
        key = projected[channels : 2 * channels]
        value = projected[2 * channels :]
        go = go_ref[...].astype(jnp.float32).T
        signals = ((taps_ref[...] * scaling).T, key * value, go * query)
        for which, signal in enumerate(signals):
            for owner in range(count):
                sig_ref[owner, which] = signal[owner * width : (owner + 1) * width]
        kv_ref[0] = go
        kv_ref[1] = value
        kv_ref[2] = key


def conv_kernel(
    x_ref, m_h, m_l, t_re, t_im, f_h, f_l, i_h, i_l, u_h, u_l, y_ref, flat
):
    blocks, _, width, rows = x_ref.shape
    for p in range(blocks):
        for s in range(3):
            flat[p * width : (p + 1) * width, s * rows : (s + 1) * rows] = x_ref[p, s]
    turn_re, turn_im = t_re[...], t_im[...]
    count = turn_re.shape[0]
    mixed = dot32((m_h[...], m_l[...]), halves(flat[...]))
    turned = []
    for s in range(3):
        re = mixed[:count, s * rows : (s + 1) * rows]
        im = mixed[count:, s * rows : (s + 1) * rows]
        turned.append(
            jnp.concatenate([re * turn_re + im * turn_im, im * turn_re - re * turn_im], axis=1)
        )
    spectrum = dot32(halves(jnp.concatenate(turned, axis=0)), (f_h[...], f_l[...]))
    (k_re, k_im), (g_re, g_im), (b_re, b_im) = [
        (spectrum[s * count : (s + 1) * count, :rows], spectrum[s * count : (s + 1) * count, rows:])
        for s in range(3)
    ]
    products = jnp.concatenate(
        [
            jnp.concatenate([k_re * g_re - k_im * g_im, k_re * g_im + k_im * g_re], axis=1),
            jnp.concatenate([k_re * b_re + k_im * b_im, k_re * b_im - k_im * b_re], axis=1),
            jnp.concatenate([b_re * g_re + b_im * g_im, b_im * g_re - b_re * g_im], axis=1),
        ],
        axis=0,
    )
    back = dot32(halves(products), (i_h[...], i_l[...]))
    parts_re, parts_im = [], []
    for s in range(3):
        re = back[s * count : (s + 1) * count, :rows]
        im = back[s * count : (s + 1) * count, rows:]
        parts_re.append(re * turn_re - im * turn_im)
        parts_im.append(im * turn_re + re * turn_im)
    stacked = jnp.concatenate(
        [jnp.concatenate(parts_re, axis=1), jnp.concatenate(parts_im, axis=1)], axis=0
    )
    result = dot32((u_h[...], u_l[...]), halves(stacked))
    for p in range(blocks):
        for s in range(3):
            y_ref[p, s] = result[p * width : (p + 1) * width, s * rows : (s + 1) * rows]


def gate_kernel(scaling, y_ref, kv_ref, *refs):
    gp_ref, taps_ref, *sent_refs, flat = refs[SIDE - 1 :]
    count, _, width, _ = y_ref.shape
    channels = count * width
    for s in range(3):
        for owner in range(count):
            flat[s, owner * width : (owner + 1) * width] = y_ref[owner, s]
    back = flat[1]
    for index, value in enumerate((kv_ref[0] * flat[0], kv_ref[1] * back, kv_ref[2] * back)):
        rounded = value.T.astype(jnp.bfloat16)
        gp_ref[:, index * channels : (index + 1) * channels] = rounded
        sent_refs[index][...] = rounded.astype(jnp.float32)
    taps_ref[...] = flat[2].T * scaling


def turn_kernel(*refs):
    x_refs, out_refs = refs[:SIDE], refs[SIDE:]
    far, _, rows, part = x_refs[0].shape
    for which, x_ref in enumerate(x_refs):
        for core, out_ref in enumerate(out_refs):
            for f in range(far):
                out_ref[f * part : (f + 1) * part, which * rows : (which + 1) * rows] = (
                    x_ref[f, core].T.astype(jnp.bfloat16)
                )


def joined(gp_refs):
    return jnp.concatenate([gp_ref[...].astype(jnp.bfloat16) for gp_ref in gp_refs], axis=0)


def other_kernel(x_ref, *refs):
    gp_refs, out_ref = refs[:SIDE], refs[SIDE]
    out_ref[...] = jnp.dot(x_ref[...], joined(gp_refs), preferred_element_type=jnp.float32)


def own_kernel(x_ref, *refs):
    gp_refs, add_ref, out_refs = refs[:SIDE], refs[SIDE], refs[SIDE + 1 :]
    gp = joined(gp_refs)
    part = out_refs[0].shape[0]
    for which, out_ref in enumerate(out_refs):
        span = slice(which * part, (which + 1) * part)
        product = jnp.dot(x_ref[span], gp, preferred_element_type=jnp.float32)
        out_ref[...] = product + add_ref[span]


def sum_kernel(scaling, groups, *refs):
    *in_refs, out_ref = refs
    terms = len(in_refs) // groups
    cols = in_refs[0].shape[1]
    for group in range(groups):
        total = in_refs[group * terms][...]
        for in_ref in in_refs[group * terms + 1 : (group + 1) * terms]:
            total = total + in_ref[...]
        out_ref[:, group * cols : (group + 1) * cols] = total * scaling


def per_device(inputs, in_weight, filter_taps, grad_out):
    rows, depth = inputs.shape
    channels = filter_taps.shape[1]
    columns = in_weight.shape[1]
    blocks = lax.axis_size("seq")
    width = channels // blocks
    part = depth // blocks
    far = blocks // (2 * SIDE)
    chunk = max(2 * part, 512)
    steps = depth // chunk
    scaling = 1.0 / math.sqrt(rows * blocks)
    f32, bf16 = jnp.float32, jnp.bfloat16
    params = pltpu.CompilerParams(vmem_limit_bytes=VMEM_LIMIT)

    def shaped(*shape, dtype=f32):
        return jax.ShapeDtypeStruct(shape, dtype)

    def exchange(value, flip):
        return lax.ppermute(value, "seq", [(i, i ^ flip) for i in range(blocks)])

    device = lax.axis_index("seq")
    place = jnp.stack([device // (2 * SIDE), (device // 2) % SIDE, device % 2]).astype(jnp.int32)
    whole = lambda *shape: pl.BlockSpec(shape, lambda i, place: (0,) * len(shape))
    *moved, signals, gates = pl.pallas_call(
        functools.partial(project_kernel, scaling),
        grid_spec=pltpu.PrefetchScalarGridSpec(
            num_scalar_prefetch=1,
            grid=(steps,),
            in_specs=[
                pl.BlockSpec((rows, chunk), lambda i, place: (0, i)),
                pl.BlockSpec((chunk, columns), lambda i, place: (i, 0)),
                whole(rows, channels),
                whole(rows, channels),
            ],
            out_specs=[whole(far, 2, rows, part)] * SIDE
            + [whole(blocks, 3, width, rows), whole(3, channels, rows)],
            scratch_shapes=[pltpu.VMEM((rows, columns), f32)],
        ),
        out_shape=[shaped(far, 2, rows, part)] * SIDE
        + [shaped(blocks, 3, width, rows), shaped(3, channels, rows)],
        compiler_params=params,
    )(place, inputs, in_weight, filter_taps, grad_out)

    signals = lax.all_to_all(signals, "seq", split_axis=0, concat_axis=0, tiled=True)
    held = [moved[0]] + [exchange(moved[k], 2 * k) for k in range(1, SIDE)]
    tables = [jnp.asarray(table) for table in transform_tables(blocks, width, rows)]
    results = pl.pallas_call(
        conv_kernel,
        out_shape=shaped(blocks, 3, width, rows),
        scratch_shapes=[pltpu.VMEM((blocks * width, 3 * rows), f32)],
        compiler_params=params,
    )(signals, *tables)
    results = lax.all_to_all(results, "seq", split_axis=0, concat_axis=0, tiled=True)
    anywhere = pl.BlockSpec(memory_space=pl.ANY)
    inside = pl.BlockSpec(memory_space=pltpu.VMEM)
    grad_proj, grad_taps, *sent = pl.pallas_call(
        functools.partial(gate_kernel, scaling),
        in_specs=[inside, inside] + [anywhere] * (SIDE - 1),
        out_shape=[shaped(rows, columns, dtype=bf16), shaped(rows, channels)]
        + [shaped(rows, channels)] * 3,
        scratch_shapes=[pltpu.VMEM((3, channels, rows), f32)],
        compiler_params=params,
    )(results, gates, *held[1:])
    turned = pl.pallas_call(
        turn_kernel,
        out_shape=[shaped(far * part, SIDE * rows, dtype=bf16)] * 2,
        compiler_params=params,
        cost_estimate=pl.CostEstimate(
            flops=0, bytes_accessed=10 * SIDE * far * rows * part, transcendentals=0
        ),
    )(*held)
    grad_inputs = lax.dot_general(
        grad_proj, in_weight, (((1,), (1,)), ((), ())), preferred_element_type=f32
    ).astype(bf16)
    cost = pl.CostEstimate(
        flops=2 * far * part * SIDE * rows * channels,
        bytes_accessed=4 * far * part * channels,
        transcendentals=0,
    )
    terms = []
    for block in sent:
        gathered = [block] + [exchange(block, 2 * k) for k in range(1, SIDE)]
        other = pl.pallas_call(
            other_kernel,
            out_shape=shaped(far * part, channels),
            compiler_params=params,
            cost_estimate=cost,
        )(turned[1], *gathered)
        kept, *leaving = pl.pallas_call(
            own_kernel,
            out_shape=[shaped(part, channels)] * far,
            compiler_params=params,
            cost_estimate=cost,
        )(turned[0], *gathered, exchange(other, 1))
        terms += [kept] + [exchange(v, 2 * SIDE * (k + 1)) for k, v in enumerate(leaving)]
    grad_weight = pl.pallas_call(
        functools.partial(sum_kernel, scaling, len(sent)),
        out_shape=shaped(part, columns),
        compiler_params=params,
    )(*terms)
    return grad_inputs, grad_weight, grad_taps


def solution(mesh):
    in_specs = (P(("grp", "seq"), None), P(), P("seq", None), P(("grp", "seq"), None))
    out_specs = (P(("grp", "seq"), None), P(("grp", "seq"), None), P(("grp", "seq"), None))
    return jax.shard_map(
        per_device, mesh=mesh, in_specs=in_specs, out_specs=out_specs, check_vma=False
    )
```

```python
import functools
import math

import jax
import jax.numpy as jnp
import numpy as np
from jax import lax
from jax.experimental import pallas as pl
from jax.experimental.pallas import tpu as pltpu
from jax.sharding import PartitionSpec as P

VMEM_LIMIT = 48 * 1024 * 1024
VMEM_WIDE = 60 * 1024 * 1024
SIDE = 4


def split_pair(table):
    high = table.astype(np.float32).astype(jnp.bfloat16)
    low = (table - high.astype(np.float64)).astype(np.float32).astype(jnp.bfloat16)
    return high, low


def transform_tables(blocks, width, rows):
    length = 2 * blocks * rows
    kept = blocks + 1
    padded = -(-kept * width // 16) * 16
    k1 = np.arange(kept)
    block = np.arange(blocks)
    angle = 2.0 * np.pi * ((k1[:, None] * block[None, :]) % (2 * blocks)) / (2 * blocks)
    eye = np.eye(width)

    def spread(matrix):
        wide = np.kron(matrix, eye)
        return np.pad(wide, ((0, padded - wide.shape[0]), (0, 0)))

    mix = np.concatenate([spread(np.cos(angle)), spread(-np.sin(angle))], axis=0)
    weight = np.where((k1 == 0) | (k1 == blocks), 1.0, 2.0)[:, None] / length
    unmix = np.concatenate(
        [spread(weight * np.cos(angle)), spread(-weight * np.sin(angle))], axis=0
    ).T
    row = np.arange(rows)
    turn = 2.0 * np.pi * ((k1[:, None] * row[None, :]) % length) / length
    turn = np.pad(np.repeat(turn, width, axis=0), ((0, padded - kept * width), (0, 0)))
    inner = 2.0 * np.pi * ((row[:, None] * row[None, :]) % rows) / rows
    cos, sin = np.cos(inner), np.sin(inner)
    forward = np.block([[cos, -sin], [sin, cos]])
    inverse = np.block([[cos, sin], [-sin, cos]])
    tables = split_pair(mix) + (np.cos(turn).astype(np.float32), np.sin(turn).astype(np.float32))
    return tables + split_pair(forward) + split_pair(inverse) + split_pair(unmix)


def halves(value):
    high = value.astype(jnp.bfloat16)
    return high, (value - high.astype(jnp.float32)).astype(jnp.bfloat16)


def dot32(left, right):
    (lh, ll), (rh, rl) = left, right
    dot = functools.partial(jnp.dot, preferred_element_type=jnp.float32)
    return dot(lh, rh) + (dot(lh, rl) + dot(ll, rh))


def layout_kernel(place_ref, x_ref, *moved_refs):
    far, _, _, part = moved_refs[0].shape
    for chip in range(far * SIDE):
        distance = (chip // SIDE) ^ place_ref[0]
        near = (chip % SIDE) ^ place_ref[1]
        for which, moved_ref in enumerate(moved_refs):

            @pl.when(near == which)
            def _():
                for c in range(2):
                    first = (2 * chip + c) * part
                    moved_ref[distance, place_ref[2] ^ c] = x_ref[:, first : first + part].astype(
                        jnp.float32
                    )


def project_kernel(scaling, x_ref, w_ref, taps_ref, go_ref, sig_ref, kv_ref, acc):
    step = pl.program_id(0)
    product = jnp.dot(x_ref[...], w_ref[...], preferred_element_type=jnp.float32)

    @pl.when(step == 0)
    def _():
        acc[...] = product

    @pl.when(step > 0)
    def _():
        acc[...] += product

    @pl.when(step == pl.num_programs(0) - 1)
    def _():
        count, _, width, _ = sig_ref.shape
        channels = count * width
        projected = acc[...].astype(jnp.bfloat16).astype(jnp.float32).T
        query = projected[:channels]
        key = projected[channels : 2 * channels]
        value = projected[2 * channels :]
        go = go_ref[...].astype(jnp.float32).T
        signals = ((taps_ref[...] * scaling).T, key * value, go * query)
        for which, signal in enumerate(signals):
            for owner in range(count):
                sig_ref[owner, which] = signal[owner * width : (owner + 1) * width]
        kv_ref[0] = go
        kv_ref[1] = value
        kv_ref[2] = key


def conv_kernel(
    x_ref, m_h, m_l, t_re, t_im, f_h, f_l, i_h, i_l, u_h, u_l, *refs
):
    y_ref, flat = refs[-2:]
    blocks, _, width, rows = x_ref.shape
    for p in range(blocks):
        for s in range(3):
            flat[p * width : (p + 1) * width, s * rows : (s + 1) * rows] = x_ref[p, s]
    turn_re, turn_im = t_re[...], t_im[...]
    count = turn_re.shape[0]
    mixed = dot32((m_h[...], m_l[...]), halves(flat[...]))
    turned = []
    for s in range(3):
        re = mixed[:count, s * rows : (s + 1) * rows]
        im = mixed[count:, s * rows : (s + 1) * rows]
        turned.append(
            jnp.concatenate([re * turn_re + im * turn_im, im * turn_re - re * turn_im], axis=1)
        )
    spectrum = dot32(halves(jnp.concatenate(turned, axis=0)), (f_h[...], f_l[...]))
    (k_re, k_im), (g_re, g_im), (b_re, b_im) = [
        (spectrum[s * count : (s + 1) * count, :rows], spectrum[s * count : (s + 1) * count, rows:])
        for s in range(3)
    ]
    products = jnp.concatenate(
        [
            jnp.concatenate([k_re * g_re - k_im * g_im, k_re * g_im + k_im * g_re], axis=1),
            jnp.concatenate([k_re * b_re + k_im * b_im, k_re * b_im - k_im * b_re], axis=1),
            jnp.concatenate([b_re * g_re + b_im * g_im, b_im * g_re - b_re * g_im], axis=1),
        ],
        axis=0,
    )
    back = dot32(halves(products), (i_h[...], i_l[...]))
    parts_re, parts_im = [], []
    for s in range(3):
        re = back[s * count : (s + 1) * count, :rows]
        im = back[s * count : (s + 1) * count, rows:]
        parts_re.append(re * turn_re - im * turn_im)
        parts_im.append(im * turn_re + re * turn_im)
    stacked = jnp.concatenate(
        [jnp.concatenate(parts_re, axis=1), jnp.concatenate(parts_im, axis=1)], axis=0
    )
    result = dot32((u_h[...], u_l[...]), halves(stacked))
    for p in range(blocks):
        for s in range(3):
            y_ref[p, s] = result[p * width : (p + 1) * width, s * rows : (s + 1) * rows]


def gate_first_kernel(y_ref, kv_ref, gp_ref, sent_ref, flat):
    count, _, width, _ = y_ref.shape
    for owner in range(count):
        flat[owner * width : (owner + 1) * width] = y_ref[owner, 0]
    rounded = (kv_ref[0] * flat[...]).T.astype(jnp.bfloat16)
    gp_ref[...] = rounded
    sent_ref[...] = rounded.astype(jnp.float32)


def gate_rest_kernel(scaling, y_ref, kv_ref, first_ref, *refs):
    gp_ref, sent_ref, taps_ref, flat = refs[-4:]
    count, _, width, _ = y_ref.shape
    channels = count * width
    for s in range(2):
        for owner in range(count):
            flat[s, owner * width : (owner + 1) * width] = y_ref[owner, s + 1]
    gp_ref[:, :channels] = first_ref[...]
    for index in range(2):
        rounded = (kv_ref[index + 1] * flat[0]).T.astype(jnp.bfloat16)
        gp_ref[:, (index + 1) * channels : (index + 2) * channels] = rounded
        sent_ref[:, index * channels : (index + 1) * channels] = rounded.astype(jnp.float32)
    taps_ref[...] = flat[1].T * scaling


def turn_kernel(*refs):
    x_refs, out_refs = refs[:SIDE], refs[SIDE:]
    far, _, rows, part = x_refs[0].shape
    for which, x_ref in enumerate(x_refs):
        for core, out_ref in enumerate(out_refs):
            for f in range(far):
                out_ref[f * part : (f + 1) * part, which * rows : (which + 1) * rows] = (
                    x_ref[f, core].T.astype(jnp.bfloat16)
                )


def joined(gp_refs):
    return jnp.concatenate([gp_ref[...].astype(jnp.bfloat16) for gp_ref in gp_refs], axis=0)


def other_kernel(x_ref, *refs):
    gp_refs, out_ref = refs[:SIDE], refs[-1]
    out_ref[...] = jnp.dot(x_ref[...], joined(gp_refs), preferred_element_type=jnp.float32)


def own_kernel(x_ref, *refs):
    gp_refs, add_ref, out_refs = refs[:SIDE], refs[SIDE], refs[SIDE + 1 :]
    gp = joined(gp_refs)
    part = out_refs[0].shape[0]
    for which, out_ref in enumerate(out_refs):
        span = slice(which * part, (which + 1) * part)
        product = jnp.dot(x_ref[span], gp, preferred_element_type=jnp.float32)
        out_ref[...] = product + add_ref[span]


def sum_kernel(scaling, groups, *refs):
    *in_refs, out_ref = refs
    terms = len(in_refs) // groups
    first = 0
    for group in range(groups):
        total = in_refs[group * terms][...]
        for in_ref in in_refs[group * terms + 1 : (group + 1) * terms]:
            total = total + in_ref[...]
        out_ref[:, first : first + total.shape[1]] = total * scaling
        first += total.shape[1]


def per_device(inputs, in_weight, filter_taps, grad_out):
    rows, depth = inputs.shape
    channels = filter_taps.shape[1]
    columns = in_weight.shape[1]
    blocks = lax.axis_size("seq")
    width = channels // blocks
    part = depth // blocks
    far = blocks // (2 * SIDE)
    chunk = min(1024, depth)
    steps = depth // chunk
    scaling = 1.0 / math.sqrt(rows * blocks)
    f32, bf16 = jnp.float32, jnp.bfloat16
    params = pltpu.CompilerParams(vmem_limit_bytes=VMEM_LIMIT)
    wide = pltpu.CompilerParams(vmem_limit_bytes=VMEM_WIDE)

    def shaped(*shape, dtype=f32):
        return jax.ShapeDtypeStruct(shape, dtype)

    def exchange(value, flip):
        return lax.ppermute(value, "seq", [(i, i ^ flip) for i in range(blocks)])

    device = lax.axis_index("seq")
    place = jnp.stack([device // (2 * SIDE), (device // 2) % SIDE, device % 2]).astype(jnp.int32)
    anywhere = pl.BlockSpec(memory_space=pl.ANY)
    inside = pl.BlockSpec(memory_space=pltpu.VMEM)
    moved = pl.pallas_call(
        layout_kernel,
        in_specs=[pl.BlockSpec(memory_space=pltpu.SMEM), inside],
        out_shape=[shaped(far, 2, rows, part)] * SIDE,
        compiler_params=wide,
    )(place, inputs)
    held = [moved[0]] + [exchange(moved[k], 2 * k) for k in range(1, SIDE)]
    signals, gates = pl.pallas_call(
        functools.partial(project_kernel, scaling),
        grid=(steps,),
        in_specs=[
            pl.BlockSpec((rows, chunk), lambda i: (0, i)),
            pl.BlockSpec((chunk, columns), lambda i: (i, 0)),
            pl.BlockSpec((rows, channels), lambda i: (0, 0)),
            pl.BlockSpec((rows, channels), lambda i: (0, 0)),
        ],
        out_specs=[
            pl.BlockSpec((blocks, 3, width, rows), lambda i: (0, 0, 0, 0)),
            pl.BlockSpec((3, channels, rows), lambda i: (0, 0, 0)),
        ],
        out_shape=[shaped(blocks, 3, width, rows), shaped(3, channels, rows)],
        scratch_shapes=[pltpu.VMEM((rows, columns), f32)],
        compiler_params=wide,
        cost_estimate=pl.CostEstimate(
            flops=2 * rows * depth * columns,
            bytes_accessed=2 * depth * (rows + columns),
            transcendentals=0,
        ),
    )(inputs, in_weight, filter_taps, grad_out)

    signals = lax.all_to_all(signals, "seq", split_axis=0, concat_axis=0, tiled=True)
    tables = [jnp.asarray(table) for table in transform_tables(blocks, width, rows)]
    results = pl.pallas_call(
        conv_kernel,
        in_specs=[inside] * (1 + len(tables)) + [anywhere] * (SIDE - 1),
        out_shape=shaped(blocks, 3, width, rows),
        scratch_shapes=[pltpu.VMEM((blocks * width, 3 * rows), f32)],
        compiler_params=params,
    )(signals, *tables, *held[1:])
    results = lax.all_to_all(results, "seq", split_axis=0, concat_axis=0, tiled=True)
    first, sent_first = pl.pallas_call(
        gate_first_kernel,
        out_shape=[shaped(rows, channels, dtype=bf16), shaped(rows, channels)],
        scratch_shapes=[pltpu.VMEM((channels, rows), f32)],
        compiler_params=params,
    )(results, gates)
    gathered_first = [sent_first] + [exchange(sent_first, 2 * k) for k in range(1, SIDE)]
    grad_proj, sent_rest, grad_taps = pl.pallas_call(
        functools.partial(gate_rest_kernel, scaling),
        in_specs=[inside] * 3 + [anywhere] * (SIDE - 1),
        out_shape=[
            shaped(rows, columns, dtype=bf16),
            shaped(rows, 2 * channels),
            shaped(rows, channels),
        ],
        scratch_shapes=[pltpu.VMEM((2, channels, rows), f32)],
        compiler_params=params,
    )(results, gates, first, *gathered_first[1:])
    gathered_rest = [sent_rest] + [exchange(sent_rest, 2 * k) for k in range(1, SIDE)]
    turned = pl.pallas_call(
        turn_kernel,
        out_shape=[shaped(far * part, SIDE * rows, dtype=bf16)] * 2,
        compiler_params=params,
        cost_estimate=pl.CostEstimate(
            flops=0, bytes_accessed=10 * SIDE * far * rows * part, transcendentals=0
        ),
    )(*held)
    grad_inputs = lax.dot_general(
        grad_proj, in_weight, (((1,), (1,)), ((), ())), preferred_element_type=f32
    ).astype(bf16)
    terms = []
    for gathered in (gathered_first, gathered_rest):
        cols = gathered[0].shape[1]
        cost = pl.CostEstimate(
            flops=2 * far * part * SIDE * rows * cols,
            bytes_accessed=4 * far * part * cols,
            transcendentals=0,
        )
        other = pl.pallas_call(
            other_kernel,
            in_specs=[inside] * (1 + SIDE) + [anywhere] * len(terms[1:]),
            out_shape=shaped(far * part, cols),
            compiler_params=params,
            cost_estimate=cost,
        )(turned[1], *gathered, *terms[1:])
        kept, *leaving = pl.pallas_call(
            own_kernel,
            out_shape=[shaped(part, cols)] * far,
            compiler_params=params,
            cost_estimate=cost,
        )(turned[0], *gathered, exchange(other, 1))
        terms += [kept] + [exchange(v, 2 * SIDE * (k + 1)) for k, v in enumerate(leaving)]
    grad_weight = pl.pallas_call(
        functools.partial(sum_kernel, scaling, 2),
        out_shape=shaped(part, columns),
        compiler_params=params,
    )(*terms)
    return grad_inputs, grad_weight, grad_taps


def solution(mesh):
    in_specs = (P(("grp", "seq"), None), P(), P("seq", None), P(("grp", "seq"), None))
    out_specs = (P(("grp", "seq"), None), P(("grp", "seq"), None), P(("grp", "seq"), None))
    return jax.shard_map(
        per_device, mesh=mesh, in_specs=in_specs, out_specs=out_specs, check_vma=False
    )
```

```python
import functools
import math

import jax
import jax.numpy as jnp
import numpy as np
from jax import lax
from jax.experimental import pallas as pl
from jax.experimental.pallas import tpu as pltpu
from jax.sharding import PartitionSpec as P

VMEM_LIMIT = 48 * 1024 * 1024
VMEM_WIDE = 60 * 1024 * 1024
SIDE = 4


def split_pair(table):
    high = table.astype(np.float32).astype(jnp.bfloat16)
    low = (table - high.astype(np.float64)).astype(np.float32).astype(jnp.bfloat16)
    return high, low


def transform_tables(blocks, width, rows):
    length = 2 * blocks * rows
    kept = blocks + 1
    padded = -(-kept * width // 16) * 16
    k1 = np.arange(kept)
    block = np.arange(blocks)
    angle = 2.0 * np.pi * ((k1[:, None] * block[None, :]) % (2 * blocks)) / (2 * blocks)
    eye = np.eye(width)

    def spread(matrix):
        wide = np.kron(matrix, eye)
        return np.pad(wide, ((0, padded - wide.shape[0]), (0, 0)))

    mix = np.concatenate([spread(np.cos(angle)), spread(-np.sin(angle))], axis=0)
    weight = np.where((k1 == 0) | (k1 == blocks), 1.0, 2.0)[:, None] / length
    unmix = np.concatenate(
        [spread(weight * np.cos(angle)), spread(-weight * np.sin(angle))], axis=0
    ).T
    row = np.arange(rows)
    turn = 2.0 * np.pi * ((k1[:, None] * row[None, :]) % length) / length
    turn = np.pad(np.repeat(turn, width, axis=0), ((0, padded - kept * width), (0, 0)))
    inner = 2.0 * np.pi * ((row[:, None] * row[None, :]) % rows) / rows
    cos, sin = np.cos(inner), np.sin(inner)
    forward = np.block([[cos, -sin], [sin, cos]])
    inverse = np.block([[cos, sin], [-sin, cos]])
    turn = np.concatenate([np.cos(turn), np.sin(turn)], axis=1).astype(np.float32)
    return [split_pair(matrix) for matrix in (mix, forward, inverse, unmix)], turn


def packed(tables):
    width = max(min(high.shape) for high, _ in tables)
    slabs, places, first = [], [], 0
    for pair in tables:
        for table in pair:
            pieces = []
            for start in range(0, table.shape[1], width):
                slab = table[:, start : start + width]
                pieces.append((first, slab.shape))
                first += slab.shape[0]
                slabs.append(np.pad(slab, ((0, 0), (0, width - slab.shape[1]))))
            places.append(pieces)
    return np.concatenate(slabs, axis=0), places


def halves(value):
    high = value.astype(jnp.bfloat16)
    return high, (value - high.astype(jnp.float32)).astype(jnp.bfloat16)


def dot32(left, right):
    (lh, ll), (rh, rl) = left, right
    dot = functools.partial(jnp.dot, preferred_element_type=jnp.float32)
    return dot(lh, rh) + (dot(lh, rl) + dot(ll, rh))


def layout_kernel(x_ref, *moved_refs):
    far, _, _, part = moved_refs[0].shape
    device = lax.axis_index("seq")
    for chip in range(far * SIDE):
        distance = (chip // SIDE) ^ (device // (2 * SIDE))
        near = (chip % SIDE) ^ ((device // 2) % SIDE)
        for which, moved_ref in enumerate(moved_refs):

            @pl.when(near == which)
            def _():
                for c in range(2):
                    first = (2 * chip + c) * part
                    moved_ref[distance, (device % 2) ^ c] = x_ref[:, first : first + part].astype(
                        jnp.float32
                    )


def project_kernel(scaling, x_ref, w_ref, taps_ref, go_ref, *refs):
    sig_ref, kv_ref, acc = refs[-3:]
    step = pl.program_id(0)
    product = jnp.dot(x_ref[...], w_ref[...], preferred_element_type=jnp.float32)

    @pl.when(step == 0)
    def _():
        acc[...] = product

    @pl.when(step > 0)
    def _():
        acc[...] += product

    @pl.when(step == pl.num_programs(0) - 1)
    def _():
        count, _, width, _ = sig_ref.shape
        channels = count * width
        projected = acc[...].astype(jnp.bfloat16).astype(jnp.float32).T
        query = projected[:channels]
        key = projected[channels : 2 * channels]
        value = projected[2 * channels :]
        go = go_ref[...].astype(jnp.float32).T
        signals = ((taps_ref[...] * scaling).T, key * value, go * query)
        for which, signal in enumerate(signals):
            for owner in range(count):
                sig_ref[owner, which] = signal[owner * width : (owner + 1) * width]
        kv_ref[0] = go
        kv_ref[1] = value
        kv_ref[2] = key


def conv_kernel(places, x_ref, table_ref, turn_ref, *refs):
    y_ref, flat = refs[-2:]
    blocks, _, width, rows = x_ref.shape

    def table(which):
        slabs = [table_ref[at : at + shape[0], : shape[1]] for at, shape in places[which]]
        return slabs[0] if len(slabs) == 1 else jnp.concatenate(slabs, axis=1)

    m_h, m_l, f_h, f_l, i_h, i_l, u_h, u_l = [functools.partial(table, w) for w in range(8)]
    for p in range(blocks):
        for s in range(3):
            flat[p * width : (p + 1) * width, s * rows : (s + 1) * rows] = x_ref[p, s]
    turn_re, turn_im = turn_ref[:, :rows], turn_ref[:, rows:]
    count = turn_re.shape[0]
    mixed = dot32((m_h(), m_l()), halves(flat[...]))
    turned = []
    for s in range(3):
        re = mixed[:count, s * rows : (s + 1) * rows]
        im = mixed[count:, s * rows : (s + 1) * rows]
        turned.append(
            jnp.concatenate([re * turn_re + im * turn_im, im * turn_re - re * turn_im], axis=1)
        )
    spectrum = dot32(halves(jnp.concatenate(turned, axis=0)), (f_h(), f_l()))
    (k_re, k_im), (g_re, g_im), (b_re, b_im) = [
        (spectrum[s * count : (s + 1) * count, :rows], spectrum[s * count : (s + 1) * count, rows:])
        for s in range(3)
    ]
    products = jnp.concatenate(
        [
            jnp.concatenate([k_re * g_re - k_im * g_im, k_re * g_im + k_im * g_re], axis=1),
            jnp.concatenate([k_re * b_re + k_im * b_im, k_re * b_im - k_im * b_re], axis=1),
            jnp.concatenate([b_re * g_re + b_im * g_im, b_im * g_re - b_re * g_im], axis=1),
        ],
        axis=0,
    )
    back = dot32(halves(products), (i_h(), i_l()))
    parts_re, parts_im = [], []
    for s in range(3):
        re = back[s * count : (s + 1) * count, :rows]
        im = back[s * count : (s + 1) * count, rows:]
        parts_re.append(re * turn_re - im * turn_im)
        parts_im.append(im * turn_re + re * turn_im)
    stacked = jnp.concatenate(
        [jnp.concatenate(parts_re, axis=1), jnp.concatenate(parts_im, axis=1)], axis=0
    )
    result = dot32((u_h(), u_l()), halves(stacked))
    for p in range(blocks):
        for s in range(3):
            y_ref[p, s] = result[p * width : (p + 1) * width, s * rows : (s + 1) * rows]


def gate_first_kernel(y_ref, kv_ref, gp_ref, sent_ref, flat):
    count, _, width, _ = y_ref.shape
    for owner in range(count):
        flat[owner * width : (owner + 1) * width] = y_ref[owner, 0]
    rounded = (kv_ref[0] * flat[...]).T.astype(jnp.bfloat16)
    gp_ref[...] = rounded
    sent_ref[...] = rounded.astype(jnp.float32)


def gate_rest_kernel(scaling, y_ref, kv_ref, first_ref, *refs):
    gp_ref, sent_ref, taps_ref, flat = refs[-4:]
    count, _, width, _ = y_ref.shape
    channels = count * width
    for s in range(2):
        for owner in range(count):
            flat[s, owner * width : (owner + 1) * width] = y_ref[owner, s + 1]
    gp_ref[:, :channels] = first_ref[...]
    for index in range(2):
        rounded = (kv_ref[index + 1] * flat[0]).T.astype(jnp.bfloat16)
        gp_ref[:, (index + 1) * channels : (index + 2) * channels] = rounded
        sent_ref[:, index * channels : (index + 1) * channels] = rounded.astype(jnp.float32)
    taps_ref[...] = flat[1].T * scaling


def turn_kernel(*refs):
    x_refs, out_refs = refs[:SIDE], refs[SIDE:]
    far, _, rows, part = x_refs[0].shape
    for which, x_ref in enumerate(x_refs):
        for core, out_ref in enumerate(out_refs):
            for f in range(far):
                out_ref[f * part : (f + 1) * part, which * rows : (which + 1) * rows] = (
                    x_ref[f, core].T.astype(jnp.bfloat16)
                )


def joined(gp_refs):
    return jnp.concatenate([gp_ref[...].astype(jnp.bfloat16) for gp_ref in gp_refs], axis=0)


def other_kernel(x_ref, *refs):
    gp_refs, out_ref = refs[:SIDE], refs[-1]
    out_ref[...] = jnp.dot(x_ref[...], joined(gp_refs), preferred_element_type=jnp.float32)


def own_kernel(x_ref, *refs):
    gp_refs, add_ref, out_refs = refs[:SIDE], refs[SIDE], refs[SIDE + 1 :]
    gp = joined(gp_refs)
    part = out_refs[0].shape[0]
    for which, out_ref in enumerate(out_refs):
        span = slice(which * part, (which + 1) * part)
        product = jnp.dot(x_ref[span], gp, preferred_element_type=jnp.float32)
        out_ref[...] = product + add_ref[span]


def sum_kernel(scaling, groups, *refs):
    *in_refs, out_ref = refs
    terms = len(in_refs) // groups
    first = 0
    for group in range(groups):
        total = in_refs[group * terms][...]
        for in_ref in in_refs[group * terms + 1 : (group + 1) * terms]:
            total = total + in_ref[...]
        out_ref[:, first : first + total.shape[1]] = total * scaling
        first += total.shape[1]


def per_device(inputs, in_weight, filter_taps, grad_out):
    rows, depth = inputs.shape
    channels = filter_taps.shape[1]
    columns = in_weight.shape[1]
    blocks = lax.axis_size("seq")
    width = channels // blocks
    part = depth // blocks
    far = blocks // (2 * SIDE)
    chunk = min(1024, depth)
    steps = depth // chunk
    scaling = 1.0 / math.sqrt(rows * blocks)
    f32, bf16 = jnp.float32, jnp.bfloat16
    params = pltpu.CompilerParams(vmem_limit_bytes=VMEM_LIMIT)
    wide = pltpu.CompilerParams(vmem_limit_bytes=VMEM_WIDE)

    def shaped(*shape, dtype=f32):
        return jax.ShapeDtypeStruct(shape, dtype)

    def exchange(value, flip):
        return lax.ppermute(value, "seq", [(i, i ^ flip) for i in range(blocks)])

    anywhere = pl.BlockSpec(memory_space=pl.ANY)
    inside = pl.BlockSpec(memory_space=pltpu.VMEM)
    moved = pl.pallas_call(
        layout_kernel,
        out_shape=[shaped(far, 2, rows, part)] * SIDE,
        compiler_params=wide,
    )(inputs)
    held = [moved[0]] + [exchange(moved[k], 2 * k) for k in range(1, SIDE)]
    signals, gates = pl.pallas_call(
        functools.partial(project_kernel, scaling),
        grid=(steps,),
        in_specs=[
            pl.BlockSpec((rows, chunk), lambda i: (0, i)),
            pl.BlockSpec((chunk, columns), lambda i: (i, 0)),
            pl.BlockSpec((rows, channels), lambda i: (0, 0)),
            pl.BlockSpec((rows, channels), lambda i: (0, 0)),
        ]
        + [anywhere] * (SIDE - 1),
        out_specs=[
            pl.BlockSpec((blocks, 3, width, rows), lambda i: (0, 0, 0, 0)),
            pl.BlockSpec((3, channels, rows), lambda i: (0, 0, 0)),
        ],
        out_shape=[shaped(blocks, 3, width, rows), shaped(3, channels, rows)],
        scratch_shapes=[pltpu.VMEM((rows, columns), f32)],
        compiler_params=wide,
        cost_estimate=pl.CostEstimate(
            flops=2 * rows * depth * columns,
            bytes_accessed=2 * depth * (rows + columns),
            transcendentals=0,
        ),
    )(inputs, in_weight, filter_taps, grad_out, *moved[1:])

    signals = lax.all_to_all(signals, "seq", split_axis=0, concat_axis=0, tiled=True)
    pairs, turn = transform_tables(blocks, width, rows)
    table, places = packed(pairs)
    results = pl.pallas_call(
        functools.partial(conv_kernel, places),
        in_specs=[inside] * 3 + [anywhere] * (SIDE - 1),
        out_shape=shaped(blocks, 3, width, rows),
        scratch_shapes=[pltpu.VMEM((blocks * width, 3 * rows), f32)],
        compiler_params=params,
    )(signals, jnp.asarray(table), jnp.asarray(turn), *held[1:])
    results = lax.all_to_all(results, "seq", split_axis=0, concat_axis=0, tiled=True)
    first, sent_first = pl.pallas_call(
        gate_first_kernel,
        out_shape=[shaped(rows, channels, dtype=bf16), shaped(rows, channels)],
        scratch_shapes=[pltpu.VMEM((channels, rows), f32)],
        compiler_params=params,
    )(results, gates)
    gathered_first = [sent_first] + [exchange(sent_first, 2 * k) for k in range(1, SIDE)]
    grad_proj, sent_rest, grad_taps = pl.pallas_call(
        functools.partial(gate_rest_kernel, scaling),
        out_shape=[
            shaped(rows, columns, dtype=bf16),
            shaped(rows, 2 * channels),
            shaped(rows, channels),
        ],
        scratch_shapes=[pltpu.VMEM((2, channels, rows), f32)],
        compiler_params=params,
    )(results, gates, first)
    gathered_rest = [sent_rest] + [exchange(sent_rest, 2 * k) for k in range(1, SIDE)]
    turned = pl.pallas_call(
        turn_kernel,
        out_shape=[shaped(far * part, SIDE * rows, dtype=bf16)] * 2,
        compiler_params=params,
        cost_estimate=pl.CostEstimate(
            flops=0, bytes_accessed=10 * SIDE * far * rows * part, transcendentals=0
        ),
    )(*held)
    grad_inputs = lax.dot_general(
        grad_proj, in_weight, (((1,), (1,)), ((), ())), preferred_element_type=f32
    ).astype(bf16)
    terms = []
    for gathered in (gathered_first, gathered_rest):
        cols = gathered[0].shape[1]
        cost = pl.CostEstimate(
            flops=2 * far * part * SIDE * rows * cols,
            bytes_accessed=4 * far * part * cols,
            transcendentals=0,
        )
        other = pl.pallas_call(
            other_kernel,
            in_specs=[inside] * (1 + SIDE) + [anywhere] * len(terms[1:]),
            out_shape=shaped(far * part, cols),
            compiler_params=params,
            cost_estimate=cost,
        )(turned[1], *gathered, *terms[1:])
        kept, *leaving = pl.pallas_call(
            own_kernel,
            out_shape=[shaped(part, cols)] * far,
            compiler_params=params,
            cost_estimate=cost,
        )(turned[0], *gathered, exchange(other, 1))
        terms += [kept] + [exchange(v, 2 * SIDE * (k + 1)) for k, v in enumerate(leaving)]
    grad_weight = pl.pallas_call(
        functools.partial(sum_kernel, scaling, 2),
        out_shape=shaped(part, columns),
        compiler_params=params,
    )(*terms)
    return grad_inputs, grad_weight, grad_taps


def solution(mesh):
    in_specs = (P(("grp", "seq"), None), P(), P("seq", None), P(("grp", "seq"), None))
    out_specs = (P(("grp", "seq"), None), P(("grp", "seq"), None), P(("grp", "seq"), None))
    return jax.shard_map(
        per_device, mesh=mesh, in_specs=in_specs, out_specs=out_specs, check_vma=False
    )
```

```python
import functools
import math

import jax
import jax.numpy as jnp
import numpy as np
from jax import lax
from jax.experimental import pallas as pl
from jax.experimental.pallas import tpu as pltpu
from jax.sharding import PartitionSpec as P

VMEM_LIMIT = 48 * 1024 * 1024
VMEM_WIDE = 60 * 1024 * 1024
SIDE = 4


def split_pair(table):
    high = table.astype(np.float32).astype(jnp.bfloat16)
    low = (table - high.astype(np.float64)).astype(np.float32).astype(jnp.bfloat16)
    return high, low


def transform_tables(blocks, width, rows):
    length = 2 * blocks * rows
    kept = blocks + 1
    padded = -(-kept * width // 16) * 16
    k1 = np.arange(kept)
    block = np.arange(blocks)
    angle = 2.0 * np.pi * ((k1[:, None] * block[None, :]) % (2 * blocks)) / (2 * blocks)
    eye = np.eye(width)

    def spread(matrix):
        wide = np.kron(matrix, eye)
        return np.pad(wide, ((0, padded - wide.shape[0]), (0, 0)))

    mix = np.concatenate([spread(np.cos(angle)), spread(-np.sin(angle))], axis=0)
    weight = np.where((k1 == 0) | (k1 == blocks), 1.0, 2.0)[:, None] / length
    unmix = np.concatenate(
        [spread(weight * np.cos(angle)), spread(-weight * np.sin(angle))], axis=0
    ).T
    row = np.arange(rows)
    turn = 2.0 * np.pi * ((k1[:, None] * row[None, :]) % length) / length
    turn = np.pad(np.repeat(turn, width, axis=0), ((0, padded - kept * width), (0, 0)))
    inner = 2.0 * np.pi * ((row[:, None] * row[None, :]) % rows) / rows
    cos, sin = np.cos(inner), np.sin(inner)
    forward = np.block([[cos, -sin], [sin, cos]])
    inverse = np.block([[cos, sin], [-sin, cos]])
    turn = np.concatenate([np.cos(turn), np.sin(turn)], axis=1).astype(np.float32)
    return [split_pair(matrix) for matrix in (mix, forward, inverse, unmix)], turn


def packed(tables):
    width = max(min(high.shape) for high, _ in tables)
    slabs, places, first = [], [], 0
    for pair in tables:
        for table in pair:
            pieces = []
            for start in range(0, table.shape[1], width):
                slab = table[:, start : start + width]
                pieces.append((first, slab.shape))
                first += slab.shape[0]
                slabs.append(np.pad(slab, ((0, 0), (0, width - slab.shape[1]))))
            places.append(pieces)
    return np.concatenate(slabs, axis=0), places


def halves(value):
    high = value.astype(jnp.bfloat16)
    return high, (value - high.astype(jnp.float32)).astype(jnp.bfloat16)


def dot32(left, right):
    (lh, ll), (rh, rl) = left, right
    dot = functools.partial(jnp.dot, preferred_element_type=jnp.float32)
    return dot(lh, rh) + (dot(lh, rl) + dot(ll, rh))


def layout_kernel(x_ref, *moved_refs):
    far, _, _, part = moved_refs[0].shape
    device = lax.axis_index("seq")
    for chip in range(far * SIDE):
        distance = (chip // SIDE) ^ (device // (2 * SIDE))
        near = (chip % SIDE) ^ ((device // 2) % SIDE)
        for which, moved_ref in enumerate(moved_refs):

            @pl.when(near == which)
            def _():
                for c in range(2):
                    first = (2 * chip + c) * part
                    moved_ref[distance, (device % 2) ^ c] = x_ref[:, first : first + part].astype(
                        jnp.float32
                    )


def project_kernel(scaling, x_ref, w_ref, taps_ref, go_ref, *refs):
    sig_ref, kv_ref, acc = refs[-3:]
    step = pl.program_id(0)
    product = jnp.dot(x_ref[...], w_ref[...], preferred_element_type=jnp.float32)

    @pl.when(step == 0)
    def _():
        acc[...] = product

    @pl.when(step > 0)
    def _():
        acc[...] += product

    @pl.when(step == pl.num_programs(0) - 1)
    def _():
        count, _, width, _ = sig_ref.shape
        channels = count * width
        projected = acc[...].astype(jnp.bfloat16).astype(jnp.float32).T
        query = projected[:channels]
        key = projected[channels : 2 * channels]
        value = projected[2 * channels :]
        go = go_ref[...].astype(jnp.float32).T
        signals = ((taps_ref[...] * scaling).T, key * value, go * query)
        for which, signal in enumerate(signals):
            for owner in range(count):
                sig_ref[owner, which] = signal[owner * width : (owner + 1) * width]
        kv_ref[0] = go
        kv_ref[1] = value
        kv_ref[2] = key


def conv_kernel(places, x_ref, table_ref, turn_ref, *refs):
    y_ref, flat = refs[-2:]
    blocks, _, width, rows = x_ref.shape

    def table(which):
        slabs = [table_ref[at : at + shape[0], : shape[1]] for at, shape in places[which]]
        return slabs[0] if len(slabs) == 1 else jnp.concatenate(slabs, axis=1)

    m_h, m_l, f_h, f_l, i_h, i_l, u_h, u_l = [functools.partial(table, w) for w in range(8)]
    for p in range(blocks):
        for s in range(3):
            flat[p * width : (p + 1) * width, s * rows : (s + 1) * rows] = x_ref[p, s]
    turn_re, turn_im = turn_ref[:, :rows], turn_ref[:, rows:]
    count = turn_re.shape[0]
    mixed = dot32((m_h(), m_l()), halves(flat[...]))
    turned = []
    for s in range(3):
        re = mixed[:count, s * rows : (s + 1) * rows]
        im = mixed[count:, s * rows : (s + 1) * rows]
        turned.append(
            jnp.concatenate([re * turn_re + im * turn_im, im * turn_re - re * turn_im], axis=1)
        )
    spectrum = dot32(halves(jnp.concatenate(turned, axis=0)), (f_h(), f_l()))
    (k_re, k_im), (g_re, g_im), (b_re, b_im) = [
        (spectrum[s * count : (s + 1) * count, :rows], spectrum[s * count : (s + 1) * count, rows:])
        for s in range(3)
    ]
    products = jnp.concatenate(
        [
            jnp.concatenate([k_re * g_re - k_im * g_im, k_re * g_im + k_im * g_re], axis=1),
            jnp.concatenate([k_re * b_re + k_im * b_im, k_re * b_im - k_im * b_re], axis=1),
            jnp.concatenate([b_re * g_re + b_im * g_im, b_im * g_re - b_re * g_im], axis=1),
        ],
        axis=0,
    )
    back = dot32(halves(products), (i_h(), i_l()))
    parts_re, parts_im = [], []
    for s in range(3):
        re = back[s * count : (s + 1) * count, :rows]
        im = back[s * count : (s + 1) * count, rows:]
        parts_re.append(re * turn_re - im * turn_im)
        parts_im.append(im * turn_re + re * turn_im)
    stacked = jnp.concatenate(
        [jnp.concatenate(parts_re, axis=1), jnp.concatenate(parts_im, axis=1)], axis=0
    )
    result = dot32((u_h(), u_l()), halves(stacked))
    for p in range(blocks):
        for s in range(3):
            y_ref[p, s] = result[p * width : (p + 1) * width, s * rows : (s + 1) * rows]


def gate_first_kernel(y_ref, kv_ref, *refs):
    gp_ref, sent_ref, flat = refs[-3:]
    count, _, width, _ = y_ref.shape
    for owner in range(count):
        flat[owner * width : (owner + 1) * width] = y_ref[owner, 0]
    rounded = (kv_ref[0] * flat[...]).T.astype(jnp.bfloat16)
    gp_ref[...] = rounded
    sent_ref[...] = rounded.astype(jnp.float32)


def gate_rest_kernel(scaling, y_ref, kv_ref, first_ref, *refs):
    gp_ref, sent_ref, taps_ref, flat = refs[-4:]
    count, _, width, _ = y_ref.shape
    channels = count * width
    for s in range(2):
        for owner in range(count):
            flat[s, owner * width : (owner + 1) * width] = y_ref[owner, s + 1]
    gp_ref[:, :channels] = first_ref[...]
    for index in range(2):
        rounded = (kv_ref[index + 1] * flat[0]).T.astype(jnp.bfloat16)
        gp_ref[:, (index + 1) * channels : (index + 2) * channels] = rounded
        sent_ref[:, index * channels : (index + 1) * channels] = rounded.astype(jnp.float32)
    taps_ref[...] = flat[1].T * scaling


def turn_kernel(*refs):
    x_refs, out_refs = refs[:SIDE], refs[SIDE:]
    far, _, rows, part = x_refs[0].shape
    for which, x_ref in enumerate(x_refs):
        for core, out_ref in enumerate(out_refs):
            for f in range(far):
                out_ref[f * part : (f + 1) * part, which * rows : (which + 1) * rows] = (
                    x_ref[f, core].T.astype(jnp.bfloat16)
                )


def joined(gp_refs):
    return jnp.concatenate([gp_ref[...].astype(jnp.bfloat16) for gp_ref in gp_refs], axis=0)


def other_kernel(x_ref, *refs):
    gp_refs, out_ref = refs[:SIDE], refs[-1]
    out_ref[...] = jnp.dot(x_ref[...], joined(gp_refs), preferred_element_type=jnp.float32)


def own_kernel(x_ref, *refs):
    gp_refs, add_ref, out_refs = refs[:SIDE], refs[SIDE], refs[SIDE + 1 :]
    gp = joined(gp_refs)
    part = out_refs[0].shape[0]
    for which, out_ref in enumerate(out_refs):
        span = slice(which * part, (which + 1) * part)
        product = jnp.dot(x_ref[span], gp, preferred_element_type=jnp.float32)
        out_ref[...] = product + add_ref[span]


def sum_kernel(scaling, groups, *refs):
    *in_refs, out_ref = refs
    terms = len(in_refs) // groups
    first = 0
    for group in range(groups):
        total = in_refs[group * terms][...]
        for in_ref in in_refs[group * terms + 1 : (group + 1) * terms]:
            total = total + in_ref[...]
        out_ref[:, first : first + total.shape[1]] = total * scaling
        first += total.shape[1]


def per_device(inputs, in_weight, filter_taps, grad_out):
    rows, depth = inputs.shape
    channels = filter_taps.shape[1]
    columns = in_weight.shape[1]
    blocks = lax.axis_size("seq")
    width = channels // blocks
    part = depth // blocks
    far = blocks // (2 * SIDE)
    chunk = min(1024, depth)
    steps = depth // chunk
    scaling = 1.0 / math.sqrt(rows * blocks)
    f32, bf16 = jnp.float32, jnp.bfloat16
    params = pltpu.CompilerParams(vmem_limit_bytes=VMEM_LIMIT)
    wide = pltpu.CompilerParams(vmem_limit_bytes=VMEM_WIDE)

    def shaped(*shape, dtype=f32):
        return jax.ShapeDtypeStruct(shape, dtype)

    def exchange(value, flip):
        return lax.ppermute(value, "seq", [(i, i ^ flip) for i in range(blocks)])

    def gather(value):
        near, far_one = exchange(value, 2), exchange(value, 4)
        return [value, near, far_one, exchange(far_one, 2)]

    anywhere = pl.BlockSpec(memory_space=pl.ANY)
    inside = pl.BlockSpec(memory_space=pltpu.VMEM)
    moved = pl.pallas_call(
        layout_kernel,
        out_shape=[shaped(far, 2, rows, part)] * SIDE,
        compiler_params=wide,
    )(inputs)
    held = [moved[0]] + [exchange(moved[k], 2 * k) for k in range(1, SIDE)]
    signals, gates = pl.pallas_call(
        functools.partial(project_kernel, scaling),
        grid=(steps,),
        in_specs=[
            pl.BlockSpec((rows, chunk), lambda i: (0, i)),
            pl.BlockSpec((chunk, columns), lambda i: (i, 0)),
            pl.BlockSpec((rows, channels), lambda i: (0, 0)),
            pl.BlockSpec((rows, channels), lambda i: (0, 0)),
        ],
        out_specs=[
            pl.BlockSpec((blocks, 3, width, rows), lambda i: (0, 0, 0, 0)),
            pl.BlockSpec((3, channels, rows), lambda i: (0, 0, 0)),
        ],
        out_shape=[shaped(blocks, 3, width, rows), shaped(3, channels, rows)],
        scratch_shapes=[pltpu.VMEM((rows, columns), f32)],
        compiler_params=wide,
        cost_estimate=pl.CostEstimate(
            flops=2 * rows * depth * columns,
            bytes_accessed=2 * depth * (rows + columns),
            transcendentals=0,
        ),
    )(inputs, in_weight, filter_taps, grad_out)

    signals = lax.all_to_all(signals, "seq", split_axis=0, concat_axis=0, tiled=True)
    pairs, turn = transform_tables(blocks, width, rows)
    table, places = packed(pairs)
    results = pl.pallas_call(
        functools.partial(conv_kernel, places),
        in_specs=[inside] * 3 + [anywhere] * 2,
        out_shape=shaped(blocks, 3, width, rows),
        scratch_shapes=[pltpu.VMEM((blocks * width, 3 * rows), f32)],
        compiler_params=wide,
    )(signals, jnp.asarray(table), jnp.asarray(turn), *held[1:3])
    results = lax.all_to_all(results, "seq", split_axis=0, concat_axis=0, tiled=True)
    first, sent_first = pl.pallas_call(
        gate_first_kernel,
        in_specs=[inside] * 2 + [anywhere],
        out_shape=[shaped(rows, channels, dtype=bf16), shaped(rows, channels)],
        scratch_shapes=[pltpu.VMEM((channels, rows), f32)],
        compiler_params=params,
    )(results, gates, held[3])
    gathered_first = gather(sent_first)
    grad_proj, sent_rest, grad_taps = pl.pallas_call(
        functools.partial(gate_rest_kernel, scaling),
        out_shape=[
            shaped(rows, columns, dtype=bf16),
            shaped(rows, 2 * channels),
            shaped(rows, channels),
        ],
        scratch_shapes=[pltpu.VMEM((2, channels, rows), f32)],
        compiler_params=params,
    )(results, gates, first)
    gathered_rest = gather(sent_rest)
    turned = pl.pallas_call(
        turn_kernel,
        out_shape=[shaped(far * part, SIDE * rows, dtype=bf16)] * 2,
        compiler_params=params,
        cost_estimate=pl.CostEstimate(
            flops=0, bytes_accessed=10 * SIDE * far * rows * part, transcendentals=0
        ),
    )(*held)
    grad_inputs = lax.dot_general(
        grad_proj, in_weight, (((1,), (1,)), ((), ())), preferred_element_type=f32
    ).astype(bf16)
    terms = []
    for gathered in (gathered_first, gathered_rest):
        cols = gathered[0].shape[1]
        cost = pl.CostEstimate(
            flops=2 * far * part * SIDE * rows * cols,
            bytes_accessed=4 * far * part * cols,
            transcendentals=0,
        )
        other = pl.pallas_call(
            other_kernel,
            in_specs=[inside] * (1 + SIDE) + [anywhere] * len(terms[1:]),
            out_shape=shaped(far * part, cols),
            compiler_params=params,
            cost_estimate=cost,
        )(turned[1], *gathered, *terms[1:])
        kept, *leaving = pl.pallas_call(
            own_kernel,
            out_shape=[shaped(part, cols)] * far,
            compiler_params=params,
            cost_estimate=cost,
        )(turned[0], *gathered, exchange(other, 1))
        terms += [kept] + [exchange(v, 2 * SIDE * (k + 1)) for k, v in enumerate(leaving)]
    grad_weight = pl.pallas_call(
        functools.partial(sum_kernel, scaling, 2),
        out_shape=shaped(part, columns),
        compiler_params=params,
    )(*terms)
    return grad_inputs, grad_weight, grad_taps


def solution(mesh):
    in_specs = (P(("grp", "seq"), None), P(), P("seq", None), P(("grp", "seq"), None))
    out_specs = (P(("grp", "seq"), None), P(("grp", "seq"), None), P(("grp", "seq"), None))
    return jax.shard_map(
        per_device, mesh=mesh, in_specs=in_specs, out_specs=out_specs, check_vma=False
    )
```

```python
import functools
import math

import jax
import jax.numpy as jnp
import numpy as np
from jax import lax
from jax.experimental import pallas as pl
from jax.experimental.pallas import tpu as pltpu
from jax.sharding import PartitionSpec as P

VMEM_LIMIT = 48 * 1024 * 1024
VMEM_WIDE = 60 * 1024 * 1024
SIDE = 4


def split_pair(table):
    high = table.astype(np.float32).astype(jnp.bfloat16)
    low = (table - high.astype(np.float64)).astype(np.float32).astype(jnp.bfloat16)
    return high, low


def transform_tables(blocks, width, rows):
    length = 2 * blocks * rows
    kept = blocks + 1
    padded = -(-kept * width // 16) * 16
    k1 = np.arange(kept)
    block = np.arange(blocks)
    angle = 2.0 * np.pi * ((k1[:, None] * block[None, :]) % (2 * blocks)) / (2 * blocks)
    eye = np.eye(width)

    def spread(matrix):
        wide = np.kron(matrix, eye)
        return np.pad(wide, ((0, padded - wide.shape[0]), (0, 0)))

    mix = np.concatenate([spread(np.cos(angle)), spread(-np.sin(angle))], axis=0)
    weight = np.where((k1 == 0) | (k1 == blocks), 1.0, 2.0)[:, None] / length
    unmix = np.concatenate(
        [spread(weight * np.cos(angle)), spread(-weight * np.sin(angle))], axis=0
    ).T
    row = np.arange(rows)
    turn = 2.0 * np.pi * ((k1[:, None] * row[None, :]) % length) / length
    turn = np.pad(np.repeat(turn, width, axis=0), ((0, padded - kept * width), (0, 0)))
    inner = 2.0 * np.pi * ((row[:, None] * row[None, :]) % rows) / rows
    cos, sin = np.cos(inner), np.sin(inner)
    forward = np.block([[cos, -sin], [sin, cos]])
    inverse = np.block([[cos, sin], [-sin, cos]])
    turn = np.concatenate([np.cos(turn), np.sin(turn)], axis=1).astype(np.float32)
    return [split_pair(matrix) for matrix in (mix, forward, inverse, unmix)], turn


def packed(tables):
    width = max(min(high.shape) for high, _ in tables)
    slabs, places, first = [], [], 0
    for pair in tables:
        for table in pair:
            pieces = []
            for start in range(0, table.shape[1], width):
                slab = table[:, start : start + width]
                pieces.append((first, slab.shape))
                first += slab.shape[0]
                slabs.append(np.pad(slab, ((0, 0), (0, width - slab.shape[1]))))
            places.append(pieces)
    return np.concatenate(slabs, axis=0), places


def halves(value):
    high = value.astype(jnp.bfloat16)
    return high, (value - high.astype(jnp.float32)).astype(jnp.bfloat16)


def dot32(left, right):
    (lh, ll), (rh, rl) = left, right
    dot = functools.partial(jnp.dot, preferred_element_type=jnp.float32)
    return dot(lh, rh) + (dot(lh, rl) + dot(ll, rh))


def layout_kernel(x_ref, own_ref, y_ref, z_ref):
    _, far, _, part = own_ref.shape
    device = lax.axis_index("seq")
    places = {
        (0, 0): (own_ref, 0),
        (0, 1): (own_ref, 1),
        (1, 0): (y_ref, 0),
        (3, 0): (y_ref, 1),
        (1, 1): (y_ref, 2),
        (2, 1): (z_ref, 0),
        (3, 1): (z_ref, 1),
        (2, 0): (z_ref, 2),
    }
    for chip in range(far * SIDE):
        distance = (chip // SIDE) ^ (device // (2 * SIDE))
        near = (chip % SIDE) ^ ((device // 2) % SIDE)
        for core in range(2):
            first = (2 * chip + core) * part
            flip = (device % 2) ^ core
            for (side, cross), (out_ref, slot) in places.items():

                @pl.when((near == side) & (flip == cross))
                def _():
                    out_ref[slot, distance] = x_ref[:, first : first + part].astype(jnp.float32)


def project_kernel(scaling, x_ref, w_ref, taps_ref, go_ref, *refs):
    sig_ref, go_out_ref, key_ref, value_ref, acc = refs[-5:]
    step = pl.program_id(0)
    product = jnp.dot(x_ref[...], w_ref[...], preferred_element_type=jnp.float32)

    @pl.when(step == 0)
    def _():
        acc[...] = product

    @pl.when(step > 0)
    def _():
        acc[...] += product

    @pl.when(step == pl.num_programs(0) - 1)
    def _():
        count, _, width, _ = sig_ref.shape
        channels = count * width
        projected = acc[...].astype(jnp.bfloat16).astype(jnp.float32).T
        query = projected[:channels]
        key = projected[channels : 2 * channels]
        value = projected[2 * channels :]
        go = go_ref[...].astype(jnp.float32).T
        signals = ((taps_ref[...] * scaling).T, key * value, go * query)
        for which, signal in enumerate(signals):
            for owner in range(count):
                sig_ref[owner, which] = signal[owner * width : (owner + 1) * width]
        go_out_ref[...] = go
        key_ref[...] = key
        value_ref[...] = value


def conv_kernel(places, x_ref, table_ref, turn_ref, *refs):
    y_ref, flat = refs[-2:]
    blocks, _, width, rows = x_ref.shape

    def table(which):
        slabs = [table_ref[at : at + shape[0], : shape[1]] for at, shape in places[which]]
        return slabs[0] if len(slabs) == 1 else jnp.concatenate(slabs, axis=1)

    m_h, m_l, f_h, f_l, i_h, i_l, u_h, u_l = [functools.partial(table, w) for w in range(8)]
    for p in range(blocks):
        for s in range(3):
            flat[p * width : (p + 1) * width, s * rows : (s + 1) * rows] = x_ref[p, s]
    turn_re, turn_im = turn_ref[:, :rows], turn_ref[:, rows:]
    count = turn_re.shape[0]
    mixed = dot32((m_h(), m_l()), halves(flat[...]))
    turned = []
    for s in range(3):
        re = mixed[:count, s * rows : (s + 1) * rows]
        im = mixed[count:, s * rows : (s + 1) * rows]
        turned.append(
            jnp.concatenate([re * turn_re + im * turn_im, im * turn_re - re * turn_im], axis=1)
        )
    spectrum = dot32(halves(jnp.concatenate(turned, axis=0)), (f_h(), f_l()))
    (k_re, k_im), (g_re, g_im), (b_re, b_im) = [
        (spectrum[s * count : (s + 1) * count, :rows], spectrum[s * count : (s + 1) * count, rows:])
        for s in range(3)
    ]
    products = jnp.concatenate(
        [
            jnp.concatenate([k_re * g_re - k_im * g_im, k_re * g_im + k_im * g_re], axis=1),
            jnp.concatenate([k_re * b_re + k_im * b_im, k_re * b_im - k_im * b_re], axis=1),
            jnp.concatenate([b_re * g_re + b_im * g_im, b_im * g_re - b_re * g_im], axis=1),
        ],
        axis=0,
    )
    back = dot32(halves(products), (i_h(), i_l()))
    parts_re, parts_im = [], []
    for s in range(3):
        re = back[s * count : (s + 1) * count, :rows]
        im = back[s * count : (s + 1) * count, rows:]
        parts_re.append(re * turn_re - im * turn_im)
        parts_im.append(im * turn_re + re * turn_im)
    stacked = jnp.concatenate(
        [jnp.concatenate(parts_re, axis=1), jnp.concatenate(parts_im, axis=1)], axis=0
    )
    result = dot32((u_h(), u_l()), halves(stacked))
    for p in range(blocks):
        for s in range(3):
            y_ref[p, s] = result[p * width : (p + 1) * width, s * rows : (s + 1) * rows]


def gate_first_kernel(y_ref, go_ref, gp_ref, sent_ref, flat):
    count, _, width, _ = y_ref.shape
    for owner in range(count):
        flat[owner * width : (owner + 1) * width] = y_ref[owner, 0]
    rounded = (go_ref[...] * flat[...]).T.astype(jnp.bfloat16)
    gp_ref[...] = rounded
    sent_ref[...] = rounded.astype(jnp.float32)


def gate_rest_kernel(scaling, y_ref, key_ref, value_ref, first_ref, *refs):
    gp_ref, sent_ref, taps_ref, flat = refs
    count, _, width, _ = y_ref.shape
    channels = count * width
    for s in range(2):
        for owner in range(count):
            flat[s, owner * width : (owner + 1) * width] = y_ref[owner, s + 1]
    gp_ref[:, :channels] = first_ref[...]
    for index, factor_ref in enumerate((value_ref, key_ref)):
        rounded = (factor_ref[...] * flat[0]).T.astype(jnp.bfloat16)
        gp_ref[:, (index + 1) * channels : (index + 2) * channels] = rounded
        sent_ref[:, index * channels : (index + 1) * channels] = rounded.astype(jnp.float32)
    taps_ref[...] = flat[1].T * scaling


def relay_kernel(x_ref, *refs):
    refs[-1][...] = x_ref[...]


def turn_kernel(own_ref, y_ref, z_ref, corner_own_ref, corner_other_ref, *out_refs):
    _, far, rows, part = own_ref.shape
    sources = (
        ((own_ref, 0), (y_ref, 0), (z_ref, 2), (corner_own_ref, 0)),
        ((own_ref, 1), (y_ref, 2), (z_ref, 0), (corner_other_ref, 0)),
    )
    for out_ref, chips in zip(out_refs, sources):
        for which, (x_ref, slot) in enumerate(chips):
            for f in range(far):
                out_ref[f * part : (f + 1) * part, which * rows : (which + 1) * rows] = (
                    x_ref[slot, f].T.astype(jnp.bfloat16)
                )


def joined(gp_refs):
    return jnp.concatenate([gp_ref[...].astype(jnp.bfloat16) for gp_ref in gp_refs], axis=0)


def other_kernel(x_ref, *refs):
    gp_refs, out_ref = refs[:SIDE], refs[-1]
    out_ref[...] = jnp.dot(x_ref[...], joined(gp_refs), preferred_element_type=jnp.float32)


def own_kernel(x_ref, *refs):
    gp_refs, add_ref, out_refs = refs[:SIDE], refs[SIDE], refs[SIDE + 1 :]
    gp = joined(gp_refs)
    part = out_refs[0].shape[0]
    for which, out_ref in enumerate(out_refs):
        span = slice(which * part, (which + 1) * part)
        product = jnp.dot(x_ref[span], gp, preferred_element_type=jnp.float32)
        out_ref[...] = product + add_ref[span]


def sum_kernel(scaling, groups, *refs):
    *in_refs, out_ref = refs
    terms = len(in_refs) // groups
    first = 0
    for group in range(groups):
        total = in_refs[group * terms][...]
        for in_ref in in_refs[group * terms + 1 : (group + 1) * terms]:
            total = total + in_ref[...]
        out_ref[:, first : first + total.shape[1]] = total * scaling
        first += total.shape[1]


def per_device(inputs, in_weight, filter_taps, grad_out):
    rows, depth = inputs.shape
    channels = filter_taps.shape[1]
    columns = in_weight.shape[1]
    blocks = lax.axis_size("seq")
    width = channels // blocks
    part = depth // blocks
    far = blocks // (2 * SIDE)
    chunk = min(1024, depth)
    steps = depth // chunk
    scaling = 1.0 / math.sqrt(rows * blocks)
    f32, bf16 = jnp.float32, jnp.bfloat16
    params = pltpu.CompilerParams(vmem_limit_bytes=VMEM_LIMIT)
    wide = pltpu.CompilerParams(vmem_limit_bytes=VMEM_WIDE)

    def shaped(*shape, dtype=f32):
        return jax.ShapeDtypeStruct(shape, dtype)

    def exchange(value, flip):
        return lax.ppermute(value, "seq", [(i, i ^ flip) for i in range(blocks)])

    anywhere = pl.BlockSpec(memory_space=pl.ANY)
    inside = pl.BlockSpec(memory_space=pltpu.VMEM)
    own, to_y, to_z = pl.pallas_call(
        layout_kernel,
        out_shape=[shaped(2, far, rows, part)] + [shaped(3, far, rows, part)] * 2,
        compiler_params=wide,
    )(inputs)
    from_y, from_z = exchange(to_y, 2), exchange(to_z, 4)
    corners = exchange(from_y[1:2], 4), exchange(from_z[1:2], 2)
    held = (own, from_y, from_z) + corners
    signals, gate_out, key, value = pl.pallas_call(
        functools.partial(project_kernel, scaling),
        grid=(steps,),
        in_specs=[
            pl.BlockSpec((rows, chunk), lambda i: (0, i)),
            pl.BlockSpec((chunk, columns), lambda i: (i, 0)),
            pl.BlockSpec((rows, channels), lambda i: (0, 0)),
            pl.BlockSpec((rows, channels), lambda i: (0, 0)),
        ],
        out_specs=[
            pl.BlockSpec((blocks, 3, width, rows), lambda i: (0, 0, 0, 0)),
            ]
        + [pl.BlockSpec((channels, rows), lambda i: (0, 0))] * 3,
        out_shape=[shaped(blocks, 3, width, rows)] + [shaped(channels, rows)] * 3,
        scratch_shapes=[pltpu.VMEM((rows, columns), f32)],
        compiler_params=wide,
        cost_estimate=pl.CostEstimate(
            flops=2 * rows * depth * columns,
            bytes_accessed=2 * depth * (rows + columns),
            transcendentals=0,
        ),
    )(inputs, in_weight, filter_taps, grad_out)

    signals = lax.all_to_all(signals, "seq", split_axis=0, concat_axis=0, tiled=True)
    pairs, turn = transform_tables(blocks, width, rows)
    table, places = packed(pairs)
    results = pl.pallas_call(
        functools.partial(conv_kernel, places),
        in_specs=[inside] * 3 + [anywhere] * 2,
        out_shape=shaped(blocks, 3, width, rows),
        scratch_shapes=[pltpu.VMEM((blocks * width, 3 * rows), f32)],
        compiler_params=params,
    )(signals, jnp.asarray(table), jnp.asarray(turn), *corners)
    results = lax.all_to_all(results, "seq", split_axis=0, concat_axis=0, tiled=True)
    first, sent_first = pl.pallas_call(
        gate_first_kernel,
        out_shape=[shaped(rows, channels, dtype=bf16), shaped(rows, channels)],
        scratch_shapes=[pltpu.VMEM((channels, rows), f32)],
        compiler_params=params,
    )(results, gate_out)
    grad_proj, sent_rest, grad_taps = pl.pallas_call(
        functools.partial(gate_rest_kernel, scaling),
        out_shape=[
            shaped(rows, columns, dtype=bf16),
            shaped(rows, 2 * channels),
            shaped(rows, channels),
        ],
        scratch_shapes=[pltpu.VMEM((2, channels, rows), f32)],
        compiler_params=params,
    )(results, key, value, first)
    turned = pl.pallas_call(
        turn_kernel,
        out_shape=[shaped(far * part, SIDE * rows, dtype=bf16)] * 2,
        compiler_params=params,
        cost_estimate=pl.CostEstimate(
            flops=0, bytes_accessed=10 * SIDE * far * rows * part, transcendentals=0
        ),
    )(*held)
    grad_inputs = lax.dot_general(
        grad_proj, in_weight, (((1,), (1,)), ((), ())), preferred_element_type=f32
    ).astype(bf16)
    terms = []
    for block in (sent_first, sent_rest):
        cols = block.shape[1]
        from_far = exchange(block, 4)
        relayed = from_far
        if terms:
            relayed = pl.pallas_call(
                relay_kernel,
                in_specs=[inside, anywhere],
                out_shape=shaped(rows, cols),
                compiler_params=params,
            )(from_far, terms[0])
        gathered = [block, exchange(block, 2), from_far, exchange(relayed, 2)]
        cost = pl.CostEstimate(
            flops=2 * far * part * SIDE * rows * cols,
            bytes_accessed=4 * far * part * cols,
            transcendentals=0,
        )
        other = pl.pallas_call(
            other_kernel,
            in_specs=[inside] * (1 + SIDE) + [anywhere] * len(terms[1:]),
            out_shape=shaped(far * part, cols),
            compiler_params=params,
            cost_estimate=cost,
        )(turned[1], *gathered, *terms[1:])
        kept, *leaving = pl.pallas_call(
            own_kernel,
            out_shape=[shaped(part, cols)] * far,
            compiler_params=params,
            cost_estimate=cost,
        )(turned[0], *gathered, exchange(other, 1))
        terms += [kept] + [exchange(v, 2 * SIDE * (k + 1)) for k, v in enumerate(leaving)]
    grad_weight = pl.pallas_call(
        functools.partial(sum_kernel, scaling, 2),
        out_shape=shaped(part, columns),
        compiler_params=params,
    )(*terms)
    return grad_inputs, grad_weight, grad_taps


def solution(mesh):
    in_specs = (P(("grp", "seq"), None), P(), P("seq", None), P(("grp", "seq"), None))
    out_specs = (P(("grp", "seq"), None), P(("grp", "seq"), None), P(("grp", "seq"), None))
    return jax.shard_map(
        per_device, mesh=mesh, in_specs=in_specs, out_specs=out_specs, check_vma=False
    )
```

```python
import functools
import math

import jax
import jax.numpy as jnp
import numpy as np
from jax import lax
from jax.experimental import pallas as pl
from jax.experimental.pallas import tpu as pltpu
from jax.sharding import PartitionSpec as P

VMEM_LIMIT = 48 * 1024 * 1024
VMEM_WIDE = 60 * 1024 * 1024
SIDE = 4


def split_pair(table):
    high = table.astype(np.float32).astype(jnp.bfloat16)
    low = (table - high.astype(np.float64)).astype(np.float32).astype(jnp.bfloat16)
    return high, low


def transform_tables(blocks, width, rows):
    length = 2 * blocks * rows
    kept = blocks + 1
    padded = -(-kept * width // 16) * 16
    k1 = np.arange(kept)
    block = np.arange(blocks)
    angle = 2.0 * np.pi * ((k1[:, None] * block[None, :]) % (2 * blocks)) / (2 * blocks)
    eye = np.eye(width)

    def spread(matrix):
        wide = np.kron(matrix, eye)
        return np.pad(wide, ((0, padded - wide.shape[0]), (0, 0)))

    mix = np.concatenate([spread(np.cos(angle)), spread(-np.sin(angle))], axis=0)
    weight = np.where((k1 == 0) | (k1 == blocks), 1.0, 2.0)[:, None] / length
    unmix = np.concatenate(
        [spread(weight * np.cos(angle)), spread(-weight * np.sin(angle))], axis=0
    ).T
    row = np.arange(rows)
    turn = 2.0 * np.pi * ((k1[:, None] * row[None, :]) % length) / length
    turn = np.pad(np.repeat(turn, width, axis=0), ((0, padded - kept * width), (0, 0)))
    inner = 2.0 * np.pi * ((row[:, None] * row[None, :]) % rows) / rows
    cos, sin = np.cos(inner), np.sin(inner)
    forward = np.block([[cos, -sin], [sin, cos]])
    inverse = np.block([[cos, sin], [-sin, cos]])
    turn = np.concatenate([np.cos(turn), np.sin(turn)], axis=1).astype(np.float32)
    return [split_pair(matrix) for matrix in (mix, forward, inverse, unmix)], turn


def packed(tables):
    width = max(min(high.shape) for high, _ in tables)
    slabs, places, first = [], [], 0
    for pair in tables:
        for table in pair:
            pieces = []
            for start in range(0, table.shape[1], width):
                slab = table[:, start : start + width]
                pieces.append((first, slab.shape))
                first += slab.shape[0]
                slabs.append(np.pad(slab, ((0, 0), (0, width - slab.shape[1]))))
            places.append(pieces)
    return np.concatenate(slabs, axis=0), places


def halves(value):
    high = value.astype(jnp.bfloat16)
    return high, (value - high.astype(jnp.float32)).astype(jnp.bfloat16)


def dot32(left, right):
    (lh, ll), (rh, rl) = left, right
    dot = functools.partial(jnp.dot, preferred_element_type=jnp.float32)
    return dot(lh, rh) + (dot(lh, rl) + dot(ll, rh))


def layout_kernel(x_ref, own_ref, y_ref, z_ref):
    _, far, _, part = own_ref.shape
    device = lax.axis_index("seq")
    places = {
        (0, 0): (own_ref, 0),
        (0, 1): (own_ref, 1),
        (1, 0): (y_ref, 0),
        (3, 0): (y_ref, 1),
        (1, 1): (y_ref, 2),
        (2, 1): (z_ref, 0),
        (3, 1): (z_ref, 1),
        (2, 0): (z_ref, 2),
    }
    for chip in range(far * SIDE):
        distance = (chip // SIDE) ^ (device // (2 * SIDE))
        near = (chip % SIDE) ^ ((device // 2) % SIDE)
        for core in range(2):
            first = (2 * chip + core) * part
            flip = (device % 2) ^ core
            for (side, cross), (out_ref, slot) in places.items():

                @pl.when((near == side) & (flip == cross))
                def _():
                    out_ref[slot, distance] = x_ref[:, first : first + part].astype(jnp.float32)


def project_kernel(scaling, x_ref, w_ref, taps_ref, go_ref, *refs):
    sig_ref, go_out_ref, key_ref, value_ref, acc = refs[-5:]
    step = pl.program_id(0)
    product = jnp.dot(x_ref[...], w_ref[...], preferred_element_type=jnp.float32)

    @pl.when(step == 0)
    def _():
        acc[...] = product

    @pl.when(step > 0)
    def _():
        acc[...] += product

    @pl.when(step == pl.num_programs(0) - 1)
    def _():
        count, _, width, _ = sig_ref.shape
        channels = count * width
        projected = acc[...].astype(jnp.bfloat16).astype(jnp.float32).T
        query = projected[:channels]
        key = projected[channels : 2 * channels]
        value = projected[2 * channels :]
        go = go_ref[...].astype(jnp.float32).T
        signals = ((taps_ref[...] * scaling).T, key * value, go * query)
        for which, signal in enumerate(signals):
            for owner in range(count):
                sig_ref[owner, which] = signal[owner * width : (owner + 1) * width]
        go_out_ref[...] = go
        key_ref[...] = key
        value_ref[...] = value


def conv_kernel(places, x_ref, table_ref, turn_ref, *refs):
    y_ref, flat = refs[-2:]
    blocks, _, width, rows = x_ref.shape

    def table(which):
        slabs = [table_ref[at : at + shape[0], : shape[1]] for at, shape in places[which]]
        return slabs[0] if len(slabs) == 1 else jnp.concatenate(slabs, axis=1)

    m_h, m_l, f_h, f_l, i_h, i_l, u_h, u_l = [functools.partial(table, w) for w in range(8)]
    for p in range(blocks):
        for s in range(3):
            flat[p * width : (p + 1) * width, s * rows : (s + 1) * rows] = x_ref[p, s]
    turn_re, turn_im = turn_ref[:, :rows], turn_ref[:, rows:]
    count = turn_re.shape[0]
    mixed = dot32((m_h(), m_l()), halves(flat[...]))
    turned = []
    for s in range(3):
        re = mixed[:count, s * rows : (s + 1) * rows]
        im = mixed[count:, s * rows : (s + 1) * rows]
        turned.append(
            jnp.concatenate([re * turn_re + im * turn_im, im * turn_re - re * turn_im], axis=1)
        )
    spectrum = dot32(halves(jnp.concatenate(turned, axis=0)), (f_h(), f_l()))
    (k_re, k_im), (g_re, g_im), (b_re, b_im) = [
        (spectrum[s * count : (s + 1) * count, :rows], spectrum[s * count : (s + 1) * count, rows:])
        for s in range(3)
    ]
    products = jnp.concatenate(
        [
            jnp.concatenate([k_re * g_re - k_im * g_im, k_re * g_im + k_im * g_re], axis=1),
            jnp.concatenate([k_re * b_re + k_im * b_im, k_re * b_im - k_im * b_re], axis=1),
            jnp.concatenate([b_re * g_re + b_im * g_im, b_im * g_re - b_re * g_im], axis=1),
        ],
        axis=0,
    )
    back = dot32(halves(products), (i_h(), i_l()))
    parts_re, parts_im = [], []
    for s in range(3):
        re = back[s * count : (s + 1) * count, :rows]
        im = back[s * count : (s + 1) * count, rows:]
        parts_re.append(re * turn_re - im * turn_im)
        parts_im.append(im * turn_re + re * turn_im)
    stacked = jnp.concatenate(
        [jnp.concatenate(parts_re, axis=1), jnp.concatenate(parts_im, axis=1)], axis=0
    )
    result = dot32((u_h(), u_l()), halves(stacked))
    for p in range(blocks):
        for s in range(3):
            y_ref[p, s] = result[p * width : (p + 1) * width, s * rows : (s + 1) * rows]


def gate_kernel(scaling, y_ref, go_ref, value_ref, key_ref, *refs):
    gp_ref, first_ref, rest_ref, taps_ref, flat = refs[-5:]
    count, _, width, _ = y_ref.shape
    channels = count * width
    for s in range(3):
        for owner in range(count):
            flat[s, owner * width : (owner + 1) * width] = y_ref[owner, s]
    for index, factor_ref in enumerate((go_ref, value_ref, key_ref)):
        rounded = (factor_ref[...] * flat[min(index, 1)]).T.astype(jnp.bfloat16)
        gp_ref[:, index * channels : (index + 1) * channels] = rounded
        if index == 0:
            first_ref[...] = rounded.astype(jnp.float32)
        else:
            span = slice((index - 1) * channels, index * channels)
            rest_ref[:, span] = rounded.astype(jnp.float32)
    taps_ref[...] = flat[2].T * scaling


def turn_blocks(sources, out_ref):
    for which, (x_ref, slot) in enumerate(sources):
        _, far, rows, part = x_ref.shape
        for f in range(far):
            out_ref[f * part : (f + 1) * part, which * rows : (which + 1) * rows] = x_ref[
                slot, f
            ].T.astype(jnp.bfloat16)


def turn_kernel(own_ref, y_ref, z_ref, out_own_ref, out_other_ref):
    turn_blocks(((own_ref, 0), (y_ref, 0), (z_ref, 2)), out_own_ref)
    turn_blocks(((own_ref, 1), (y_ref, 2), (z_ref, 0)), out_other_ref)


def corner_kernel(corner_own_ref, corner_other_ref, out_own_ref, out_other_ref):
    turn_blocks(((corner_own_ref, 0),), out_own_ref)
    turn_blocks(((corner_other_ref, 0),), out_other_ref)


def joined_columns(x_ref, corner_ref, span):
    return jnp.concatenate([x_ref[span], corner_ref[span]], axis=1)


def joined(gp_refs):
    return jnp.concatenate([gp_ref[...].astype(jnp.bfloat16) for gp_ref in gp_refs], axis=0)


def other_kernel(x_ref, corner_ref, *refs):
    gp_refs, out_ref = refs[:SIDE], refs[-1]
    columns = joined_columns(x_ref, corner_ref, slice(None))
    out_ref[...] = jnp.dot(columns, joined(gp_refs), preferred_element_type=jnp.float32)


def own_kernel(x_ref, corner_ref, *refs):
    gp_refs, add_ref, out_refs = refs[:SIDE], refs[SIDE], refs[SIDE + 1 :]
    gp = joined(gp_refs)
    part = out_refs[0].shape[0]
    for which, out_ref in enumerate(out_refs):
        span = slice(which * part, (which + 1) * part)
        columns = joined_columns(x_ref, corner_ref, span)
        product = jnp.dot(columns, gp, preferred_element_type=jnp.float32)
        out_ref[...] = product + add_ref[span]


def sum_kernel(scaling, groups, *refs):
    *in_refs, out_ref = refs
    terms = len(in_refs) // groups
    first = 0
    for group in range(groups):
        total = in_refs[group * terms][...]
        for in_ref in in_refs[group * terms + 1 : (group + 1) * terms]:
            total = total + in_ref[...]
        out_ref[:, first : first + total.shape[1]] = total * scaling
        first += total.shape[1]


def per_device(inputs, in_weight, filter_taps, grad_out):
    rows, depth = inputs.shape
    channels = filter_taps.shape[1]
    columns = in_weight.shape[1]
    blocks = lax.axis_size("seq")
    width = channels // blocks
    part = depth // blocks
    far = blocks // (2 * SIDE)
    chunk = min(1024, depth)
    steps = depth // chunk
    scaling = 1.0 / math.sqrt(rows * blocks)
    f32, bf16 = jnp.float32, jnp.bfloat16
    params = pltpu.CompilerParams(vmem_limit_bytes=VMEM_LIMIT)
    wide = pltpu.CompilerParams(vmem_limit_bytes=VMEM_WIDE)

    def shaped(*shape, dtype=f32):
        return jax.ShapeDtypeStruct(shape, dtype)

    def exchange(value, flip):
        return lax.ppermute(value, "seq", [(i, i ^ flip) for i in range(blocks)])

    anywhere = pl.BlockSpec(memory_space=pl.ANY)
    inside = pl.BlockSpec(memory_space=pltpu.VMEM)
    own, to_y, to_z = pl.pallas_call(
        layout_kernel,
        out_shape=[shaped(2, far, rows, part)] + [shaped(3, far, rows, part)] * 2,
        compiler_params=wide,
    )(inputs)
    from_y, from_z = exchange(to_y, 2), exchange(to_z, 4)
    corners = exchange(from_y[1:2], 4), exchange(from_z[1:2], 2)
    turned = pl.pallas_call(
        turn_kernel,
        out_shape=[shaped(far * part, (SIDE - 1) * rows, dtype=bf16)] * 2,
        compiler_params=params,
        cost_estimate=pl.CostEstimate(
            flops=0, bytes_accessed=200 * SIDE * far * rows * part, transcendentals=0
        ),
    )(own, from_y, from_z)
    signals, gate_out, key, value = pl.pallas_call(
        functools.partial(project_kernel, scaling),
        grid=(steps,),
        in_specs=[
            pl.BlockSpec((rows, chunk), lambda i: (0, i)),
            pl.BlockSpec((chunk, columns), lambda i: (i, 0)),
            pl.BlockSpec((rows, channels), lambda i: (0, 0)),
            pl.BlockSpec((rows, channels), lambda i: (0, 0)),
        ],
        out_specs=[
            pl.BlockSpec((blocks, 3, width, rows), lambda i: (0, 0, 0, 0)),
            ]
        + [pl.BlockSpec((channels, rows), lambda i: (0, 0))] * 3,
        out_shape=[shaped(blocks, 3, width, rows)] + [shaped(channels, rows)] * 3,
        scratch_shapes=[pltpu.VMEM((rows, columns), f32)],
        compiler_params=wide,
        cost_estimate=pl.CostEstimate(
            flops=2 * rows * depth * columns,
            bytes_accessed=2 * depth * (rows + columns),
            transcendentals=0,
        ),
    )(inputs, in_weight, filter_taps, grad_out)

    signals = lax.all_to_all(signals, "seq", split_axis=0, concat_axis=0, tiled=True)
    pairs, turn = transform_tables(blocks, width, rows)
    table, places = packed(pairs)
    results = pl.pallas_call(
        functools.partial(conv_kernel, places),
        in_specs=[inside] * 3 + [anywhere] * 2,
        out_shape=shaped(blocks, 3, width, rows),
        scratch_shapes=[pltpu.VMEM((blocks * width, 3 * rows), f32)],
        compiler_params=params,
    )(signals, jnp.asarray(table), jnp.asarray(turn), *turned)
    results = lax.all_to_all(results, "seq", split_axis=0, concat_axis=0, tiled=True)
    grad_proj, sent_first, sent_rest, grad_taps = pl.pallas_call(
        functools.partial(gate_kernel, scaling),
        in_specs=[inside] * 4 + [anywhere] * 2,
        out_shape=[
            shaped(rows, columns, dtype=bf16),
            shaped(rows, channels),
            shaped(rows, 2 * channels),
            shaped(rows, channels),
        ],
        scratch_shapes=[pltpu.VMEM((3, channels, rows), f32)],
        compiler_params=params,
    )(results, gate_out, value, key, *corners)
    turned_corners = pl.pallas_call(
        corner_kernel,
        out_shape=[shaped(far * part, rows, dtype=bf16)] * 2,
        compiler_params=params,
    )(*corners)
    grad_inputs = lax.dot_general(
        grad_proj, in_weight, (((1,), (1,)), ((), ())), preferred_element_type=f32
    ).astype(bf16)
    terms = []
    for block in (sent_first, sent_rest):
        cols = block.shape[1]
        gathered = [block] + [exchange(block, 2 * k) for k in range(1, SIDE)]
        cost = pl.CostEstimate(
            flops=2 * far * part * SIDE * rows * cols,
            bytes_accessed=4 * far * part * cols,
            transcendentals=0,
        )
        other = pl.pallas_call(
            other_kernel,
            in_specs=[inside] * (2 + SIDE) + [anywhere] * len(terms[1:]),
            out_shape=shaped(far * part, cols),
            compiler_params=params,
            cost_estimate=cost,
        )(turned[1], turned_corners[1], *gathered, *terms[1:])
        kept, *leaving = pl.pallas_call(
            own_kernel,
            out_shape=[shaped(part, cols)] * far,
            compiler_params=params,
            cost_estimate=cost,
        )(turned[0], turned_corners[0], *gathered, exchange(other, 1))
        terms += [kept] + [exchange(v, 2 * SIDE * (k + 1)) for k, v in enumerate(leaving)]
    grad_weight = pl.pallas_call(
        functools.partial(sum_kernel, scaling, 2),
        out_shape=shaped(part, columns),
        compiler_params=params,
    )(*terms)
    return grad_inputs, grad_weight, grad_taps


def solution(mesh):
    in_specs = (P(("grp", "seq"), None), P(), P("seq", None), P(("grp", "seq"), None))
    out_specs = (P(("grp", "seq"), None), P(("grp", "seq"), None), P(("grp", "seq"), None))
    return jax.shard_map(
        per_device, mesh=mesh, in_specs=in_specs, out_specs=out_specs, check_vma=False
    )
```

```python
import functools
import math

import jax
import jax.numpy as jnp
import numpy as np
from jax import lax
from jax.experimental import pallas as pl
from jax.experimental.pallas import tpu as pltpu
from jax.sharding import PartitionSpec as P

VMEM_LIMIT = 48 * 1024 * 1024
VMEM_WIDE = 60 * 1024 * 1024
SIDE = 4


def split_pair(table):
    high = table.astype(np.float32).astype(jnp.bfloat16)
    low = (table - high.astype(np.float64)).astype(np.float32).astype(jnp.bfloat16)
    return high, low


def transform_tables(blocks, width, rows):
    length = 2 * blocks * rows
    kept = blocks + 1
    padded = -(-kept * width // 16) * 16
    k1 = np.arange(kept)
    block = np.arange(blocks)
    angle = 2.0 * np.pi * ((k1[:, None] * block[None, :]) % (2 * blocks)) / (2 * blocks)
    eye = np.eye(width)

    def spread(matrix):
        wide = np.kron(matrix, eye)
        return np.pad(wide, ((0, padded - wide.shape[0]), (0, 0)))

    mix = np.concatenate([spread(np.cos(angle)), spread(-np.sin(angle))], axis=0)
    weight = np.where((k1 == 0) | (k1 == blocks), 1.0, 2.0)[:, None] / length
    unmix = np.concatenate(
        [spread(weight * np.cos(angle)), spread(-weight * np.sin(angle))], axis=0
    ).T
    row = np.arange(rows)
    turn = 2.0 * np.pi * ((k1[:, None] * row[None, :]) % length) / length
    turn = np.pad(np.repeat(turn, width, axis=0), ((0, padded - kept * width), (0, 0)))
    inner = 2.0 * np.pi * ((row[:, None] * row[None, :]) % rows) / rows
    cos, sin = np.cos(inner), np.sin(inner)
    forward = np.block([[cos, -sin], [sin, cos]])
    inverse = np.block([[cos, sin], [-sin, cos]])
    turn = np.concatenate([np.cos(turn), np.sin(turn)], axis=1).astype(np.float32)
    return [split_pair(matrix) for matrix in (mix, forward, inverse, unmix)], turn


def packed(tables):
    width = max(min(high.shape) for high, _ in tables)
    slabs, places, first = [], [], 0
    for pair in tables:
        for table in pair:
            pieces = []
            for start in range(0, table.shape[1], width):
                slab = table[:, start : start + width]
                pieces.append((first, slab.shape))
                first += slab.shape[0]
                slabs.append(np.pad(slab, ((0, 0), (0, width - slab.shape[1]))))
            places.append(pieces)
    return np.concatenate(slabs, axis=0), places


def halves(value):
    high = value.astype(jnp.bfloat16)
    return high, (value - high.astype(jnp.float32)).astype(jnp.bfloat16)


def dot32(left, right):
    (lh, ll), (rh, rl) = left, right
    dot = functools.partial(jnp.dot, preferred_element_type=jnp.float32)
    return dot(lh, rh) + (dot(lh, rl) + dot(ll, rh))


def layout_kernel(x_ref, own_ref, y_ref, z_ref):
    _, far, _, part = own_ref.shape
    device = lax.axis_index("seq")
    places = {
        (0, 0): (own_ref, 0),
        (0, 1): (own_ref, 1),
        (1, 0): (y_ref, 0),
        (3, 0): (y_ref, 1),
        (1, 1): (y_ref, 2),
        (2, 1): (z_ref, 0),
        (3, 1): (z_ref, 1),
        (2, 0): (z_ref, 2),
    }
    for chip in range(far * SIDE):
        distance = (chip // SIDE) ^ (device // (2 * SIDE))
        near = (chip % SIDE) ^ ((device // 2) % SIDE)
        for core in range(2):
            first = (2 * chip + core) * part
            flip = (device % 2) ^ core
            for (side, cross), (out_ref, slot) in places.items():

                @pl.when((near == side) & (flip == cross))
                def _():
                    out_ref[slot, distance] = x_ref[:, first : first + part].astype(jnp.float32)


def project_kernel(scaling, x_ref, w_ref, taps_ref, go_ref, *refs):
    sig_ref, gates_ref, acc = refs[-3:]
    step = pl.program_id(0)
    product = jnp.dot(x_ref[...], w_ref[...], preferred_element_type=jnp.float32)

    @pl.when(step == 0)
    def _():
        acc[...] = product

    @pl.when(step > 0)
    def _():
        acc[...] += product

    @pl.when(step == pl.num_programs(0) - 1)
    def _():
        count, _, width, _ = sig_ref.shape
        channels = count * width
        projected = acc[...].astype(jnp.bfloat16).astype(jnp.float32).T
        query = projected[:channels]
        key = projected[channels : 2 * channels]
        value = projected[2 * channels :]
        go = go_ref[...].astype(jnp.float32).T
        signals = ((taps_ref[...] * scaling).T, key * value, go * query)
        for which, signal in enumerate(signals):
            for owner in range(count):
                sig_ref[owner, which] = signal[owner * width : (owner + 1) * width]
        for index, gate in enumerate((go, value, key)):
            gates_ref[index] = gate.astype(jnp.bfloat16)


def conv_kernel(places, x_ref, table_ref, turn_ref, *refs):
    y_ref, flat = refs[-2:]
    blocks, _, width, rows = x_ref.shape

    def table(which):
        slabs = [table_ref[at : at + shape[0], : shape[1]] for at, shape in places[which]]
        return slabs[0] if len(slabs) == 1 else jnp.concatenate(slabs, axis=1)

    m_h, m_l, f_h, f_l, i_h, i_l, u_h, u_l = [functools.partial(table, w) for w in range(8)]
    for p in range(blocks):
        for s in range(3):
            flat[p * width : (p + 1) * width, s * rows : (s + 1) * rows] = x_ref[p, s]
    turn_re, turn_im = turn_ref[:, :rows], turn_ref[:, rows:]
    count = turn_re.shape[0]
    mixed = dot32((m_h(), m_l()), halves(flat[...]))
    turned = []
    for s in range(3):
        re = mixed[:count, s * rows : (s + 1) * rows]
        im = mixed[count:, s * rows : (s + 1) * rows]
        turned.append(
            jnp.concatenate([re * turn_re + im * turn_im, im * turn_re - re * turn_im], axis=1)
        )
    spectrum = dot32(halves(jnp.concatenate(turned, axis=0)), (f_h(), f_l()))
    (k_re, k_im), (g_re, g_im), (b_re, b_im) = [
        (spectrum[s * count : (s + 1) * count, :rows], spectrum[s * count : (s + 1) * count, rows:])
        for s in range(3)
    ]
    products = jnp.concatenate(
        [
            jnp.concatenate([k_re * g_re - k_im * g_im, k_re * g_im + k_im * g_re], axis=1),
            jnp.concatenate([k_re * b_re + k_im * b_im, k_re * b_im - k_im * b_re], axis=1),
            jnp.concatenate([b_re * g_re + b_im * g_im, b_im * g_re - b_re * g_im], axis=1),
        ],
        axis=0,
    )
    back = dot32(halves(products), (i_h(), i_l()))
    parts_re, parts_im = [], []
    for s in range(3):
        re = back[s * count : (s + 1) * count, :rows]
        im = back[s * count : (s + 1) * count, rows:]
        parts_re.append(re * turn_re - im * turn_im)
        parts_im.append(im * turn_re + re * turn_im)
    stacked = jnp.concatenate(
        [jnp.concatenate(parts_re, axis=1), jnp.concatenate(parts_im, axis=1)], axis=0
    )
    result = dot32((u_h(), u_l()), halves(stacked))
    for p in range(blocks):
        for s in range(3):
            y_ref[p, s] = result[p * width : (p + 1) * width, s * rows : (s + 1) * rows]


def gate_kernel(scaling, y_ref, gates_ref, *refs):
    gp_ref, first_ref, rest_ref, taps_ref, flat = refs[-5:]
    count, _, width, _ = y_ref.shape
    channels = count * width
    for s in range(3):
        for owner in range(count):
            flat[s, owner * width : (owner + 1) * width] = y_ref[owner, s]
    for index in range(3):
        gate = gates_ref[index].astype(jnp.float32)
        rounded = (gate * flat[min(index, 1)]).T.astype(jnp.bfloat16)
        gp_ref[:, index * channels : (index + 1) * channels] = rounded
        if index == 0:
            first_ref[...] = rounded.astype(jnp.float32)
        else:
            span = slice((index - 1) * channels, index * channels)
            rest_ref[:, span] = rounded.astype(jnp.float32)
    taps_ref[...] = flat[2].T * scaling


def turn_blocks(sources, out_ref):
    for which, (x_ref, slot) in enumerate(sources):
        _, far, rows, part = x_ref.shape
        for f in range(far):
            out_ref[f * part : (f + 1) * part, which * rows : (which + 1) * rows] = x_ref[
                slot, f
            ].T.astype(jnp.bfloat16)


def turn_kernel(own_ref, y_ref, z_ref, out_own_ref, out_other_ref, relay_z_ref, relay_y_ref):
    relay_z_ref[0] = y_ref[1]
    relay_y_ref[0] = z_ref[1]
    turn_blocks(((own_ref, 0), (y_ref, 0), (z_ref, 2)), out_own_ref)
    turn_blocks(((own_ref, 1), (y_ref, 2), (z_ref, 0)), out_other_ref)


def corner_kernel(corner_own_ref, corner_other_ref, out_own_ref, out_other_ref):
    turn_blocks(((corner_own_ref, 0),), out_own_ref)
    turn_blocks(((corner_other_ref, 0),), out_other_ref)


def joined_columns(x_ref, corner_ref, span):
    return jnp.concatenate([x_ref[span], corner_ref[span]], axis=1)


def joined(gp_ref):
    here = (lax.axis_index("seq") // 2) % SIDE
    return jnp.concatenate([gp_ref[here ^ k].astype(jnp.bfloat16) for k in range(SIDE)], axis=0)


def other_kernel(x_ref, corner_ref, gp_ref, *refs):
    out_ref = refs[-1]
    columns = joined_columns(x_ref, corner_ref, slice(None))
    out_ref[...] = jnp.dot(columns, joined(gp_ref), preferred_element_type=jnp.float32)


def own_kernel(x_ref, corner_ref, gp_ref, add_ref, *out_refs):
    gp = joined(gp_ref)
    part = out_refs[0].shape[0]
    for which, out_ref in enumerate(out_refs):
        span = slice(which * part, (which + 1) * part)
        columns = joined_columns(x_ref, corner_ref, span)
        product = jnp.dot(columns, gp, preferred_element_type=jnp.float32)
        out_ref[...] = product + add_ref[span]


def sum_kernel(scaling, groups, *refs):
    *in_refs, out_ref = refs
    terms = len(in_refs) // groups
    first = 0
    for group in range(groups):
        total = in_refs[group * terms][...]
        for in_ref in in_refs[group * terms + 1 : (group + 1) * terms]:
            total = total + in_ref[...]
        out_ref[:, first : first + total.shape[1]] = total * scaling
        first += total.shape[1]


def per_device(inputs, in_weight, filter_taps, grad_out):
    rows, depth = inputs.shape
    channels = filter_taps.shape[1]
    columns = in_weight.shape[1]
    blocks = lax.axis_size("seq")
    width = channels // blocks
    part = depth // blocks
    far = blocks // (2 * SIDE)
    chunk = min(1024, depth)
    steps = depth // chunk
    scaling = 1.0 / math.sqrt(rows * blocks)
    f32, bf16 = jnp.float32, jnp.bfloat16
    params = pltpu.CompilerParams(vmem_limit_bytes=VMEM_LIMIT)
    wide = pltpu.CompilerParams(vmem_limit_bytes=VMEM_WIDE)

    def shaped(*shape, dtype=f32):
        return jax.ShapeDtypeStruct(shape, dtype)

    def exchange(value, flip):
        return lax.ppermute(value, "seq", [(i, i ^ flip) for i in range(blocks)])

    anywhere = pl.BlockSpec(memory_space=pl.ANY)
    inside = pl.BlockSpec(memory_space=pltpu.VMEM)
    own, to_y, to_z = pl.pallas_call(
        layout_kernel,
        out_shape=[shaped(2, far, rows, part)] + [shaped(3, far, rows, part)] * 2,
        compiler_params=wide,
    )(inputs)
    from_y, from_z = exchange(to_y, 2), exchange(to_z, 4)
    *turned, relay_z, relay_y = pl.pallas_call(
        turn_kernel,
        out_shape=[shaped(far * part, (SIDE - 1) * rows, dtype=bf16)] * 2
        + [shaped(1, far, rows, part)] * 2,
        compiler_params=wide,
        cost_estimate=pl.CostEstimate(
            flops=0, bytes_accessed=200 * SIDE * far * rows * part, transcendentals=0
        ),
    )(own, from_y, from_z)
    corners = exchange(relay_z, 4), exchange(relay_y, 2)
    signals, gates = pl.pallas_call(
        functools.partial(project_kernel, scaling),
        grid=(steps,),
        in_specs=[
            pl.BlockSpec((rows, chunk), lambda i: (0, i)),
            pl.BlockSpec((chunk, columns), lambda i: (i, 0)),
            pl.BlockSpec((rows, channels), lambda i: (0, 0)),
            pl.BlockSpec((rows, channels), lambda i: (0, 0)),
        ],
        out_specs=[
            pl.BlockSpec((blocks, 3, width, rows), lambda i: (0, 0, 0, 0)),
            ]
        + [pl.BlockSpec((3, channels, rows), lambda i: (0, 0, 0))],
        out_shape=[shaped(blocks, 3, width, rows), shaped(3, channels, rows, dtype=bf16)],
        scratch_shapes=[pltpu.VMEM((rows, columns), f32)],
        compiler_params=wide,
        cost_estimate=pl.CostEstimate(
            flops=2 * rows * depth * columns,
            bytes_accessed=2 * depth * (rows + columns),
            transcendentals=0,
        ),
    )(inputs, in_weight, filter_taps, grad_out)

    signals = lax.all_to_all(signals, "seq", split_axis=0, concat_axis=0, tiled=True)
    pairs, turn = transform_tables(blocks, width, rows)
    table, places = packed(pairs)
    results = pl.pallas_call(
        functools.partial(conv_kernel, places),
        in_specs=[inside] * 3 + [anywhere] * 2,
        out_shape=shaped(blocks, 3, width, rows),
        scratch_shapes=[pltpu.VMEM((blocks * width, 3 * rows), f32)],
        compiler_params=params,
    )(signals, jnp.asarray(table), jnp.asarray(turn), *turned)
    results = lax.all_to_all(results, "seq", split_axis=0, concat_axis=0, tiled=True)
    grad_proj, sent_first, sent_rest, grad_taps = pl.pallas_call(
        functools.partial(gate_kernel, scaling),
        in_specs=[inside] * 2 + [anywhere] * 2,
        out_shape=[
            shaped(rows, columns, dtype=bf16),
            shaped(rows, channels),
            shaped(rows, 2 * channels),
            shaped(rows, channels),
        ],
        scratch_shapes=[pltpu.VMEM((3, channels, rows), f32)],
        compiler_params=params,
    )(results, gates, *corners)
    turned_corners = pl.pallas_call(
        corner_kernel,
        out_shape=[shaped(far * part, rows, dtype=bf16)] * 2,
        compiler_params=params,
    )(*corners)
    grad_inputs = lax.dot_general(
        grad_proj, in_weight, (((1,), (1,)), ((), ())), preferred_element_type=f32
    ).astype(bf16)
    squares = [
        [base + core + 2 * k for k in range(SIDE)]
        for base in range(0, blocks, 2 * SIDE)
        for core in range(2)
    ]
    terms = []
    for block in (sent_first, sent_rest):
        cols = block.shape[1]
        gathered = lax.all_gather(block, "seq", axis_index_groups=squares)
        cost = pl.CostEstimate(
            flops=2 * far * part * SIDE * rows * cols,
            bytes_accessed=4 * far * part * cols,
            transcendentals=0,
        )
        other = pl.pallas_call(
            other_kernel,
            in_specs=[inside] * 3 + [anywhere] * len(terms[1:]),
            out_shape=shaped(far * part, cols),
            compiler_params=params,
            cost_estimate=cost,
        )(turned[1], turned_corners[1], gathered, *terms[1:])
        kept, *leaving = pl.pallas_call(
            own_kernel,
            out_shape=[shaped(part, cols)] * far,
            compiler_params=params,
            cost_estimate=cost,
        )(turned[0], turned_corners[0], gathered, exchange(other, 1))
        terms += [kept] + [exchange(v, 2 * SIDE * (k + 1)) for k, v in enumerate(leaving)]
    grad_weight = pl.pallas_call(
        functools.partial(sum_kernel, scaling, 2),
        out_shape=shaped(part, columns),
        compiler_params=params,
    )(*terms)
    return grad_inputs, grad_weight, grad_taps


def solution(mesh):
    in_specs = (P(("grp", "seq"), None), P(), P("seq", None), P(("grp", "seq"), None))
    out_specs = (P(("grp", "seq"), None), P(("grp", "seq"), None), P(("grp", "seq"), None))
    return jax.shard_map(
        per_device, mesh=mesh, in_specs=in_specs, out_specs=out_specs, check_vma=False
    )
```

```python
import functools
import math

import jax
import jax.numpy as jnp
import numpy as np
from jax import lax
from jax.experimental import pallas as pl
from jax.experimental.pallas import tpu as pltpu
from jax.sharding import PartitionSpec as P

VMEM_LIMIT = 48 * 1024 * 1024
VMEM_WIDE = 60 * 1024 * 1024
SIDE = 4


def split_pair(table):
    high = table.astype(np.float32).astype(jnp.bfloat16)
    low = (table - high.astype(np.float64)).astype(np.float32).astype(jnp.bfloat16)
    return high, low


def transform_tables(blocks, width, rows):
    length = 2 * blocks * rows
    kept = blocks + 1
    padded = -(-kept * width // 16) * 16
    k1 = np.arange(kept)
    block = np.arange(blocks)
    angle = 2.0 * np.pi * ((k1[:, None] * block[None, :]) % (2 * blocks)) / (2 * blocks)
    eye = np.eye(width)

    def spread(matrix):
        wide = np.kron(matrix, eye)
        return np.pad(wide, ((0, padded - wide.shape[0]), (0, 0)))

    mix = np.concatenate([spread(np.cos(angle)), spread(-np.sin(angle))], axis=0)
    weight = np.where((k1 == 0) | (k1 == blocks), 1.0, 2.0)[:, None] / length
    unmix = np.concatenate(
        [spread(weight * np.cos(angle)), spread(-weight * np.sin(angle))], axis=0
    ).T
    row = np.arange(rows)
    turn = 2.0 * np.pi * ((k1[:, None] * row[None, :]) % length) / length
    turn = np.pad(np.repeat(turn, width, axis=0), ((0, padded - kept * width), (0, 0)))
    inner = 2.0 * np.pi * ((row[:, None] * row[None, :]) % rows) / rows
    cos, sin = np.cos(inner), np.sin(inner)
    forward = np.block([[cos, -sin], [sin, cos]])
    inverse = np.block([[cos, sin], [-sin, cos]])
    turn = np.concatenate([np.cos(turn), np.sin(turn)], axis=1).astype(np.float32)
    return [split_pair(matrix) for matrix in (mix, forward, inverse, unmix)], turn


def packed(tables):
    width = max(min(high.shape) for high, _ in tables)
    slabs, places, first = [], [], 0
    for pair in tables:
        for table in pair:
            pieces = []
            for start in range(0, table.shape[1], width):
                slab = table[:, start : start + width]
                pieces.append((first, slab.shape))
                first += slab.shape[0]
                slabs.append(np.pad(slab, ((0, 0), (0, width - slab.shape[1]))))
            places.append(pieces)
    return np.concatenate(slabs, axis=0), places


def halves(value):
    high = value.astype(jnp.bfloat16)
    return high, (value - high.astype(jnp.float32)).astype(jnp.bfloat16)


def dot32(left, right):
    (lh, ll), (rh, rl) = left, right
    dot = functools.partial(jnp.dot, preferred_element_type=jnp.float32)
    return dot(lh, rh) + (dot(lh, rl) + dot(ll, rh))


def layout_kernel(x_ref, own_ref, y_ref, z_ref):
    _, far, _, part = own_ref.shape
    device = lax.axis_index("seq")
    places = {
        (0, 0): (own_ref, 0),
        (0, 1): (own_ref, 1),
        (1, 0): (y_ref, 0),
        (3, 0): (y_ref, 1),
        (1, 1): (y_ref, 2),
        (2, 1): (z_ref, 0),
        (3, 1): (z_ref, 1),
        (2, 0): (z_ref, 2),
    }
    for chip in range(far * SIDE):
        distance = (chip // SIDE) ^ (device // (2 * SIDE))
        near = (chip % SIDE) ^ ((device // 2) % SIDE)
        for core in range(2):
            first = (2 * chip + core) * part
            flip = (device % 2) ^ core
            for (side, cross), (out_ref, slot) in places.items():

                @pl.when((near == side) & (flip == cross))
                def _():
                    out_ref[slot, distance] = x_ref[:, first : first + part].astype(jnp.float32)


def project_kernel(scaling, x_ref, w_ref, taps_ref, go_ref, *refs):
    sig_ref, gates_ref, acc = refs[-3:]
    step = pl.program_id(0)
    product = jnp.dot(x_ref[...], w_ref[...], preferred_element_type=jnp.float32)

    @pl.when(step == 0)
    def _():
        acc[...] = product

    @pl.when(step > 0)
    def _():
        acc[...] += product

    @pl.when(step == pl.num_programs(0) - 1)
    def _():
        count, _, width, _ = sig_ref.shape
        channels = count * width
        projected = acc[...].astype(jnp.bfloat16).astype(jnp.float32).T
        query = projected[:channels]
        key = projected[channels : 2 * channels]
        value = projected[2 * channels :]
        go = go_ref[...].astype(jnp.float32).T
        signals = ((taps_ref[...] * scaling).T, key * value, go * query)
        for which, signal in enumerate(signals):
            for owner in range(count):
                sig_ref[owner, which] = signal[owner * width : (owner + 1) * width]
        for index, gate in enumerate((go, value, key)):
            gates_ref[index] = gate.astype(jnp.bfloat16)


def conv_kernel(places, x_ref, table_ref, turn_ref, *refs):
    y_ref, flat = refs[-2:]
    blocks, _, width, rows = x_ref.shape

    def table(which):
        slabs = [table_ref[at : at + shape[0], : shape[1]] for at, shape in places[which]]
        return slabs[0] if len(slabs) == 1 else jnp.concatenate(slabs, axis=1)

    m_h, m_l, f_h, f_l, i_h, i_l, u_h, u_l = [functools.partial(table, w) for w in range(8)]
    for p in range(blocks):
        for s in range(3):
            flat[p * width : (p + 1) * width, s * rows : (s + 1) * rows] = x_ref[p, s]
    turn_re, turn_im = turn_ref[:, :rows], turn_ref[:, rows:]
    count = turn_re.shape[0]
    mixed = dot32((m_h(), m_l()), halves(flat[...]))
    turned = []
    for s in range(3):
        re = mixed[:count, s * rows : (s + 1) * rows]
        im = mixed[count:, s * rows : (s + 1) * rows]
        turned.append(
            jnp.concatenate([re * turn_re + im * turn_im, im * turn_re - re * turn_im], axis=1)
        )
    spectrum = dot32(halves(jnp.concatenate(turned, axis=0)), (f_h(), f_l()))
    (k_re, k_im), (g_re, g_im), (b_re, b_im) = [
        (spectrum[s * count : (s + 1) * count, :rows], spectrum[s * count : (s + 1) * count, rows:])
        for s in range(3)
    ]
    products = jnp.concatenate(
        [
            jnp.concatenate([k_re * g_re - k_im * g_im, k_re * g_im + k_im * g_re], axis=1),
            jnp.concatenate([k_re * b_re + k_im * b_im, k_re * b_im - k_im * b_re], axis=1),
            jnp.concatenate([b_re * g_re + b_im * g_im, b_im * g_re - b_re * g_im], axis=1),
        ],
        axis=0,
    )
    back = dot32(halves(products), (i_h(), i_l()))
    parts_re, parts_im = [], []
    for s in range(3):
        re = back[s * count : (s + 1) * count, :rows]
        im = back[s * count : (s + 1) * count, rows:]
        parts_re.append(re * turn_re - im * turn_im)
        parts_im.append(im * turn_re + re * turn_im)
    stacked = jnp.concatenate(
        [jnp.concatenate(parts_re, axis=1), jnp.concatenate(parts_im, axis=1)], axis=0
    )
    result = dot32((u_h(), u_l()), halves(stacked))
    for p in range(blocks):
        for s in range(3):
            y_ref[p, s] = result[p * width : (p + 1) * width, s * rows : (s + 1) * rows]


def gate_kernel(scaling, y_ref, gates_ref, *refs):
    gp_ref, first_ref, rest_ref, taps_ref, flat = refs[-5:]
    count, _, width, _ = y_ref.shape
    channels = count * width
    for s in range(3):
        for owner in range(count):
            flat[s, owner * width : (owner + 1) * width] = y_ref[owner, s]
    for index in range(3):
        gate = gates_ref[index].astype(jnp.float32)
        rounded = (gate * flat[min(index, 1)]).T.astype(jnp.bfloat16)
        gp_ref[:, index * channels : (index + 1) * channels] = rounded
        if index == 0:
            first_ref[...] = rounded.astype(jnp.float32)
        else:
            span = slice((index - 1) * channels, index * channels)
            rest_ref[:, span] = rounded.astype(jnp.float32)
    taps_ref[...] = flat[2].T * scaling


def turn_blocks(sources, out_ref):
    for which, (x_ref, slot) in enumerate(sources):
        _, far, rows, part = x_ref.shape
        for f in range(far):
            out_ref[f * part : (f + 1) * part, which * rows : (which + 1) * rows] = x_ref[
                slot, f
            ].T.astype(jnp.bfloat16)


def turn_kernel(own_ref, y_ref, z_ref, out_own_ref, out_other_ref, relay_z_ref, relay_y_ref):
    relay_z_ref[0] = y_ref[1]
    relay_y_ref[0] = z_ref[1]
    turn_blocks(((own_ref, 0), (y_ref, 0), (z_ref, 2)), out_own_ref)
    turn_blocks(((own_ref, 1), (y_ref, 2), (z_ref, 0)), out_other_ref)


def corner_kernel(corner_own_ref, corner_other_ref, out_own_ref, out_other_ref):
    turn_blocks(((corner_own_ref, 0),), out_own_ref)
    turn_blocks(((corner_other_ref, 0),), out_other_ref)


def joined_columns(x_ref, corner_ref, span):
    return jnp.concatenate([x_ref[span], corner_ref[span]], axis=1)


def joined(gp_refs):
    return jnp.concatenate([gp_ref[...].astype(jnp.bfloat16) for gp_ref in gp_refs], axis=0)


def other_kernel(x_ref, corner_ref, *refs):
    gp_refs, out_ref = refs[:SIDE], refs[-1]
    columns = joined_columns(x_ref, corner_ref, slice(None))
    out_ref[...] = jnp.dot(columns, joined(gp_refs), preferred_element_type=jnp.float32)


def own_kernel(x_ref, corner_ref, *refs):
    gp_refs, add_ref, out_refs = refs[:SIDE], refs[SIDE], refs[SIDE + 1 :]
    gp = joined(gp_refs)
    part = out_refs[0].shape[0]
    for which, out_ref in enumerate(out_refs):
        span = slice(which * part, (which + 1) * part)
        columns = joined_columns(x_ref, corner_ref, span)
        product = jnp.dot(columns, gp, preferred_element_type=jnp.float32)
        out_ref[...] = product + add_ref[span]


def sum_kernel(scaling, groups, *refs):
    *in_refs, out_ref = refs
    terms = len(in_refs) // groups
    first = 0
    for group in range(groups):
        total = in_refs[group * terms][...]
        for in_ref in in_refs[group * terms + 1 : (group + 1) * terms]:
            total = total + in_ref[...]
        out_ref[:, first : first + total.shape[1]] = total * scaling
        first += total.shape[1]


def per_device(inputs, in_weight, filter_taps, grad_out):
    rows, depth = inputs.shape
    channels = filter_taps.shape[1]
    columns = in_weight.shape[1]
    blocks = lax.axis_size("seq")
    width = channels // blocks
    part = depth // blocks
    far = blocks // (2 * SIDE)
    chunk = min(1024, depth)
    steps = depth // chunk
    scaling = 1.0 / math.sqrt(rows * blocks)
    f32, bf16 = jnp.float32, jnp.bfloat16
    params = pltpu.CompilerParams(vmem_limit_bytes=VMEM_LIMIT)
    wide = pltpu.CompilerParams(vmem_limit_bytes=VMEM_WIDE)

    def shaped(*shape, dtype=f32):
        return jax.ShapeDtypeStruct(shape, dtype)

    def exchange(value, flip):
        return lax.ppermute(value, "seq", [(i, i ^ flip) for i in range(blocks)])

    anywhere = pl.BlockSpec(memory_space=pl.ANY)
    inside = pl.BlockSpec(memory_space=pltpu.VMEM)
    own, to_y, to_z = pl.pallas_call(
        layout_kernel,
        out_shape=[shaped(2, far, rows, part)] + [shaped(3, far, rows, part)] * 2,
        compiler_params=wide,
    )(inputs)
    from_y, from_z = exchange(to_y, 2), exchange(to_z, 4)
    *turned, relay_z, relay_y = pl.pallas_call(
        turn_kernel,
        out_shape=[shaped(far * part, (SIDE - 1) * rows, dtype=bf16)] * 2
        + [shaped(1, far, rows, part)] * 2,
        compiler_params=params,
        cost_estimate=pl.CostEstimate(
            flops=0, bytes_accessed=200 * SIDE * far * rows * part, transcendentals=0
        ),
    )(own, from_y, from_z)
    corners = exchange(relay_z, 4), exchange(relay_y, 2)
    signals, gates = pl.pallas_call(
        functools.partial(project_kernel, scaling),
        grid=(steps,),
        in_specs=[
            pl.BlockSpec((rows, chunk), lambda i: (0, i)),
            pl.BlockSpec((chunk, columns), lambda i: (i, 0)),
            pl.BlockSpec((rows, channels), lambda i: (0, 0)),
            pl.BlockSpec((rows, channels), lambda i: (0, 0)),
        ],
        out_specs=[
            pl.BlockSpec((blocks, 3, width, rows), lambda i: (0, 0, 0, 0)),
            ]
        + [pl.BlockSpec((3, channels, rows), lambda i: (0, 0, 0))],
        out_shape=[shaped(blocks, 3, width, rows), shaped(3, channels, rows, dtype=bf16)],
        scratch_shapes=[pltpu.VMEM((rows, columns), f32)],
        compiler_params=wide,
        cost_estimate=pl.CostEstimate(
            flops=2 * rows * depth * columns,
            bytes_accessed=2 * depth * (rows + columns),
            transcendentals=0,
        ),
    )(inputs, in_weight, filter_taps, grad_out)

    signals = lax.all_to_all(signals, "seq", split_axis=0, concat_axis=0, tiled=True)
    pairs, turn = transform_tables(blocks, width, rows)
    table, places = packed(pairs)
    results = pl.pallas_call(
        functools.partial(conv_kernel, places),
        in_specs=[inside] * 3 + [anywhere] * 2,
        out_shape=shaped(blocks, 3, width, rows),
        scratch_shapes=[pltpu.VMEM((blocks * width, 3 * rows), f32)],
        compiler_params=params,
    )(signals, jnp.asarray(table), jnp.asarray(turn), *turned)
    results = lax.all_to_all(results, "seq", split_axis=0, concat_axis=0, tiled=True)
    turned_corners = pl.pallas_call(
        corner_kernel,
        out_shape=[shaped(far * part, rows, dtype=bf16)] * 2,
        compiler_params=params,
        cost_estimate=pl.CostEstimate(
            flops=0, bytes_accessed=200 * SIDE * far * rows * part, transcendentals=0
        ),
    )(*corners)
    grad_proj, sent_first, sent_rest, grad_taps = pl.pallas_call(
        functools.partial(gate_kernel, scaling),
        in_specs=[inside] * 2 + [anywhere] * 2,
        out_shape=[
            shaped(rows, columns, dtype=bf16),
            shaped(rows, channels),
            shaped(rows, columns - channels),
            shaped(rows, channels),
        ],
        scratch_shapes=[pltpu.VMEM((3, channels, rows), f32)],
        compiler_params=params,
    )(results, gates, *turned_corners)
    grad_inputs = lax.dot_general(
        grad_proj, in_weight, (((1,), (1,)), ((), ())), preferred_element_type=f32
    ).astype(bf16)
    terms = []
    for block in (sent_first, sent_rest):
        cols = block.shape[1]
        gathered = [block] + [exchange(block, 2 * k) for k in range(1, SIDE)]
        cost = pl.CostEstimate(
            flops=2 * far * part * SIDE * rows * cols,
            bytes_accessed=4 * far * part * cols,
            transcendentals=0,
        )
        other = pl.pallas_call(
            other_kernel,
            in_specs=[inside] * (2 + SIDE) + [anywhere] * len(terms[1:]),
            out_shape=shaped(far * part, cols),
            compiler_params=params,
            cost_estimate=cost,
        )(turned[1], turned_corners[1], *gathered, *terms[1:])
        kept, *leaving = pl.pallas_call(
            own_kernel,
            out_shape=[shaped(part, cols)] * far,
            compiler_params=params,
            cost_estimate=cost,
        )(turned[0], turned_corners[0], *gathered, exchange(other, 1))
        terms += [kept] + [exchange(v, 2 * SIDE * (k + 1)) for k, v in enumerate(leaving)]
    grad_weight = pl.pallas_call(
        functools.partial(sum_kernel, scaling, 2),
        out_shape=shaped(part, columns),
        compiler_params=params,
    )(*terms)
    return grad_inputs, grad_weight, grad_taps


def solution(mesh):
    in_specs = (P(("grp", "seq"), None), P(), P("seq", None), P(("grp", "seq"), None))
    out_specs = (P(("grp", "seq"), None), P(("grp", "seq"), None), P(("grp", "seq"), None))
    return jax.shard_map(
        per_device, mesh=mesh, in_specs=in_specs, out_specs=out_specs, check_vma=False
    )
```

```python
import functools
import math

import jax
import jax.numpy as jnp
import numpy as np
from jax import lax
from jax.experimental import pallas as pl
from jax.experimental.pallas import tpu as pltpu
from jax.sharding import PartitionSpec as P

VMEM_LIMIT = 28 * 1024 * 1024
SIDE = 4


def split_pair(table):
    high = table.astype(np.float32).astype(jnp.bfloat16)
    low = (table - high.astype(np.float64)).astype(np.float32).astype(jnp.bfloat16)
    return high, low


def transform_tables(blocks, width, rows):
    length = 2 * blocks * rows
    kept = blocks + 1
    padded = -(-kept * width // 16) * 16
    k1 = np.arange(kept)
    block = np.arange(blocks)
    angle = 2.0 * np.pi * ((k1[:, None] * block[None, :]) % (2 * blocks)) / (2 * blocks)
    eye = np.eye(width)

    def spread(matrix):
        wide = np.kron(matrix, eye)
        return np.pad(wide, ((0, padded - wide.shape[0]), (0, 0)))

    mix = np.concatenate([spread(np.cos(angle)), spread(-np.sin(angle))], axis=0)
    weight = np.where((k1 == 0) | (k1 == blocks), 1.0, 2.0)[:, None] / length
    unmix = np.concatenate(
        [spread(weight * np.cos(angle)), spread(-weight * np.sin(angle))], axis=0
    ).T
    row = np.arange(rows)
    turn = 2.0 * np.pi * ((k1[:, None] * row[None, :]) % length) / length
    turn = np.pad(np.repeat(turn, width, axis=0), ((0, padded - kept * width), (0, 0)))
    inner = 2.0 * np.pi * ((row[:, None] * row[None, :]) % rows) / rows
    cos, sin = np.cos(inner), np.sin(inner)
    forward = np.block([[cos, -sin], [sin, cos]])
    inverse = np.block([[cos, sin], [-sin, cos]])
    turn = np.concatenate([np.cos(turn), np.sin(turn)], axis=1).astype(np.float32)
    return [split_pair(matrix) for matrix in (mix, forward, inverse, unmix)], turn


def packed(tables):
    width = max(min(high.shape) for high, _ in tables)
    slabs, places, first = [], [], 0
    for pair in tables:
        for table in pair:
            pieces = []
            for start in range(0, table.shape[1], width):
                slab = table[:, start : start + width]
                pieces.append((first, slab.shape))
                first += slab.shape[0]
                slabs.append(np.pad(slab, ((0, 0), (0, width - slab.shape[1]))))
            places.append(pieces)
    return np.concatenate(slabs, axis=0), places


def halves(value):
    high = value.astype(jnp.bfloat16)
    return high, (value - high.astype(jnp.float32)).astype(jnp.bfloat16)


def dot32(left, right):
    (lh, ll), (rh, rl) = left, right
    dot = functools.partial(jnp.dot, preferred_element_type=jnp.float32)
    return dot(lh, rh) + (dot(lh, rl) + dot(ll, rh))


def layout_kernel(x_ref, own_ref, y_ref, z_ref):
    _, far, _, part = own_ref.shape
    device = lax.axis_index("seq")
    places = {
        (0, 0): (own_ref, 0),
        (0, 1): (own_ref, 1),
        (1, 0): (y_ref, 0),
        (3, 0): (y_ref, 1),
        (1, 1): (y_ref, 2),
        (2, 1): (z_ref, 0),
        (3, 1): (z_ref, 1),
        (2, 0): (z_ref, 2),
    }
    for chip in range(far * SIDE):
        distance = (chip // SIDE) ^ (device // (2 * SIDE))
        near = (chip % SIDE) ^ ((device // 2) % SIDE)
        for core in range(2):
            first = (2 * chip + core) * part
            flip = (device % 2) ^ core
            for (side, cross), (out_ref, slot) in places.items():

                @pl.when((near == side) & (flip == cross))
                def _():
                    out_ref[slot, distance] = x_ref[:, first : first + part].astype(jnp.float32)


def project_kernel(scaling, x_ref, w_ref, taps_ref, go_ref, *refs):
    sig_ref, gates_ref, acc = refs[-3:]
    step = pl.program_id(0)
    product = jnp.dot(x_ref[...], w_ref[...], preferred_element_type=jnp.float32)

    @pl.when(step == 0)
    def _():
        acc[...] = product

    @pl.when(step > 0)
    def _():
        acc[...] += product

    @pl.when(step == pl.num_programs(0) - 1)
    def _():
        count, _, width, _ = sig_ref.shape
        channels = count * width
        projected = acc[...].astype(jnp.bfloat16).astype(jnp.float32).T
        query = projected[:channels]
        key = projected[channels : 2 * channels]
        value = projected[2 * channels :]
        go = go_ref[...].astype(jnp.float32).T
        signals = ((taps_ref[...] * scaling).T, key * value, go * query)
        for which, signal in enumerate(signals):
            for owner in range(count):
                sig_ref[owner, which] = signal[owner * width : (owner + 1) * width]
        for index, gate in enumerate((go, value, key)):
            gates_ref[index] = gate.astype(jnp.bfloat16)


def conv_kernel(places, x_ref, table_ref, turn_ref, *refs):
    y_ref, flat = refs[-2:]
    blocks, _, width, rows = x_ref.shape

    def table(which):
        slabs = [table_ref[at : at + shape[0], : shape[1]] for at, shape in places[which]]
        return slabs[0] if len(slabs) == 1 else jnp.concatenate(slabs, axis=1)

    m_h, m_l, f_h, f_l, i_h, i_l, u_h, u_l = [functools.partial(table, w) for w in range(8)]
    for p in range(blocks):
        for s in range(3):
            flat[p * width : (p + 1) * width, s * rows : (s + 1) * rows] = x_ref[p, s]
    turn_re, turn_im = turn_ref[:, :rows], turn_ref[:, rows:]
    count = turn_re.shape[0]
    mixed = dot32((m_h(), m_l()), halves(flat[...]))
    turned = []
    for s in range(3):
        re = mixed[:count, s * rows : (s + 1) * rows]
        im = mixed[count:, s * rows : (s + 1) * rows]
        turned.append(
            jnp.concatenate([re * turn_re + im * turn_im, im * turn_re - re * turn_im], axis=1)
        )
    spectrum = dot32(halves(jnp.concatenate(turned, axis=0)), (f_h(), f_l()))
    (k_re, k_im), (g_re, g_im), (b_re, b_im) = [
        (spectrum[s * count : (s + 1) * count, :rows], spectrum[s * count : (s + 1) * count, rows:])
        for s in range(3)
    ]
    products = jnp.concatenate(
        [
            jnp.concatenate([k_re * g_re - k_im * g_im, k_re * g_im + k_im * g_re], axis=1),
            jnp.concatenate([k_re * b_re + k_im * b_im, k_re * b_im - k_im * b_re], axis=1),
            jnp.concatenate([b_re * g_re + b_im * g_im, b_im * g_re - b_re * g_im], axis=1),
        ],
        axis=0,
    )
    back = dot32(halves(products), (i_h(), i_l()))
    parts_re, parts_im = [], []
    for s in range(3):
        re = back[s * count : (s + 1) * count, :rows]
        im = back[s * count : (s + 1) * count, rows:]
        parts_re.append(re * turn_re - im * turn_im)
        parts_im.append(im * turn_re + re * turn_im)
    stacked = jnp.concatenate(
        [jnp.concatenate(parts_re, axis=1), jnp.concatenate(parts_im, axis=1)], axis=0
    )
    result = dot32((u_h(), u_l()), halves(stacked))
    for p in range(blocks):
        for s in range(3):
            y_ref[p, s] = result[p * width : (p + 1) * width, s * rows : (s + 1) * rows]


def gate_kernel(scaling, y_ref, gates_ref, *refs):
    gp_ref, first_ref, rest_ref, taps_ref, flat = refs[-5:]
    count, _, width, _ = y_ref.shape
    channels = count * width
    for s in range(3):
        for owner in range(count):
            flat[s, owner * width : (owner + 1) * width] = y_ref[owner, s]
    for index in range(3):
        gate = gates_ref[index].astype(jnp.float32)
        rounded = (gate * flat[min(index, 1)]).T.astype(jnp.bfloat16)
        gp_ref[:, index * channels : (index + 1) * channels] = rounded
        if index == 0:
            first_ref[...] = rounded.astype(jnp.float32)
        else:
            span = slice((index - 1) * channels, index * channels)
            rest_ref[:, span] = rounded.astype(jnp.float32)
    taps_ref[...] = flat[2].T * scaling


def turn_blocks(sources, out_ref):
    for which, (x_ref, slot) in enumerate(sources):
        _, far, rows, part = x_ref.shape
        for f in range(far):
            out_ref[f * part : (f + 1) * part, which * rows : (which + 1) * rows] = x_ref[
                slot, f
            ].T.astype(jnp.bfloat16)


def turn_kernel(own_ref, y_ref, z_ref, out_own_ref, out_other_ref, relay_z_ref, relay_y_ref):
    relay_z_ref[0] = y_ref[1]
    relay_y_ref[0] = z_ref[1]
    turn_blocks(((own_ref, 0), (y_ref, 0), (z_ref, 2)), out_own_ref)
    turn_blocks(((own_ref, 1), (y_ref, 2), (z_ref, 0)), out_other_ref)


def corner_kernel(corner_own_ref, corner_other_ref, out_own_ref, out_other_ref):
    turn_blocks(((corner_own_ref, 0),), out_own_ref)
    turn_blocks(((corner_other_ref, 0),), out_other_ref)


def joined_columns(x_ref, corner_ref, span):
    return jnp.concatenate([x_ref[span], corner_ref[span]], axis=1)


def joined(gp_refs):
    return jnp.concatenate([gp_ref[...].astype(jnp.bfloat16) for gp_ref in gp_refs], axis=0)


def other_kernel(x_ref, corner_ref, *refs):
    gp_refs, out_ref = refs[:SIDE], refs[-1]
    columns = joined_columns(x_ref, corner_ref, slice(None))
    out_ref[...] = jnp.dot(columns, joined(gp_refs), preferred_element_type=jnp.float32)


def own_kernel(x_ref, corner_ref, *refs):
    gp_refs, add_ref, out_refs = refs[:SIDE], refs[SIDE], refs[SIDE + 1 :]
    gp = joined(gp_refs)
    part = out_refs[0].shape[0]
    for which, out_ref in enumerate(out_refs):
        span = slice(which * part, (which + 1) * part)
        columns = joined_columns(x_ref, corner_ref, span)
        product = jnp.dot(columns, gp, preferred_element_type=jnp.float32)
        out_ref[...] = product + add_ref[span]


def sum_kernel(scaling, groups, *refs):
    *in_refs, out_ref = refs
    terms = len(in_refs) // groups
    first = 0
    for group in range(groups):
        total = in_refs[group * terms][...]
        for in_ref in in_refs[group * terms + 1 : (group + 1) * terms]:
            total = total + in_ref[...]
        out_ref[:, first : first + total.shape[1]] = total * scaling
        first += total.shape[1]


def per_device(inputs, in_weight, filter_taps, grad_out):
    rows, depth = inputs.shape
    channels = filter_taps.shape[1]
    columns = in_weight.shape[1]
    blocks = lax.axis_size("seq")
    width = channels // blocks
    part = depth // blocks
    far = blocks // (2 * SIDE)
    chunk = min(1024, depth)
    steps = depth // chunk
    scaling = 1.0 / math.sqrt(rows * blocks)
    f32, bf16 = jnp.float32, jnp.bfloat16
    params = pltpu.CompilerParams(vmem_limit_bytes=VMEM_LIMIT)

    def shaped(*shape, dtype=f32):
        return jax.ShapeDtypeStruct(shape, dtype)

    def exchange(value, flip):
        return lax.ppermute(value, "seq", [(i, i ^ flip) for i in range(blocks)])

    anywhere = pl.BlockSpec(memory_space=pl.ANY)
    inside = pl.BlockSpec(memory_space=pltpu.VMEM)
    own, to_y, to_z = pl.pallas_call(
        layout_kernel,
        out_shape=[shaped(2, far, rows, part)] + [shaped(3, far, rows, part)] * 2,
        compiler_params=params,
    )(inputs)
    from_y, from_z = exchange(to_y, 2), exchange(to_z, 4)
    *turned, relay_z, relay_y = pl.pallas_call(
        turn_kernel,
        out_shape=[shaped(far * part, (SIDE - 1) * rows, dtype=bf16)] * 2
        + [shaped(1, far, rows, part)] * 2,
        compiler_params=params,
        cost_estimate=pl.CostEstimate(
            flops=0, bytes_accessed=200 * SIDE * far * rows * part, transcendentals=0
        ),
    )(own, from_y, from_z)
    corners = exchange(relay_z, 4), exchange(relay_y, 2)
    signals, gates = pl.pallas_call(
        functools.partial(project_kernel, scaling),
        grid=(steps,),
        in_specs=[
            pl.BlockSpec((rows, chunk), lambda i: (0, i)),
            pl.BlockSpec((chunk, columns), lambda i: (i, 0)),
            pl.BlockSpec((rows, channels), lambda i: (0, 0)),
            pl.BlockSpec((rows, channels), lambda i: (0, 0)),
        ],
        out_specs=[
            pl.BlockSpec((blocks, 3, width, rows), lambda i: (0, 0, 0, 0)),
            ]
        + [pl.BlockSpec((3, channels, rows), lambda i: (0, 0, 0))],
        out_shape=[shaped(blocks, 3, width, rows), shaped(3, channels, rows, dtype=bf16)],
        scratch_shapes=[pltpu.VMEM((rows, columns), f32)],
        compiler_params=params,
        cost_estimate=pl.CostEstimate(
            flops=2 * rows * depth * columns,
            bytes_accessed=2 * depth * (rows + columns),
            transcendentals=0,
        ),
    )(inputs, in_weight, filter_taps, grad_out)

    signals = lax.all_to_all(signals, "seq", split_axis=0, concat_axis=0, tiled=True)
    pairs, turn = transform_tables(blocks, width, rows)
    table, places = packed(pairs)
    results = pl.pallas_call(
        functools.partial(conv_kernel, places),
        in_specs=[inside] * 3 + [anywhere] * 2,
        out_shape=shaped(blocks, 3, width, rows),
        scratch_shapes=[pltpu.VMEM((blocks * width, 3 * rows), f32)],
        compiler_params=params,
    )(signals, jnp.asarray(table), jnp.asarray(turn), *turned)
    results = lax.all_to_all(results, "seq", split_axis=0, concat_axis=0, tiled=True)
    turned_corners = pl.pallas_call(
        corner_kernel,
        out_shape=[shaped(far * part, rows, dtype=bf16)] * 2,
        compiler_params=params,
        cost_estimate=pl.CostEstimate(
            flops=0, bytes_accessed=800 * SIDE * far * rows * part, transcendentals=0
        ),
    )(*corners)
    grad_proj, sent_first, sent_rest, grad_taps = pl.pallas_call(
        functools.partial(gate_kernel, scaling),
        in_specs=[inside] * 2 + [anywhere] * 2,
        out_shape=[
            shaped(rows, columns, dtype=bf16),
            shaped(rows, channels),
            shaped(rows, columns - channels),
            shaped(rows, channels),
        ],
        scratch_shapes=[pltpu.VMEM((3, channels, rows), f32)],
        compiler_params=params,
    )(results, gates, *turned_corners)
    grad_inputs = lax.dot_general(
        grad_proj, in_weight, (((1,), (1,)), ((), ())), preferred_element_type=f32
    ).astype(bf16)
    terms = []
    for block in (sent_first, sent_rest):
        cols = block.shape[1]
        gathered = [block] + [exchange(block, 2 * k) for k in range(1, SIDE)]
        cost = pl.CostEstimate(
            flops=2 * far * part * SIDE * rows * cols,
            bytes_accessed=4 * far * part * cols,
            transcendentals=0,
        )
        other = pl.pallas_call(
            other_kernel,
            in_specs=[inside] * (2 + SIDE) + [anywhere] * len(terms[1:]),
            out_shape=shaped(far * part, cols),
            compiler_params=params,
            cost_estimate=cost,
        )(turned[1], turned_corners[1], *gathered, *terms[1:])
        kept, *leaving = pl.pallas_call(
            own_kernel,
            out_shape=[shaped(part, cols)] * far,
            compiler_params=params,
            cost_estimate=cost,
        )(turned[0], turned_corners[0], *gathered, exchange(other, 1))
        terms += [kept] + [exchange(v, 2 * SIDE * (k + 1)) for k, v in enumerate(leaving)]
    grad_weight = pl.pallas_call(
        functools.partial(sum_kernel, scaling, 2),
        out_shape=shaped(part, columns),
        compiler_params=params,
    )(*terms)
    return grad_inputs, grad_weight, grad_taps


def solution(mesh):
    in_specs = (P(("grp", "seq"), None), P(), P("seq", None), P(("grp", "seq"), None))
    out_specs = (P(("grp", "seq"), None), P(("grp", "seq"), None), P(("grp", "seq"), None))
    return jax.shard_map(
        per_device, mesh=mesh, in_specs=in_specs, out_specs=out_specs, check_vma=False
    )
```

```python
import functools
import math

import jax
import jax.numpy as jnp
import numpy as np
from jax import lax
from jax.experimental import pallas as pl
from jax.experimental.pallas import tpu as pltpu
from jax.sharding import PartitionSpec as P

VMEM_LIMIT = 28 * 1024 * 1024
VMEM_STREAM = 57 * 1024 * 1024
SIDE = 4


def split_pair(table):
    high = table.astype(np.float32).astype(jnp.bfloat16)
    low = (table - high.astype(np.float64)).astype(np.float32).astype(jnp.bfloat16)
    return high, low


def transform_tables(blocks, width, rows):
    length = 2 * blocks * rows
    kept = blocks + 1
    padded = -(-kept * width // 16) * 16
    k1 = np.arange(kept)
    block = np.arange(blocks)
    angle = 2.0 * np.pi * ((k1[:, None] * block[None, :]) % (2 * blocks)) / (2 * blocks)
    eye = np.eye(width)

    def spread(matrix):
        wide = np.kron(matrix, eye)
        return np.pad(wide, ((0, padded - wide.shape[0]), (0, 0)))

    mix = np.concatenate([spread(np.cos(angle)), spread(-np.sin(angle))], axis=0)
    weight = np.where((k1 == 0) | (k1 == blocks), 1.0, 2.0)[:, None] / length
    unmix = np.concatenate(
        [spread(weight * np.cos(angle)), spread(-weight * np.sin(angle))], axis=0
    ).T
    row = np.arange(rows)
    turn = 2.0 * np.pi * ((k1[:, None] * row[None, :]) % length) / length
    turn = np.pad(np.repeat(turn, width, axis=0), ((0, padded - kept * width), (0, 0)))
    inner = 2.0 * np.pi * ((row[:, None] * row[None, :]) % rows) / rows
    cos, sin = np.cos(inner), np.sin(inner)
    forward = np.block([[cos, -sin], [sin, cos]])
    inverse = np.block([[cos, sin], [-sin, cos]])
    turn = np.concatenate([np.cos(turn), np.sin(turn)], axis=1).astype(np.float32)
    return [split_pair(matrix) for matrix in (mix, forward, inverse, unmix)], turn


def packed(tables):
    width = max(min(high.shape) for high, _ in tables)
    slabs, places, first = [], [], 0
    for pair in tables:
        for table in pair:
            pieces = []
            for start in range(0, table.shape[1], width):
                slab = table[:, start : start + width]
                pieces.append((first, slab.shape))
                first += slab.shape[0]
                slabs.append(np.pad(slab, ((0, 0), (0, width - slab.shape[1]))))
            places.append(pieces)
    return np.concatenate(slabs, axis=0), places


def halves(value):
    high = value.astype(jnp.bfloat16)
    return high, (value - high.astype(jnp.float32)).astype(jnp.bfloat16)


def dot32(left, right):
    (lh, ll), (rh, rl) = left, right
    dot = functools.partial(jnp.dot, preferred_element_type=jnp.float32)
    return dot(lh, rh) + (dot(lh, rl) + dot(ll, rh))


def layout_kernel(x_ref, own_ref, y_ref, z_ref):
    _, far, _, part = own_ref.shape
    device = lax.axis_index("seq")
    places = {
        (0, 0): (own_ref, 0),
        (0, 1): (own_ref, 1),
        (1, 0): (y_ref, 0),
        (3, 0): (y_ref, 1),
        (1, 1): (y_ref, 2),
        (2, 1): (z_ref, 0),
        (3, 1): (z_ref, 1),
        (2, 0): (z_ref, 2),
    }
    for chip in range(far * SIDE):
        distance = (chip // SIDE) ^ (device // (2 * SIDE))
        near = (chip % SIDE) ^ ((device // 2) % SIDE)
        for core in range(2):
            first = (2 * chip + core) * part
            flip = (device % 2) ^ core
            for (side, cross), (out_ref, slot) in places.items():

                @pl.when((near == side) & (flip == cross))
                def _():
                    out_ref[slot, distance] = x_ref[:, first : first + part].astype(jnp.float32)


def project_kernel(scaling, x_ref, w_ref, taps_ref, go_ref, *refs):
    sig_ref, gates_ref, acc = refs[-3:]
    step = pl.program_id(0)
    product = jnp.dot(x_ref[...], w_ref[...], preferred_element_type=jnp.float32)

    @pl.when(step == 0)
    def _():
        acc[...] = product

    @pl.when(step > 0)
    def _():
        acc[...] += product

    @pl.when(step == pl.num_programs(0) - 1)
    def _():
        count, _, width, _ = sig_ref.shape
        channels = count * width
        projected = acc[...].astype(jnp.bfloat16).astype(jnp.float32).T
        query = projected[:channels]
        key = projected[channels : 2 * channels]
        value = projected[2 * channels :]
        go = go_ref[...].astype(jnp.float32).T
        signals = ((taps_ref[...] * scaling).T, key * value, go * query)
        for which, signal in enumerate(signals):
            for owner in range(count):
                sig_ref[owner, which] = signal[owner * width : (owner + 1) * width]
        for index, gate in enumerate((go, value, key)):
            gates_ref[index] = gate.astype(jnp.bfloat16)


def conv_kernel(places, x_ref, table_ref, turn_ref, *refs):
    y_ref, taps_ref, flat = refs[-3:]
    blocks, _, width, rows = x_ref.shape

    def table(which):
        slabs = [table_ref[at : at + shape[0], : shape[1]] for at, shape in places[which]]
        return slabs[0] if len(slabs) == 1 else jnp.concatenate(slabs, axis=1)

    m_h, m_l, f_h, f_l, i_h, i_l, u_h, u_l = [functools.partial(table, w) for w in range(8)]
    for p in range(blocks):
        for s in range(3):
            flat[p * width : (p + 1) * width, s * rows : (s + 1) * rows] = x_ref[p, s]
    turn_re, turn_im = turn_ref[:, :rows], turn_ref[:, rows:]
    count = turn_re.shape[0]
    mixed = dot32((m_h(), m_l()), halves(flat[...]))
    turned = []
    for s in range(3):
        re = mixed[:count, s * rows : (s + 1) * rows]
        im = mixed[count:, s * rows : (s + 1) * rows]
        turned.append(
            jnp.concatenate([re * turn_re + im * turn_im, im * turn_re - re * turn_im], axis=1)
        )
    spectrum = dot32(halves(jnp.concatenate(turned, axis=0)), (f_h(), f_l()))
    (k_re, k_im), (g_re, g_im), (b_re, b_im) = [
        (spectrum[s * count : (s + 1) * count, :rows], spectrum[s * count : (s + 1) * count, rows:])
        for s in range(3)
    ]
    products = jnp.concatenate(
        [
            jnp.concatenate([k_re * g_re - k_im * g_im, k_re * g_im + k_im * g_re], axis=1),
            jnp.concatenate([k_re * b_re + k_im * b_im, k_re * b_im - k_im * b_re], axis=1),
            jnp.concatenate([b_re * g_re + b_im * g_im, b_im * g_re - b_re * g_im], axis=1),
        ],
        axis=0,
    )
    back = dot32(halves(products), (i_h(), i_l()))
    parts_re, parts_im = [], []
    for s in range(3):
        re = back[s * count : (s + 1) * count, :rows]
        im = back[s * count : (s + 1) * count, rows:]
        parts_re.append(re * turn_re - im * turn_im)
        parts_im.append(im * turn_re + re * turn_im)
    stacked = jnp.concatenate(
        [jnp.concatenate(parts_re, axis=1), jnp.concatenate(parts_im, axis=1)], axis=0
    )
    result = dot32((u_h(), u_l()), halves(stacked))
    for p in range(blocks):
        piece = result[p * width : (p + 1) * width]
        for s in range(2):
            y_ref[p, s] = piece[:, s * rows : (s + 1) * rows]
        taps_ref[p] = piece[:, 2 * rows :]


def taps_kernel(scaling, y_ref, taps_ref, flat):
    count, width, _ = y_ref.shape
    for owner in range(count):
        flat[owner * width : (owner + 1) * width] = y_ref[owner]
    taps_ref[...] = flat[...].T * scaling


def gate_kernel(y_ref, gates_ref, *refs):
    gp_ref, first_ref, rest_ref, flat = refs[-4:]
    count, _, width, _ = y_ref.shape
    channels = count * width
    for s in range(2):
        for owner in range(count):
            flat[s, owner * width : (owner + 1) * width] = y_ref[owner, s]
    for index in range(3):
        gate = gates_ref[index].astype(jnp.float32)
        rounded = (gate * flat[min(index, 1)]).T.astype(jnp.bfloat16)
        gp_ref[:, index * channels : (index + 1) * channels] = rounded
        if index == 0:
            first_ref[...] = rounded.astype(jnp.float32)
        else:
            span = slice((index - 1) * channels, index * channels)
            rest_ref[:, span] = rounded.astype(jnp.float32)


def turn_blocks(sources, out_ref):
    for which, (x_ref, slot) in enumerate(sources):
        _, far, rows, part = x_ref.shape
        for f in range(far):
            out_ref[f * part : (f + 1) * part, which * rows : (which + 1) * rows] = x_ref[
                slot, f
            ].T.astype(jnp.bfloat16)


def turn_kernel(own_ref, y_ref, z_ref, out_own_ref, out_other_ref, relay_z_ref, relay_y_ref):
    relay_z_ref[0] = y_ref[1]
    relay_y_ref[0] = z_ref[1]
    turn_blocks(((own_ref, 0), (y_ref, 0), (z_ref, 2)), out_own_ref)
    turn_blocks(((own_ref, 1), (y_ref, 2), (z_ref, 0)), out_other_ref)


def corner_kernel(corner_own_ref, corner_other_ref, out_own_ref, out_other_ref):
    turn_blocks(((corner_own_ref, 0),), out_own_ref)
    turn_blocks(((corner_other_ref, 0),), out_other_ref)


def joined_columns(x_ref, corner_ref, span):
    return jnp.concatenate([x_ref[span], corner_ref[span]], axis=1)


def joined(gp_refs):
    return jnp.concatenate([gp_ref[...].astype(jnp.bfloat16) for gp_ref in gp_refs], axis=0)


def other_kernel(x_ref, corner_ref, *refs):
    gp_refs, out_ref = refs[:SIDE], refs[-1]
    columns = joined_columns(x_ref, corner_ref, slice(None))
    out_ref[...] = jnp.dot(columns, joined(gp_refs), preferred_element_type=jnp.float32)


def own_kernel(x_ref, corner_ref, *refs):
    gp_refs, add_ref, out_refs = refs[:SIDE], refs[SIDE], refs[SIDE + 1 :]
    gp = joined(gp_refs)
    part = out_refs[0].shape[0]
    for which, out_ref in enumerate(out_refs):
        span = slice(which * part, (which + 1) * part)
        columns = joined_columns(x_ref, corner_ref, span)
        product = jnp.dot(columns, gp, preferred_element_type=jnp.float32)
        out_ref[...] = product + add_ref[span]


def sum_kernel(scaling, groups, *refs):
    *in_refs, out_ref = refs
    terms = len(in_refs) // groups
    first = 0
    for group in range(groups):
        total = in_refs[group * terms][...]
        for in_ref in in_refs[group * terms + 1 : (group + 1) * terms]:
            total = total + in_ref[...]
        out_ref[:, first : first + total.shape[1]] = total * scaling
        first += total.shape[1]


def per_device(inputs, in_weight, filter_taps, grad_out):
    rows, depth = inputs.shape
    channels = filter_taps.shape[1]
    columns = in_weight.shape[1]
    blocks = lax.axis_size("seq")
    width = channels // blocks
    part = depth // blocks
    far = blocks // (2 * SIDE)
    chunk = min(1024, depth)
    steps = depth // chunk
    scaling = 1.0 / math.sqrt(rows * blocks)
    f32, bf16 = jnp.float32, jnp.bfloat16
    params = pltpu.CompilerParams(vmem_limit_bytes=VMEM_LIMIT)

    def shaped(*shape, dtype=f32):
        return jax.ShapeDtypeStruct(shape, dtype)

    def exchange(value, flip):
        return lax.ppermute(value, "seq", [(i, i ^ flip) for i in range(blocks)])

    anywhere = pl.BlockSpec(memory_space=pl.ANY)
    inside = pl.BlockSpec(memory_space=pltpu.VMEM)
    own, to_y, to_z = pl.pallas_call(
        layout_kernel,
        out_shape=[shaped(2, far, rows, part)] + [shaped(3, far, rows, part)] * 2,
        compiler_params=params,
    )(inputs)
    from_y, from_z = exchange(to_y, 2), exchange(to_z, 4)
    *turned, relay_z, relay_y = pl.pallas_call(
        turn_kernel,
        out_shape=[shaped(far * part, (SIDE - 1) * rows, dtype=bf16)] * 2
        + [shaped(1, far, rows, part)] * 2,
        compiler_params=params,
        cost_estimate=pl.CostEstimate(
            flops=0, bytes_accessed=200 * SIDE * far * rows * part, transcendentals=0
        ),
    )(own, from_y, from_z)
    corners = exchange(relay_z, 4), exchange(relay_y, 2)
    signals, gates = pl.pallas_call(
        functools.partial(project_kernel, scaling),
        grid=(steps,),
        in_specs=[
            pl.BlockSpec((rows, chunk), lambda i: (0, i)),
            pl.BlockSpec((chunk, columns), lambda i: (i, 0)),
            pl.BlockSpec((rows, channels), lambda i: (0, 0)),
            pl.BlockSpec((rows, channels), lambda i: (0, 0)),
        ],
        out_specs=[
            pl.BlockSpec((blocks, 3, width, rows), lambda i: (0, 0, 0, 0)),
            ]
        + [pl.BlockSpec((3, channels, rows), lambda i: (0, 0, 0))],
        out_shape=[shaped(blocks, 3, width, rows), shaped(3, channels, rows, dtype=bf16)],
        scratch_shapes=[pltpu.VMEM((rows, columns), f32)],
        compiler_params=pltpu.CompilerParams(vmem_limit_bytes=VMEM_STREAM),
        cost_estimate=pl.CostEstimate(
            flops=2 * rows * depth * columns,
            bytes_accessed=2 * depth * (rows + columns),
            transcendentals=0,
        ),
    )(inputs, in_weight, filter_taps, grad_out)

    signals = lax.all_to_all(signals, "seq", split_axis=0, concat_axis=0, tiled=True)
    pairs, turn = transform_tables(blocks, width, rows)
    table, places = packed(pairs)
    results, taps = pl.pallas_call(
        functools.partial(conv_kernel, places),
        in_specs=[inside] * 3 + [anywhere] * 2,
        out_shape=[shaped(blocks, 2, width, rows), shaped(blocks, width, rows)],
        scratch_shapes=[pltpu.VMEM((blocks * width, 3 * rows), f32)],
        compiler_params=params,
    )(signals, jnp.asarray(table), jnp.asarray(turn), *turned)
    results = lax.all_to_all(results, "seq", split_axis=0, concat_axis=0, tiled=True)
    taps = lax.all_to_all(taps, "seq", split_axis=0, concat_axis=0, tiled=True)
    grad_taps = pl.pallas_call(
        functools.partial(taps_kernel, scaling),
        out_shape=shaped(rows, channels),
        scratch_shapes=[pltpu.VMEM((channels, rows), f32)],
        compiler_params=params,
    )(taps)
    turned_corners = pl.pallas_call(
        corner_kernel,
        out_shape=[shaped(far * part, rows, dtype=bf16)] * 2,
        compiler_params=params,
        cost_estimate=pl.CostEstimate(
            flops=0, bytes_accessed=800 * SIDE * far * rows * part, transcendentals=0
        ),
    )(*corners)
    grad_proj, sent_first, sent_rest = pl.pallas_call(
        gate_kernel,
        in_specs=[inside] * 2 + [anywhere] * 2,
        out_shape=[
            shaped(rows, columns, dtype=bf16),
            shaped(rows, channels),
            shaped(rows, columns - channels),
        ],
        scratch_shapes=[pltpu.VMEM((2, channels, rows), f32)],
        compiler_params=params,
    )(results, gates, *turned_corners)
    grad_inputs = lax.dot_general(
        grad_proj, in_weight, (((1,), (1,)), ((), ())), preferred_element_type=f32
    ).astype(bf16)
    terms = []
    for block in (sent_first, sent_rest):
        cols = block.shape[1]
        before = terms[1:] + [taps] if terms else []
        gathered = [block] + [exchange(block, 2 * k) for k in range(1, SIDE)]
        cost = pl.CostEstimate(
            flops=2 * far * part * SIDE * rows * cols,
            bytes_accessed=4 * far * part * cols,
            transcendentals=0,
        )
        other = pl.pallas_call(
            other_kernel,
            in_specs=[inside] * (2 + SIDE) + [anywhere] * len(before),
            out_shape=shaped(far * part, cols),
            compiler_params=params,
            cost_estimate=cost,
        )(turned[1], turned_corners[1], *gathered, *before)
        kept, *leaving = pl.pallas_call(
            own_kernel,
            out_shape=[shaped(part, cols)] * far,
            compiler_params=params,
            cost_estimate=cost,
        )(turned[0], turned_corners[0], *gathered, exchange(other, 1))
        terms += [kept] + [exchange(v, 2 * SIDE * (k + 1)) for k, v in enumerate(leaving)]
    grad_weight = pl.pallas_call(
        functools.partial(sum_kernel, scaling, 2),
        out_shape=shaped(part, columns),
        compiler_params=params,
    )(*terms)
    return grad_inputs, grad_weight, grad_taps


def solution(mesh):
    in_specs = (P(("grp", "seq"), None), P(), P("seq", None), P(("grp", "seq"), None))
    out_specs = (P(("grp", "seq"), None), P(("grp", "seq"), None), P(("grp", "seq"), None))
    return jax.shard_map(
        per_device, mesh=mesh, in_specs=in_specs, out_specs=out_specs, check_vma=False
    )
```

```python
import functools
import math

import jax
import jax.numpy as jnp
import numpy as np
from jax import lax
from jax.experimental import pallas as pl
from jax.experimental.pallas import tpu as pltpu
from jax.sharding import PartitionSpec as P

VMEM_LIMIT = 12 * 1024 * 1024
SIDE = 4


def split_pair(table):
    high = table.astype(np.float32).astype(jnp.bfloat16)
    low = (table - high.astype(np.float64)).astype(np.float32).astype(jnp.bfloat16)
    return high, low


def transform_tables(blocks, width, rows):
    length = 2 * blocks * rows
    kept = blocks + 1
    padded = -(-kept * width // 16) * 16
    k1 = np.arange(kept)
    block = np.arange(blocks)
    angle = 2.0 * np.pi * ((k1[:, None] * block[None, :]) % (2 * blocks)) / (2 * blocks)
    eye = np.eye(width)

    def spread(matrix):
        wide = np.kron(matrix, eye)
        return np.pad(wide, ((0, padded - wide.shape[0]), (0, 0)))

    mix = np.concatenate([spread(np.cos(angle)), spread(-np.sin(angle))], axis=0)
    weight = np.where((k1 == 0) | (k1 == blocks), 1.0, 2.0)[:, None] / length
    unmix = np.concatenate(
        [spread(weight * np.cos(angle)), spread(-weight * np.sin(angle))], axis=0
    ).T
    row = np.arange(rows)
    turn = 2.0 * np.pi * ((k1[:, None] * row[None, :]) % length) / length
    turn = np.pad(np.repeat(turn, width, axis=0), ((0, padded - kept * width), (0, 0)))
    inner = 2.0 * np.pi * ((row[:, None] * row[None, :]) % rows) / rows
    cos, sin = np.cos(inner), np.sin(inner)
    forward = np.block([[cos, -sin], [sin, cos]])
    inverse = np.block([[cos, sin], [-sin, cos]])
    turn = np.concatenate([np.cos(turn), np.sin(turn)], axis=1).astype(np.float32)
    return [split_pair(matrix) for matrix in (mix, forward, inverse, unmix)], turn


def packed(tables):
    width = max(min(high.shape) for high, _ in tables)
    slabs, places, first = [], [], 0
    for pair in tables:
        for table in pair:
            pieces = []
            for start in range(0, table.shape[1], width):
                slab = table[:, start : start + width]
                pieces.append((first, slab.shape))
                first += slab.shape[0]
                slabs.append(np.pad(slab, ((0, 0), (0, width - slab.shape[1]))))
            places.append(pieces)
    return np.concatenate(slabs, axis=0), places


def halves(value):
    high = value.astype(jnp.bfloat16)
    return high, (value - high.astype(jnp.float32)).astype(jnp.bfloat16)


def dot32(left, right):
    (lh, ll), (rh, rl) = left, right
    dot = functools.partial(jnp.dot, preferred_element_type=jnp.float32)
    return dot(lh, rh) + (dot(lh, rl) + dot(ll, rh))


def layout_kernel(x_ref, own_ref, y_ref, z_ref):
    _, far, _, part = own_ref.shape
    device = lax.axis_index("seq")
    places = {
        (0, 0): (own_ref, 0),
        (0, 1): (own_ref, 1),
        (1, 0): (y_ref, 0),
        (3, 0): (y_ref, 1),
        (1, 1): (y_ref, 2),
        (2, 1): (z_ref, 0),
        (3, 1): (z_ref, 1),
        (2, 0): (z_ref, 2),
    }
    for chip in range(far * SIDE):
        distance = (chip // SIDE) ^ (device // (2 * SIDE))
        near = (chip % SIDE) ^ ((device // 2) % SIDE)
        for core in range(2):
            first = (2 * chip + core) * part
            flip = (device % 2) ^ core
            for (side, cross), (out_ref, slot) in places.items():

                @pl.when((near == side) & (flip == cross))
                def _():
                    out_ref[slot, distance] = x_ref[:, first : first + part].astype(jnp.float32)


def project_kernel(scaling, x_ref, w_ref, taps_ref, go_ref, *refs):
    sig_ref, gates_ref, acc = refs[-3:]
    step = pl.program_id(0)
    product = jnp.dot(x_ref[...], w_ref[...], preferred_element_type=jnp.float32)

    @pl.when(step == 0)
    def _():
        acc[...] = product

    @pl.when(step > 0)
    def _():
        acc[...] += product

    @pl.when(step == pl.num_programs(0) - 1)
    def _():
        count, _, width, _ = sig_ref.shape
        channels = count * width
        projected = acc[...].astype(jnp.bfloat16).astype(jnp.float32).T
        query = projected[:channels]
        key = projected[channels : 2 * channels]
        value = projected[2 * channels :]
        go = go_ref[...].astype(jnp.float32).T
        signals = ((taps_ref[...] * scaling).T, key * value, go * query)
        for which, signal in enumerate(signals):
            for owner in range(count):
                sig_ref[owner, which] = signal[owner * width : (owner + 1) * width]
        for index, gate in enumerate((go, value, key)):
            gates_ref[index] = gate.astype(jnp.bfloat16)


def conv_kernel(places, x_ref, table_ref, turn_ref, *refs):
    y_ref, flat = refs[-2:]
    blocks, _, width, rows = x_ref.shape

    def table(which):
        slabs = [table_ref[at : at + shape[0], : shape[1]] for at, shape in places[which]]
        return slabs[0] if len(slabs) == 1 else jnp.concatenate(slabs, axis=1)

    m_h, m_l, f_h, f_l, i_h, i_l, u_h, u_l = [functools.partial(table, w) for w in range(8)]
    for p in range(blocks):
        for s in range(3):
            flat[p * width : (p + 1) * width, s * rows : (s + 1) * rows] = x_ref[p, s]
    turn_re, turn_im = turn_ref[:, :rows], turn_ref[:, rows:]
    count = turn_re.shape[0]
    mixed = dot32((m_h(), m_l()), halves(flat[...]))
    turned = []
    for s in range(3):
        re = mixed[:count, s * rows : (s + 1) * rows]
        im = mixed[count:, s * rows : (s + 1) * rows]
        turned.append(
            jnp.concatenate([re * turn_re + im * turn_im, im * turn_re - re * turn_im], axis=1)
        )
    spectrum = dot32(halves(jnp.concatenate(turned, axis=0)), (f_h(), f_l()))
    (k_re, k_im), (g_re, g_im), (b_re, b_im) = [
        (spectrum[s * count : (s + 1) * count, :rows], spectrum[s * count : (s + 1) * count, rows:])
        for s in range(3)
    ]
    products = jnp.concatenate(
        [
            jnp.concatenate([k_re * g_re - k_im * g_im, k_re * g_im + k_im * g_re], axis=1),
            jnp.concatenate([k_re * b_re + k_im * b_im, k_re * b_im - k_im * b_re], axis=1),
            jnp.concatenate([b_re * g_re + b_im * g_im, b_im * g_re - b_re * g_im], axis=1),
        ],
        axis=0,
    )
    back = dot32(halves(products), (i_h(), i_l()))
    parts_re, parts_im = [], []
    for s in range(3):
        re = back[s * count : (s + 1) * count, :rows]
        im = back[s * count : (s + 1) * count, rows:]
        parts_re.append(re * turn_re - im * turn_im)
        parts_im.append(im * turn_re + re * turn_im)
    stacked = jnp.concatenate(
        [jnp.concatenate(parts_re, axis=1), jnp.concatenate(parts_im, axis=1)], axis=0
    )
    result = dot32((u_h(), u_l()), halves(stacked))
    for p in range(blocks):
        for s in range(3):
            y_ref[p, s] = result[p * width : (p + 1) * width, s * rows : (s + 1) * rows]


def gate_kernel(scaling, y_ref, gates_ref, *refs):
    gp_ref, first_ref, rest_ref, taps_ref, flat = refs[-5:]
    count, _, width, _ = y_ref.shape
    channels = count * width
    for s in range(3):
        for owner in range(count):
            flat[s, owner * width : (owner + 1) * width] = y_ref[owner, s]
    for index in range(3):
        gate = gates_ref[index].astype(jnp.float32)
        rounded = (gate * flat[min(index, 1)]).T.astype(jnp.bfloat16)
        gp_ref[:, index * channels : (index + 1) * channels] = rounded
        if index == 0:
            first_ref[...] = rounded.astype(jnp.float32)
        else:
            span = slice((index - 1) * channels, index * channels)
            rest_ref[:, span] = rounded.astype(jnp.float32)
    taps_ref[...] = flat[2].T * scaling


def turn_blocks(sources, out_ref):
    for which, (x_ref, slot) in enumerate(sources):
        _, far, rows, part = x_ref.shape
        for f in range(far):
            out_ref[f * part : (f + 1) * part, which * rows : (which + 1) * rows] = x_ref[
                slot, f
            ].T.astype(jnp.bfloat16)


def turn_kernel(own_ref, y_ref, z_ref, out_own_ref, out_other_ref, relay_z_ref, relay_y_ref):
    relay_z_ref[0] = y_ref[1]
    relay_y_ref[0] = z_ref[1]
    turn_blocks(((own_ref, 0), (y_ref, 0), (z_ref, 2)), out_own_ref)
    turn_blocks(((own_ref, 1), (y_ref, 2), (z_ref, 0)), out_other_ref)


def corner_kernel(corner_own_ref, corner_other_ref, out_own_ref, out_other_ref):
    turn_blocks(((corner_own_ref, 0),), out_own_ref)
    turn_blocks(((corner_other_ref, 0),), out_other_ref)


def joined_columns(x_ref, corner_ref, span):
    return jnp.concatenate([x_ref[span], corner_ref[span]], axis=1)


def joined(gp_refs):
    return jnp.concatenate([gp_ref[...].astype(jnp.bfloat16) for gp_ref in gp_refs], axis=0)


def other_kernel(x_ref, corner_ref, *refs):
    gp_refs, out_ref = refs[:SIDE], refs[-1]
    columns = joined_columns(x_ref, corner_ref, slice(None))
    out_ref[...] = jnp.dot(columns, joined(gp_refs), preferred_element_type=jnp.float32)


def own_kernel(x_ref, corner_ref, *refs):
    gp_refs, add_ref, out_refs = refs[:SIDE], refs[SIDE], refs[SIDE + 1 :]
    gp = joined(gp_refs)
    part = out_refs[0].shape[0]
    for which, out_ref in enumerate(out_refs):
        span = slice(which * part, (which + 1) * part)
        columns = joined_columns(x_ref, corner_ref, span)
        product = jnp.dot(columns, gp, preferred_element_type=jnp.float32)
        out_ref[...] = product + add_ref[span]


def sum_kernel(scaling, groups, *refs):
    *in_refs, out_ref = refs
    terms = len(in_refs) // groups
    first = 0
    for group in range(groups):
        total = in_refs[group * terms][...]
        for in_ref in in_refs[group * terms + 1 : (group + 1) * terms]:
            total = total + in_ref[...]
        out_ref[:, first : first + total.shape[1]] = total * scaling
        first += total.shape[1]


def per_device(inputs, in_weight, filter_taps, grad_out):
    rows, depth = inputs.shape
    channels = filter_taps.shape[1]
    columns = in_weight.shape[1]
    blocks = lax.axis_size("seq")
    width = channels // blocks
    part = depth // blocks
    far = blocks // (2 * SIDE)
    chunk = min(1024, depth)
    steps = depth // chunk
    scaling = 1.0 / math.sqrt(rows * blocks)
    f32, bf16 = jnp.float32, jnp.bfloat16
    params = pltpu.CompilerParams(vmem_limit_bytes=VMEM_LIMIT)

    def shaped(*shape, dtype=f32):
        return jax.ShapeDtypeStruct(shape, dtype)

    def exchange(value, flip):
        return lax.ppermute(value, "seq", [(i, i ^ flip) for i in range(blocks)])

    anywhere = pl.BlockSpec(memory_space=pl.ANY)
    inside = pl.BlockSpec(memory_space=pltpu.VMEM)
    own, to_y, to_z = pl.pallas_call(
        layout_kernel,
        out_shape=[shaped(2, far, rows, part)] + [shaped(3, far, rows, part)] * 2,
        compiler_params=params,
    )(inputs)
    from_y, from_z = exchange(to_y, 2), exchange(to_z, 4)
    *turned, relay_z, relay_y = pl.pallas_call(
        turn_kernel,
        out_shape=[shaped(far * part, (SIDE - 1) * rows, dtype=bf16)] * 2
        + [shaped(1, far, rows, part)] * 2,
        compiler_params=params,
        cost_estimate=pl.CostEstimate(
            flops=0, bytes_accessed=200 * SIDE * far * rows * part, transcendentals=0
        ),
    )(own, from_y, from_z)
    corners = exchange(relay_z, 4), exchange(relay_y, 2)
    signals, gates = pl.pallas_call(
        functools.partial(project_kernel, scaling),
        grid=(steps,),
        in_specs=[
            pl.BlockSpec((rows, chunk), lambda i: (0, i)),
            pl.BlockSpec((chunk, columns), lambda i: (i, 0)),
            pl.BlockSpec((rows, channels), lambda i: (0, 0)),
            pl.BlockSpec((rows, channels), lambda i: (0, 0)),
        ],
        out_specs=[
            pl.BlockSpec((blocks, 3, width, rows), lambda i: (0, 0, 0, 0)),
            ]
        + [pl.BlockSpec((3, channels, rows), lambda i: (0, 0, 0))],
        out_shape=[shaped(blocks, 3, width, rows), shaped(3, channels, rows, dtype=bf16)],
        scratch_shapes=[pltpu.VMEM((rows, columns), f32)],
        compiler_params=params,
        cost_estimate=pl.CostEstimate(
            flops=2 * rows * depth * columns,
            bytes_accessed=2 * depth * (rows + columns),
            transcendentals=0,
        ),
    )(inputs, in_weight, filter_taps, grad_out)

    signals = lax.all_to_all(signals, "seq", split_axis=0, concat_axis=0, tiled=True)
    pairs, turn = transform_tables(blocks, width, rows)
    table, places = packed(pairs)
    results = pl.pallas_call(
        functools.partial(conv_kernel, places),
        in_specs=[inside] * 3 + [anywhere] * 2,
        out_shape=shaped(blocks, 3, width, rows),
        scratch_shapes=[pltpu.VMEM((blocks * width, 3 * rows), f32)],
        compiler_params=params,
    )(signals, jnp.asarray(table), jnp.asarray(turn), *turned)
    results = lax.all_to_all(results, "seq", split_axis=0, concat_axis=0, tiled=True)
    turned_corners = pl.pallas_call(
        corner_kernel,
        out_shape=[shaped(far * part, rows, dtype=bf16)] * 2,
        compiler_params=params,
        cost_estimate=pl.CostEstimate(
            flops=0, bytes_accessed=800 * SIDE * far * rows * part, transcendentals=0
        ),
    )(*corners)
    grad_proj, sent_first, sent_rest, grad_taps = pl.pallas_call(
        functools.partial(gate_kernel, scaling),
        in_specs=[inside] * 2 + [anywhere] * 2,
        out_shape=[
            shaped(rows, columns, dtype=bf16),
            shaped(rows, channels),
            shaped(rows, columns - channels),
            shaped(rows, channels),
        ],
        scratch_shapes=[pltpu.VMEM((3, channels, rows), f32)],
        compiler_params=params,
    )(results, gates, *turned_corners)
    grad_inputs = lax.dot_general(
        grad_proj, in_weight, (((1,), (1,)), ((), ())), preferred_element_type=f32
    ).astype(bf16)
    terms = []
    for block in (sent_first, sent_rest):
        cols = block.shape[1]
        gathered = [block] + [exchange(block, 2 * k) for k in range(1, SIDE)]
        cost = pl.CostEstimate(
            flops=2 * far * part * SIDE * rows * cols,
            bytes_accessed=4 * far * part * cols,
            transcendentals=0,
        )
        other = pl.pallas_call(
            other_kernel,
            in_specs=[inside] * (2 + SIDE) + [anywhere] * len(terms[1:]),
            out_shape=shaped(far * part, cols),
            compiler_params=params,
            cost_estimate=cost,
        )(turned[1], turned_corners[1], *gathered, *terms[1:])
        kept, *leaving = pl.pallas_call(
            own_kernel,
            out_shape=[shaped(part, cols)] * far,
            compiler_params=params,
            cost_estimate=cost,
        )(turned[0], turned_corners[0], *gathered, exchange(other, 1))
        terms += [kept] + [exchange(v, 2 * SIDE * (k + 1)) for k, v in enumerate(leaving)]
    grad_weight = pl.pallas_call(
        functools.partial(sum_kernel, scaling, 2),
        out_shape=shaped(part, columns),
        compiler_params=params,
    )(*terms)
    return grad_inputs, grad_weight, grad_taps


def solution(mesh):
    in_specs = (P(("grp", "seq"), None), P(), P("seq", None), P(("grp", "seq"), None))
    out_specs = (P(("grp", "seq"), None), P(("grp", "seq"), None), P(("grp", "seq"), None))
    return jax.shard_map(
        per_device, mesh=mesh, in_specs=in_specs, out_specs=out_specs, check_vma=False
    )
```

```python
import functools
import math

import jax
import jax.numpy as jnp
import numpy as np
from jax import lax
from jax.experimental import pallas as pl
from jax.experimental.pallas import tpu as pltpu
from jax.sharding import PartitionSpec as P

VMEM_LIMIT = 12 * 1024 * 1024
SIDE = 4


def split_pair(table):
    high = table.astype(np.float32).astype(jnp.bfloat16)
    low = (table - high.astype(np.float64)).astype(np.float32).astype(jnp.bfloat16)
    return high, low


def transform_tables(blocks, width, rows):
    length = 2 * blocks * rows
    kept = blocks + 1
    padded = -(-kept * width // 16) * 16
    k1 = np.arange(kept)
    block = np.arange(blocks)
    angle = 2.0 * np.pi * ((k1[:, None] * block[None, :]) % (2 * blocks)) / (2 * blocks)
    eye = np.eye(width)

    def spread(matrix):
        wide = np.kron(matrix, eye)
        return np.pad(wide, ((0, padded - wide.shape[0]), (0, 0)))

    mix = np.concatenate([spread(np.cos(angle)), spread(-np.sin(angle))], axis=0)
    weight = np.where((k1 == 0) | (k1 == blocks), 1.0, 2.0)[:, None] / length
    unmix = np.concatenate(
        [spread(weight * np.cos(angle)), spread(-weight * np.sin(angle))], axis=0
    ).T
    row = np.arange(rows)
    turn = 2.0 * np.pi * ((k1[:, None] * row[None, :]) % length) / length
    turn = np.pad(np.repeat(turn, width, axis=0), ((0, padded - kept * width), (0, 0)))
    inner = 2.0 * np.pi * ((row[:, None] * row[None, :]) % rows) / rows
    cos, sin = np.cos(inner), np.sin(inner)
    forward = np.block([[cos, -sin], [sin, cos]])
    inverse = np.block([[cos, sin], [-sin, cos]])
    turn = np.concatenate([np.cos(turn), np.sin(turn)], axis=1).astype(np.float32)
    return [split_pair(matrix) for matrix in (mix, forward, inverse, unmix)], turn


def packed(tables):
    width = max(min(high.shape) for high, _ in tables)
    slabs, places, first = [], [], 0
    for pair in tables:
        for table in pair:
            pieces = []
            for start in range(0, table.shape[1], width):
                slab = table[:, start : start + width]
                pieces.append((first, slab.shape))
                first += slab.shape[0]
                slabs.append(np.pad(slab, ((0, 0), (0, width - slab.shape[1]))))
            places.append(pieces)
    return np.concatenate(slabs, axis=0), places


def halves(value):
    high = value.astype(jnp.bfloat16)
    return high, (value - high.astype(jnp.float32)).astype(jnp.bfloat16)


def dot32(left, right):
    (lh, ll), (rh, rl) = left, right
    dot = functools.partial(jnp.dot, preferred_element_type=jnp.float32)
    return dot(lh, rh) + (dot(lh, rl) + dot(ll, rh))


def layout_kernel(x_ref, own_ref, y_ref, z_ref):
    _, far, _, part = own_ref.shape
    device = lax.axis_index("seq")
    places = {
        (0, 0): (own_ref, 0),
        (0, 1): (own_ref, 1),
        (1, 0): (y_ref, 0),
        (3, 0): (y_ref, 1),
        (1, 1): (y_ref, 2),
        (2, 1): (z_ref, 0),
        (3, 1): (z_ref, 1),
        (2, 0): (z_ref, 2),
    }
    for chip in range(far * SIDE):
        distance = (chip // SIDE) ^ (device // (2 * SIDE))
        near = (chip % SIDE) ^ ((device // 2) % SIDE)
        for core in range(2):
            first = (2 * chip + core) * part
            flip = (device % 2) ^ core
            for (side, cross), (out_ref, slot) in places.items():

                @pl.when((near == side) & (flip == cross))
                def _():
                    out_ref[slot, distance] = x_ref[:, first : first + part].astype(jnp.float32)


def project_kernel(scaling, x_ref, w_ref, taps_ref, go_ref, *refs):
    sig_ref, gates_ref, acc = refs[-3:]
    step = pl.program_id(0)
    product = jnp.dot(x_ref[...], w_ref[...], preferred_element_type=jnp.float32)

    @pl.when(step == 0)
    def _():
        acc[...] = product

    @pl.when(step > 0)
    def _():
        acc[...] += product

    @pl.when(step == pl.num_programs(0) - 1)
    def _():
        count, _, width, _ = sig_ref.shape
        channels = count * width
        projected = acc[...].astype(jnp.bfloat16).astype(jnp.float32).T
        query = projected[:channels]
        key = projected[channels : 2 * channels]
        value = projected[2 * channels :]
        go = go_ref[...].astype(jnp.float32).T
        signals = ((taps_ref[...] * scaling).T, key * value, go * query)
        for which, signal in enumerate(signals):
            for owner in range(count):
                sig_ref[owner, which] = signal[owner * width : (owner + 1) * width]
        for index, gate in enumerate((go, value, key)):
            gates_ref[index] = gate.astype(jnp.bfloat16)


def conv_kernel(places, x_ref, table_ref, turn_ref, *refs):
    y_ref, flat = refs[-2:]
    blocks, _, width, rows = x_ref.shape

    def table(which):
        slabs = [table_ref[at : at + shape[0], : shape[1]] for at, shape in places[which]]
        return slabs[0] if len(slabs) == 1 else jnp.concatenate(slabs, axis=1)

    m_h, m_l, f_h, f_l, i_h, i_l, u_h, u_l = [functools.partial(table, w) for w in range(8)]
    for p in range(blocks):
        for s in range(3):
            flat[p * width : (p + 1) * width, s * rows : (s + 1) * rows] = x_ref[p, s]
    turn_re, turn_im = turn_ref[:, :rows], turn_ref[:, rows:]
    count = turn_re.shape[0]
    mixed = dot32((m_h(), m_l()), halves(flat[...]))
    turned = []
    for s in range(3):
        re = mixed[:count, s * rows : (s + 1) * rows]
        im = mixed[count:, s * rows : (s + 1) * rows]
        turned.append(
            jnp.concatenate([re * turn_re + im * turn_im, im * turn_re - re * turn_im], axis=1)
        )
    spectrum = dot32(halves(jnp.concatenate(turned, axis=0)), (f_h(), f_l()))
    (k_re, k_im), (g_re, g_im), (b_re, b_im) = [
        (spectrum[s * count : (s + 1) * count, :rows], spectrum[s * count : (s + 1) * count, rows:])
        for s in range(3)
    ]
    products = jnp.concatenate(
        [
            jnp.concatenate([k_re * g_re - k_im * g_im, k_re * g_im + k_im * g_re], axis=1),
            jnp.concatenate([k_re * b_re + k_im * b_im, k_re * b_im - k_im * b_re], axis=1),
            jnp.concatenate([b_re * g_re + b_im * g_im, b_im * g_re - b_re * g_im], axis=1),
        ],
        axis=0,
    )
    back = dot32(halves(products), (i_h(), i_l()))
    parts_re, parts_im = [], []
    for s in range(3):
        re = back[s * count : (s + 1) * count, :rows]
        im = back[s * count : (s + 1) * count, rows:]
        parts_re.append(re * turn_re - im * turn_im)
        parts_im.append(im * turn_re + re * turn_im)
    stacked = jnp.concatenate(
        [jnp.concatenate(parts_re, axis=1), jnp.concatenate(parts_im, axis=1)], axis=0
    )
    result = dot32((u_h(), u_l()), halves(stacked))
    for p in range(blocks):
        for s in range(3):
            y_ref[p, s] = result[p * width : (p + 1) * width, s * rows : (s + 1) * rows]


def gate_kernel(scaling, y_ref, gates_ref, *refs):
    gp_ref, first_ref, rest_ref, taps_ref, flat = refs[-5:]
    count, _, width, _ = y_ref.shape
    channels = count * width
    for s in range(3):
        for owner in range(count):
            flat[s, owner * width : (owner + 1) * width] = y_ref[owner, s]
    for index in range(3):
        gate = gates_ref[index].astype(jnp.float32)
        rounded = (gate * flat[min(index, 1)]).T.astype(jnp.bfloat16)
        gp_ref[:, index * channels : (index + 1) * channels] = rounded
        if index == 0:
            first_ref[...] = rounded.astype(jnp.float32)
        else:
            span = slice((index - 1) * channels, index * channels)
            rest_ref[:, span] = rounded.astype(jnp.float32)
    taps_ref[...] = flat[2].T * scaling


def turn_blocks(sources, out_ref):
    for which, (x_ref, slot) in enumerate(sources):
        _, far, rows, part = x_ref.shape
        for f in range(far):
            out_ref[f * part : (f + 1) * part, which * rows : (which + 1) * rows] = x_ref[
                slot, f
            ].T.astype(jnp.bfloat16)


def turn_kernel(own_ref, y_ref, z_ref, *refs):
    out_own_ref, out_other_ref, relay_z_ref, relay_y_ref = refs[-4:]
    relay_z_ref[0] = y_ref[1]
    relay_y_ref[0] = z_ref[1]
    turn_blocks(((own_ref, 0), (y_ref, 0), (z_ref, 2)), out_own_ref)
    turn_blocks(((own_ref, 1), (y_ref, 2), (z_ref, 0)), out_other_ref)


def corner_kernel(corner_own_ref, corner_other_ref, out_own_ref, out_other_ref):
    turn_blocks(((corner_own_ref, 0),), out_own_ref)
    turn_blocks(((corner_other_ref, 0),), out_other_ref)


def joined_columns(x_ref, corner_ref, span):
    return jnp.concatenate([x_ref[span], corner_ref[span]], axis=1)


def joined(gp_refs):
    return jnp.concatenate([gp_ref[...].astype(jnp.bfloat16) for gp_ref in gp_refs], axis=0)


def other_kernel(x_ref, corner_ref, *refs):
    gp_refs, out_ref = refs[:SIDE], refs[-1]
    columns = joined_columns(x_ref, corner_ref, slice(None))
    out_ref[...] = jnp.dot(columns, joined(gp_refs), preferred_element_type=jnp.float32)


def own_kernel(x_ref, corner_ref, *refs):
    gp_refs, add_ref, out_refs = refs[:SIDE], refs[SIDE], refs[SIDE + 1 :]
    gp = joined(gp_refs)
    part = out_refs[0].shape[0]
    for which, out_ref in enumerate(out_refs):
        span = slice(which * part, (which + 1) * part)
        columns = joined_columns(x_ref, corner_ref, span)
        product = jnp.dot(columns, gp, preferred_element_type=jnp.float32)
        out_ref[...] = product + add_ref[span]


def sum_kernel(scaling, groups, *refs):
    *in_refs, out_ref = refs
    terms = len(in_refs) // groups
    first = 0
    for group in range(groups):
        total = in_refs[group * terms][...]
        for in_ref in in_refs[group * terms + 1 : (group + 1) * terms]:
            total = total + in_ref[...]
        out_ref[:, first : first + total.shape[1]] = total * scaling
        first += total.shape[1]


def per_device(inputs, in_weight, filter_taps, grad_out):
    rows, depth = inputs.shape
    channels = filter_taps.shape[1]
    columns = in_weight.shape[1]
    blocks = lax.axis_size("seq")
    width = channels // blocks
    part = depth // blocks
    far = blocks // (2 * SIDE)
    chunk = min(1024, depth)
    steps = depth // chunk
    scaling = 1.0 / math.sqrt(rows * blocks)
    f32, bf16 = jnp.float32, jnp.bfloat16
    params = pltpu.CompilerParams(vmem_limit_bytes=VMEM_LIMIT)

    def shaped(*shape, dtype=f32):
        return jax.ShapeDtypeStruct(shape, dtype)

    def exchange(value, flip):
        return lax.ppermute(value, "seq", [(i, i ^ flip) for i in range(blocks)])

    anywhere = pl.BlockSpec(memory_space=pl.ANY)
    inside = pl.BlockSpec(memory_space=pltpu.VMEM)
    own, to_y, to_z = pl.pallas_call(
        layout_kernel,
        out_shape=[shaped(2, far, rows, part)] + [shaped(3, far, rows, part)] * 2,
        compiler_params=params,
    )(inputs)
    from_y, from_z = exchange(to_y, 2), exchange(to_z, 4)
    pairs, turn = transform_tables(blocks, width, rows)
    table, places = packed(pairs)
    table, turn = jnp.asarray(table), jnp.asarray(turn)
    *turned, relay_z, relay_y = pl.pallas_call(
        turn_kernel,
        out_shape=[shaped(far * part, (SIDE - 1) * rows, dtype=bf16)] * 2
        + [shaped(1, far, rows, part)] * 2,
        compiler_params=params,
        cost_estimate=pl.CostEstimate(
            flops=0, bytes_accessed=200 * SIDE * far * rows * part, transcendentals=0
        ),
    )(own, from_y, from_z, table, turn)
    corners = exchange(relay_z, 4), exchange(relay_y, 2)
    signals, gates = pl.pallas_call(
        functools.partial(project_kernel, scaling),
        grid=(steps,),
        in_specs=[
            pl.BlockSpec((rows, chunk), lambda i: (0, i)),
            pl.BlockSpec((chunk, columns), lambda i: (i, 0)),
            pl.BlockSpec((rows, channels), lambda i: (0, 0)),
            pl.BlockSpec((rows, channels), lambda i: (0, 0)),
        ],
        out_specs=[
            pl.BlockSpec((blocks, 3, width, rows), lambda i: (0, 0, 0, 0)),
            ]
        + [pl.BlockSpec((3, channels, rows), lambda i: (0, 0, 0))],
        out_shape=[shaped(blocks, 3, width, rows), shaped(3, channels, rows, dtype=bf16)],
        scratch_shapes=[pltpu.VMEM((rows, columns), f32)],
        compiler_params=params,
        cost_estimate=pl.CostEstimate(
            flops=2 * rows * depth * columns,
            bytes_accessed=2 * depth * (rows + columns),
            transcendentals=0,
        ),
    )(inputs, in_weight, filter_taps, grad_out)

    signals = lax.all_to_all(signals, "seq", split_axis=0, concat_axis=0, tiled=True)
    results = pl.pallas_call(
        functools.partial(conv_kernel, places),
        in_specs=[inside] * 3 + [anywhere] * 2,
        out_shape=shaped(blocks, 3, width, rows),
        scratch_shapes=[pltpu.VMEM((blocks * width, 3 * rows), f32)],
        compiler_params=params,
    )(signals, table, turn, *turned)
    results = lax.all_to_all(results, "seq", split_axis=0, concat_axis=0, tiled=True)
    turned_corners = pl.pallas_call(
        corner_kernel,
        out_shape=[shaped(far * part, rows, dtype=bf16)] * 2,
        compiler_params=params,
        cost_estimate=pl.CostEstimate(
            flops=0, bytes_accessed=800 * SIDE * far * rows * part, transcendentals=0
        ),
    )(*corners)
    grad_proj, sent_first, sent_rest, grad_taps = pl.pallas_call(
        functools.partial(gate_kernel, scaling),
        in_specs=[inside] * 2 + [anywhere] * 2,
        out_shape=[
            shaped(rows, columns, dtype=bf16),
            shaped(rows, channels),
            shaped(rows, columns - channels),
            shaped(rows, channels),
        ],
        scratch_shapes=[pltpu.VMEM((3, channels, rows), f32)],
        compiler_params=params,
    )(results, gates, *turned_corners)
    grad_inputs = lax.dot_general(
        grad_proj, in_weight, (((1,), (1,)), ((), ())), preferred_element_type=f32
    ).astype(bf16)
    terms = []
    for block in (sent_first, sent_rest):
        cols = block.shape[1]
        gathered = [block] + [exchange(block, 2 * k) for k in range(1, SIDE)]
        cost = pl.CostEstimate(
            flops=2 * far * part * SIDE * rows * cols,
            bytes_accessed=4 * far * part * cols,
            transcendentals=0,
        )
        other = pl.pallas_call(
            other_kernel,
            in_specs=[inside] * (2 + SIDE) + [anywhere] * len(terms[1:]),
            out_shape=shaped(far * part, cols),
            compiler_params=params,
            cost_estimate=cost,
        )(turned[1], turned_corners[1], *gathered, *terms[1:])
        kept, *leaving = pl.pallas_call(
            own_kernel,
            out_shape=[shaped(part, cols)] * far,
            compiler_params=params,
            cost_estimate=cost,
        )(turned[0], turned_corners[0], *gathered, exchange(other, 1))
        terms += [kept] + [exchange(v, 2 * SIDE * (k + 1)) for k, v in enumerate(leaving)]
    grad_weight = pl.pallas_call(
        functools.partial(sum_kernel, scaling, 2),
        out_shape=shaped(part, columns),
        compiler_params=params,
    )(*terms)
    return grad_inputs, grad_weight, grad_taps


def solution(mesh):
    in_specs = (P(("grp", "seq"), None), P(), P("seq", None), P(("grp", "seq"), None))
    out_specs = (P(("grp", "seq"), None), P(("grp", "seq"), None), P(("grp", "seq"), None))
    return jax.shard_map(
        per_device, mesh=mesh, in_specs=in_specs, out_specs=out_specs, check_vma=False
    )
```

```python
import functools
import math

import jax
import jax.numpy as jnp
import numpy as np
from jax import lax
from jax.experimental import pallas as pl
from jax.experimental.pallas import tpu as pltpu
from jax.sharding import PartitionSpec as P

VMEM_LIMIT = 12 * 1024 * 1024
VMEM_STREAM = 52 * 1024 * 1024
SIDE = 4


def split_pair(table):
    high = table.astype(np.float32).astype(jnp.bfloat16)
    low = (table - high.astype(np.float64)).astype(np.float32).astype(jnp.bfloat16)
    return high, low


def transform_tables(blocks, width, rows):
    length = 2 * blocks * rows
    kept = blocks + 1
    padded = -(-kept * width // 16) * 16
    k1 = np.arange(kept)
    block = np.arange(blocks)
    angle = 2.0 * np.pi * ((k1[:, None] * block[None, :]) % (2 * blocks)) / (2 * blocks)
    eye = np.eye(width)

    def spread(matrix):
        wide = np.kron(matrix, eye)
        return np.pad(wide, ((0, padded - wide.shape[0]), (0, 0)))

    mix = np.concatenate([spread(np.cos(angle)), spread(-np.sin(angle))], axis=0)
    weight = np.where((k1 == 0) | (k1 == blocks), 1.0, 2.0)[:, None] / length
    unmix = np.concatenate(
        [spread(weight * np.cos(angle)), spread(-weight * np.sin(angle))], axis=0
    ).T
    row = np.arange(rows)
    turn = 2.0 * np.pi * ((k1[:, None] * row[None, :]) % length) / length
    turn = np.pad(np.repeat(turn, width, axis=0), ((0, padded - kept * width), (0, 0)))
    inner = 2.0 * np.pi * ((row[:, None] * row[None, :]) % rows) / rows
    cos, sin = np.cos(inner), np.sin(inner)
    forward = np.block([[cos, -sin], [sin, cos]])
    inverse = np.block([[cos, sin], [-sin, cos]])
    turn = np.concatenate([np.cos(turn), np.sin(turn)], axis=1).astype(np.float32)
    return [split_pair(matrix) for matrix in (mix, forward, inverse, unmix)], turn


def packed(tables):
    width = max(min(high.shape) for high, _ in tables)
    slabs, places, first = [], [], 0
    for pair in tables:
        for table in pair:
            pieces = []
            for start in range(0, table.shape[1], width):
                slab = table[:, start : start + width]
                pieces.append((first, slab.shape))
                first += slab.shape[0]
                slabs.append(np.pad(slab, ((0, 0), (0, width - slab.shape[1]))))
            places.append(pieces)
    return np.concatenate(slabs, axis=0), places


def halves(value):
    high = value.astype(jnp.bfloat16)
    return high, (value - high.astype(jnp.float32)).astype(jnp.bfloat16)


def dot32(left, right):
    (lh, ll), (rh, rl) = left, right
    dot = functools.partial(jnp.dot, preferred_element_type=jnp.float32)
    return dot(lh, rh) + (dot(lh, rl) + dot(ll, rh))


def layout_kernel(x_ref, own_ref, y_ref, z_ref):
    _, far, _, part = own_ref.shape
    device = lax.axis_index("seq")
    places = {
        (0, 0): (own_ref, 0),
        (0, 1): (own_ref, 1),
        (1, 0): (y_ref, 0),
        (3, 0): (y_ref, 1),
        (1, 1): (y_ref, 2),
        (2, 1): (z_ref, 0),
        (3, 1): (z_ref, 1),
        (2, 0): (z_ref, 2),
    }
    for chip in range(far * SIDE):
        distance = (chip // SIDE) ^ (device // (2 * SIDE))
        near = (chip % SIDE) ^ ((device // 2) % SIDE)
        for core in range(2):
            first = (2 * chip + core) * part
            flip = (device % 2) ^ core
            for (side, cross), (out_ref, slot) in places.items():

                @pl.when((near == side) & (flip == cross))
                def _():
                    out_ref[slot, distance] = x_ref[:, first : first + part].astype(jnp.float32)


def project_kernel(scaling, x_ref, w_ref, taps_ref, go_ref, *refs):
    sig_ref, gates_ref, acc = refs[-3:]
    step = pl.program_id(0)
    product = jnp.dot(x_ref[...], w_ref[...], preferred_element_type=jnp.float32)

    @pl.when(step == 0)
    def _():
        acc[...] = product

    @pl.when(step > 0)
    def _():
        acc[...] += product

    @pl.when(step == pl.num_programs(0) - 1)
    def _():
        count, _, width, _ = sig_ref.shape
        channels = count * width
        projected = acc[...].astype(jnp.bfloat16).astype(jnp.float32).T
        query = projected[:channels]
        key = projected[channels : 2 * channels]
        value = projected[2 * channels :]
        go = go_ref[...].astype(jnp.float32).T
        signals = ((taps_ref[...] * scaling).T, key * value, go * query)
        for which, signal in enumerate(signals):
            for owner in range(count):
                sig_ref[owner, which] = signal[owner * width : (owner + 1) * width]
        for index, gate in enumerate((go, value, key)):
            gates_ref[index] = gate.astype(jnp.bfloat16)


def conv_kernel(places, x_ref, table_ref, turn_ref, *refs):
    y_ref, flat = refs[-2:]
    blocks, _, width, rows = x_ref.shape

    def table(which):
        slabs = [table_ref[at : at + shape[0], : shape[1]] for at, shape in places[which]]
        return slabs[0] if len(slabs) == 1 else jnp.concatenate(slabs, axis=1)

    m_h, m_l, f_h, f_l, i_h, i_l, u_h, u_l = [functools.partial(table, w) for w in range(8)]
    for p in range(blocks):
        for s in range(3):
            flat[p * width : (p + 1) * width, s * rows : (s + 1) * rows] = x_ref[p, s]
    turn_re, turn_im = turn_ref[:, :rows], turn_ref[:, rows:]
    count = turn_re.shape[0]
    mixed = dot32((m_h(), m_l()), halves(flat[...]))
    turned = []
    for s in range(3):
        re = mixed[:count, s * rows : (s + 1) * rows]
        im = mixed[count:, s * rows : (s + 1) * rows]
        turned.append(
            jnp.concatenate([re * turn_re + im * turn_im, im * turn_re - re * turn_im], axis=1)
        )
    spectrum = dot32(halves(jnp.concatenate(turned, axis=0)), (f_h(), f_l()))
    (k_re, k_im), (g_re, g_im), (b_re, b_im) = [
        (spectrum[s * count : (s + 1) * count, :rows], spectrum[s * count : (s + 1) * count, rows:])
        for s in range(3)
    ]
    products = jnp.concatenate(
        [
            jnp.concatenate([k_re * g_re - k_im * g_im, k_re * g_im + k_im * g_re], axis=1),
            jnp.concatenate([k_re * b_re + k_im * b_im, k_re * b_im - k_im * b_re], axis=1),
            jnp.concatenate([b_re * g_re + b_im * g_im, b_im * g_re - b_re * g_im], axis=1),
        ],
        axis=0,
    )
    back = dot32(halves(products), (i_h(), i_l()))
    parts_re, parts_im = [], []
    for s in range(3):
        re = back[s * count : (s + 1) * count, :rows]
        im = back[s * count : (s + 1) * count, rows:]
        parts_re.append(re * turn_re - im * turn_im)
        parts_im.append(im * turn_re + re * turn_im)
    stacked = jnp.concatenate(
        [jnp.concatenate(parts_re, axis=1), jnp.concatenate(parts_im, axis=1)], axis=0
    )
    result = dot32((u_h(), u_l()), halves(stacked))
    for p in range(blocks):
        for s in range(3):
            y_ref[p, s] = result[p * width : (p + 1) * width, s * rows : (s + 1) * rows]


def gate_kernel(scaling, y_ref, gates_ref, *refs):
    gp_ref, first_ref, rest_ref, taps_ref, flat = refs[-5:]
    count, _, width, _ = y_ref.shape
    channels = count * width
    for s in range(3):
        for owner in range(count):
            flat[s, owner * width : (owner + 1) * width] = y_ref[owner, s]
    for index in range(3):
        gate = gates_ref[index].astype(jnp.float32)
        rounded = (gate * flat[min(index, 1)]).T.astype(jnp.bfloat16)
        gp_ref[:, index * channels : (index + 1) * channels] = rounded
        if index == 0:
            first_ref[...] = rounded.astype(jnp.float32)
        else:
            span = slice((index - 1) * channels, index * channels)
            rest_ref[:, span] = rounded.astype(jnp.float32)
    taps_ref[...] = flat[2].T * scaling


def turn_blocks(sources, out_ref):
    for which, (x_ref, slot) in enumerate(sources):
        _, far, rows, part = x_ref.shape
        for f in range(far):
            out_ref[f * part : (f + 1) * part, which * rows : (which + 1) * rows] = x_ref[
                slot, f
            ].T.astype(jnp.bfloat16)


def turn_kernel(own_ref, y_ref, z_ref, out_own_ref, out_other_ref, relay_z_ref, relay_y_ref):
    relay_z_ref[0] = y_ref[1]
    relay_y_ref[0] = z_ref[1]
    turn_blocks(((own_ref, 0), (y_ref, 0), (z_ref, 2)), out_own_ref)
    turn_blocks(((own_ref, 1), (y_ref, 2), (z_ref, 0)), out_other_ref)


def corner_kernel(corner_own_ref, corner_other_ref, out_own_ref, out_other_ref):
    turn_blocks(((corner_own_ref, 0),), out_own_ref)
    turn_blocks(((corner_other_ref, 0),), out_other_ref)


def joined_columns(x_ref, corner_ref, span):
    return jnp.concatenate([x_ref[span], corner_ref[span]], axis=1)


def joined(gp_refs):
    return jnp.concatenate([gp_ref[...].astype(jnp.bfloat16) for gp_ref in gp_refs], axis=0)


def other_kernel(x_ref, corner_ref, *refs):
    gp_refs, out_ref = refs[:SIDE], refs[-1]
    columns = joined_columns(x_ref, corner_ref, slice(None))
    out_ref[...] = jnp.dot(columns, joined(gp_refs), preferred_element_type=jnp.float32)


def own_kernel(x_ref, corner_ref, *refs):
    gp_refs, add_ref, out_refs = refs[:SIDE], refs[SIDE], refs[SIDE + 1 :]
    gp = joined(gp_refs)
    part = out_refs[0].shape[0]
    for which, out_ref in enumerate(out_refs):
        span = slice(which * part, (which + 1) * part)
        columns = joined_columns(x_ref, corner_ref, span)
        product = jnp.dot(columns, gp, preferred_element_type=jnp.float32)
        out_ref[...] = product + add_ref[span]


def sum_kernel(scaling, groups, *refs):
    *in_refs, out_ref = refs
    terms = len(in_refs) // groups
    first = 0
    for group in range(groups):
        total = in_refs[group * terms][...]
        for in_ref in in_refs[group * terms + 1 : (group + 1) * terms]:
            total = total + in_ref[...]
        out_ref[:, first : first + total.shape[1]] = total * scaling
        first += total.shape[1]


def per_device(inputs, in_weight, filter_taps, grad_out):
    rows, depth = inputs.shape
    channels = filter_taps.shape[1]
    columns = in_weight.shape[1]
    blocks = lax.axis_size("seq")
    width = channels // blocks
    part = depth // blocks
    far = blocks // (2 * SIDE)
    chunk = min(1024, depth)
    steps = depth // chunk
    scaling = 1.0 / math.sqrt(rows * blocks)
    f32, bf16 = jnp.float32, jnp.bfloat16
    params = pltpu.CompilerParams(vmem_limit_bytes=VMEM_LIMIT)

    def shaped(*shape, dtype=f32):
        return jax.ShapeDtypeStruct(shape, dtype)

    def exchange(value, flip):
        return lax.ppermute(value, "seq", [(i, i ^ flip) for i in range(blocks)])

    anywhere = pl.BlockSpec(memory_space=pl.ANY)
    inside = pl.BlockSpec(memory_space=pltpu.VMEM)
    own, to_y, to_z = pl.pallas_call(
        layout_kernel,
        out_shape=[shaped(2, far, rows, part)] + [shaped(3, far, rows, part)] * 2,
        compiler_params=params,
    )(inputs)
    from_y, from_z = exchange(to_y, 2), exchange(to_z, 4)
    *turned, relay_z, relay_y = pl.pallas_call(
        turn_kernel,
        out_shape=[shaped(far * part, (SIDE - 1) * rows, dtype=bf16)] * 2
        + [shaped(1, far, rows, part)] * 2,
        compiler_params=params,
        cost_estimate=pl.CostEstimate(
            flops=0, bytes_accessed=200 * SIDE * far * rows * part, transcendentals=0
        ),
    )(own, from_y, from_z)
    corners = exchange(relay_z, 4), exchange(relay_y, 2)
    signals, gates = pl.pallas_call(
        functools.partial(project_kernel, scaling),
        grid=(steps,),
        in_specs=[
            pl.BlockSpec((rows, chunk), lambda i: (0, i)),
            pl.BlockSpec((chunk, columns), lambda i: (i, 0)),
            pl.BlockSpec((rows, channels), lambda i: (0, 0)),
            pl.BlockSpec((rows, channels), lambda i: (0, 0)),
        ],
        out_specs=[
            pl.BlockSpec((blocks, 3, width, rows), lambda i: (0, 0, 0, 0)),
            ]
        + [pl.BlockSpec((3, channels, rows), lambda i: (0, 0, 0))],
        out_shape=[shaped(blocks, 3, width, rows), shaped(3, channels, rows, dtype=bf16)],
        scratch_shapes=[pltpu.VMEM((rows, columns), f32)],
        compiler_params=pltpu.CompilerParams(vmem_limit_bytes=VMEM_STREAM),
        cost_estimate=pl.CostEstimate(
            flops=2 * rows * depth * columns,
            bytes_accessed=2 * depth * (rows + columns),
            transcendentals=0,
        ),
    )(inputs, in_weight, filter_taps, grad_out)

    signals = lax.all_to_all(signals, "seq", split_axis=0, concat_axis=0, tiled=True)
    pairs, turn = transform_tables(blocks, width, rows)
    table, places = packed(pairs)
    results = pl.pallas_call(
        functools.partial(conv_kernel, places),
        in_specs=[inside] * 3 + [anywhere] * 2,
        out_shape=shaped(blocks, 3, width, rows),
        scratch_shapes=[pltpu.VMEM((blocks * width, 3 * rows), f32)],
        compiler_params=params,
    )(signals, jnp.asarray(table), jnp.asarray(turn), *turned)
    results = lax.all_to_all(results, "seq", split_axis=0, concat_axis=0, tiled=True)
    turned_corners = pl.pallas_call(
        corner_kernel,
        out_shape=[shaped(far * part, rows, dtype=bf16)] * 2,
        compiler_params=params,
        cost_estimate=pl.CostEstimate(
            flops=0, bytes_accessed=800 * SIDE * far * rows * part, transcendentals=0
        ),
    )(*corners)
    grad_proj, sent_first, sent_rest, grad_taps = pl.pallas_call(
        functools.partial(gate_kernel, scaling),
        in_specs=[inside] * 2 + [anywhere] * 2,
        out_shape=[
            shaped(rows, columns, dtype=bf16),
            shaped(rows, channels),
            shaped(rows, columns - channels),
            shaped(rows, channels),
        ],
        scratch_shapes=[pltpu.VMEM((3, channels, rows), f32)],
        compiler_params=params,
    )(results, gates, *turned_corners)
    grad_inputs = lax.dot_general(
        grad_proj, in_weight, (((1,), (1,)), ((), ())), preferred_element_type=f32
    ).astype(bf16)
    terms = []
    for block in (sent_first, sent_rest):
        cols = block.shape[1]
        gathered = [block] + [exchange(block, 2 * k) for k in range(1, SIDE)]
        cost = pl.CostEstimate(
            flops=2 * far * part * SIDE * rows * cols,
            bytes_accessed=4 * far * part * cols,
            transcendentals=0,
        )
        other = pl.pallas_call(
            other_kernel,
            in_specs=[inside] * (2 + SIDE) + [anywhere] * len(terms[1:]),
            out_shape=shaped(far * part, cols),
            compiler_params=params,
            cost_estimate=cost,
        )(turned[1], turned_corners[1], *gathered, *terms[1:])
        kept, *leaving = pl.pallas_call(
            own_kernel,
            out_shape=[shaped(part, cols)] * far,
            compiler_params=params,
            cost_estimate=cost,
        )(turned[0], turned_corners[0], *gathered, exchange(other, 1))
        terms += [kept] + [exchange(v, 2 * SIDE * (k + 1)) for k, v in enumerate(leaving)]
    grad_weight = pl.pallas_call(
        functools.partial(sum_kernel, scaling, 2),
        out_shape=shaped(part, columns),
        compiler_params=params,
    )(*terms)
    return grad_inputs, grad_weight, grad_taps


def solution(mesh):
    in_specs = (P(("grp", "seq"), None), P(), P("seq", None), P(("grp", "seq"), None))
    out_specs = (P(("grp", "seq"), None), P(("grp", "seq"), None), P(("grp", "seq"), None))
    return jax.shard_map(
        per_device, mesh=mesh, in_specs=in_specs, out_specs=out_specs, check_vma=False
    )
```

```python
import functools
import math

import jax
import jax.numpy as jnp
import numpy as np
from jax import lax
from jax.experimental import pallas as pl
from jax.experimental.pallas import tpu as pltpu
from jax.sharding import PartitionSpec as P

VMEM_LIMIT = 12 * 1024 * 1024
SIDE = 4


def split_pair(table):
    high = table.astype(np.float32).astype(jnp.bfloat16)
    low = (table - high.astype(np.float64)).astype(np.float32).astype(jnp.bfloat16)
    return high, low


def transform_tables(blocks, width, rows):
    length = 2 * blocks * rows
    kept = blocks + 1
    padded = -(-kept * width // 16) * 16
    k1 = np.arange(kept)
    block = np.arange(blocks)
    angle = 2.0 * np.pi * ((k1[:, None] * block[None, :]) % (2 * blocks)) / (2 * blocks)
    eye = np.eye(width)

    def spread(matrix):
        wide = np.kron(matrix, eye)
        return np.pad(wide, ((0, padded - wide.shape[0]), (0, 0)))

    mix = np.concatenate([spread(np.cos(angle)), spread(-np.sin(angle))], axis=0)
    weight = np.where((k1 == 0) | (k1 == blocks), 1.0, 2.0)[:, None] / length
    unmix = np.concatenate(
        [spread(weight * np.cos(angle)), spread(-weight * np.sin(angle))], axis=0
    ).T
    row = np.arange(rows)
    turn = 2.0 * np.pi * ((k1[:, None] * row[None, :]) % length) / length
    turn = np.pad(np.repeat(turn, width, axis=0), ((0, padded - kept * width), (0, 0)))
    inner = 2.0 * np.pi * ((row[:, None] * row[None, :]) % rows) / rows
    cos, sin = np.cos(inner), np.sin(inner)
    forward = np.block([[cos, -sin], [sin, cos]])
    inverse = np.block([[cos, sin], [-sin, cos]])
    turn = np.concatenate([np.cos(turn), np.sin(turn)], axis=1).astype(np.float32)
    return [split_pair(matrix) for matrix in (mix, forward, inverse, unmix)], turn


def packed(tables):
    width = max(min(high.shape) for high, _ in tables)
    slabs, places, first = [], [], 0
    for pair in tables:
        for table in pair:
            pieces = []
            for start in range(0, table.shape[1], width):
                slab = table[:, start : start + width]
                pieces.append((first, slab.shape))
                first += slab.shape[0]
                slabs.append(np.pad(slab, ((0, 0), (0, width - slab.shape[1]))))
            places.append(pieces)
    return np.concatenate(slabs, axis=0), places


def halves(value):
    high = value.astype(jnp.bfloat16)
    return high, (value - high.astype(jnp.float32)).astype(jnp.bfloat16)


def dot32(left, right):
    (lh, ll), (rh, rl) = left, right
    dot = functools.partial(jnp.dot, preferred_element_type=jnp.float32)
    return dot(lh, rh) + (dot(lh, rl) + dot(ll, rh))


def layout_kernel(x_ref, own_ref, y_ref, z_ref):
    _, far, _, part = own_ref.shape
    device = lax.axis_index("seq")
    places = {
        (0, 0): (own_ref, 0),
        (0, 1): (own_ref, 1),
        (1, 0): (y_ref, 0),
        (3, 0): (y_ref, 1),
        (1, 1): (y_ref, 2),
        (2, 1): (z_ref, 0),
        (3, 1): (z_ref, 1),
        (2, 0): (z_ref, 2),
    }
    for chip in range(far * SIDE):
        distance = (chip // SIDE) ^ (device // (2 * SIDE))
        near = (chip % SIDE) ^ ((device // 2) % SIDE)
        for core in range(2):
            first = (2 * chip + core) * part
            flip = (device % 2) ^ core
            for (side, cross), (out_ref, slot) in places.items():

                @pl.when((near == side) & (flip == cross))
                def _():
                    out_ref[slot, distance] = x_ref[:, first : first + part].astype(jnp.float32)


def project_kernel(scaling, x_ref, w_ref, taps_ref, go_ref, *refs):
    sig_ref, gates_ref, acc = refs[-3:]
    step = pl.program_id(0)
    product = jnp.dot(x_ref[...], w_ref[...], preferred_element_type=jnp.float32)

    @pl.when(step == 0)
    def _():
        acc[...] = product

    @pl.when(step > 0)
    def _():
        acc[...] += product

    @pl.when(step == pl.num_programs(0) - 1)
    def _():
        count, _, width, _ = sig_ref.shape
        channels = count * width
        projected = acc[...].astype(jnp.bfloat16).astype(jnp.float32).T
        query = projected[:channels]
        key = projected[channels : 2 * channels]
        value = projected[2 * channels :]
        go = go_ref[...].astype(jnp.float32).T
        signals = ((taps_ref[...] * scaling).T, key * value, go * query)
        for which, signal in enumerate(signals):
            for owner in range(count):
                sig_ref[owner, which] = signal[owner * width : (owner + 1) * width]
        for index, gate in enumerate((go, value, key)):
            gates_ref[index] = gate.astype(jnp.bfloat16)


def conv_kernel(places, x_ref, table_ref, turn_ref, *refs):
    y_ref, flat = refs[-2:]
    blocks, _, width, rows = x_ref.shape

    def table(which):
        slabs = [table_ref[at : at + shape[0], : shape[1]] for at, shape in places[which]]
        return slabs[0] if len(slabs) == 1 else jnp.concatenate(slabs, axis=1)

    m_h, m_l, f_h, f_l, i_h, i_l, u_h, u_l = [functools.partial(table, w) for w in range(8)]
    for p in range(blocks):
        for s in range(3):
            flat[p * width : (p + 1) * width, s * rows : (s + 1) * rows] = x_ref[p, s]
    turn_re, turn_im = turn_ref[:, :rows], turn_ref[:, rows:]
    count = turn_re.shape[0]
    mixed = dot32((m_h(), m_l()), halves(flat[...]))
    turned = []
    for s in range(3):
        re = mixed[:count, s * rows : (s + 1) * rows]
        im = mixed[count:, s * rows : (s + 1) * rows]
        turned.append(
            jnp.concatenate([re * turn_re + im * turn_im, im * turn_re - re * turn_im], axis=1)
        )
    spectrum = dot32(halves(jnp.concatenate(turned, axis=0)), (f_h(), f_l()))
    (k_re, k_im), (g_re, g_im), (b_re, b_im) = [
        (spectrum[s * count : (s + 1) * count, :rows], spectrum[s * count : (s + 1) * count, rows:])
        for s in range(3)
    ]
    products = jnp.concatenate(
        [
            jnp.concatenate([k_re * g_re - k_im * g_im, k_re * g_im + k_im * g_re], axis=1),
            jnp.concatenate([k_re * b_re + k_im * b_im, k_re * b_im - k_im * b_re], axis=1),
            jnp.concatenate([b_re * g_re + b_im * g_im, b_im * g_re - b_re * g_im], axis=1),
        ],
        axis=0,
    )
    back = dot32(halves(products), (i_h(), i_l()))
    parts_re, parts_im = [], []
    for s in range(3):
        re = back[s * count : (s + 1) * count, :rows]
        im = back[s * count : (s + 1) * count, rows:]
        parts_re.append(re * turn_re - im * turn_im)
        parts_im.append(im * turn_re + re * turn_im)
    stacked = jnp.concatenate(
        [jnp.concatenate(parts_re, axis=1), jnp.concatenate(parts_im, axis=1)], axis=0
    )
    result = dot32((u_h(), u_l()), halves(stacked))
    for p in range(blocks):
        for s in range(3):
            y_ref[p, s] = result[p * width : (p + 1) * width, s * rows : (s + 1) * rows]


def gate_kernel(scaling, y_ref, gates_ref, *refs):
    gp_ref, first_ref, rest_ref, taps_ref, flat = refs[-5:]
    count, _, width, _ = y_ref.shape
    channels = count * width
    for s in range(3):
        for owner in range(count):
            flat[s, owner * width : (owner + 1) * width] = y_ref[owner, s]
    for index in range(3):
        gate = gates_ref[index].astype(jnp.float32)
        rounded = (gate * flat[min(index, 1)]).T.astype(jnp.bfloat16)
        gp_ref[:, index * channels : (index + 1) * channels] = rounded
        if index == 0:
            first_ref[...] = rounded.astype(jnp.float32)
        else:
            span = slice((index - 1) * channels, index * channels)
            rest_ref[:, span] = rounded.astype(jnp.float32)
    taps_ref[...] = flat[2].T * scaling


def turn_blocks(sources, out_ref):
    for which, (x_ref, slot) in enumerate(sources):
        _, far, rows, part = x_ref.shape
        for f in range(far):
            out_ref[f * part : (f + 1) * part, which * rows : (which + 1) * rows] = x_ref[
                slot, f
            ].T.astype(jnp.bfloat16)


def turn_kernel(own_ref, y_ref, z_ref, out_own_ref, out_other_ref, relay_z_ref, relay_y_ref):
    relay_z_ref[0] = y_ref[1]
    relay_y_ref[0] = z_ref[1]
    turn_blocks(((own_ref, 0), (y_ref, 0), (z_ref, 2)), out_own_ref)
    turn_blocks(((own_ref, 1), (y_ref, 2), (z_ref, 0)), out_other_ref)


def corner_kernel(corner_own_ref, corner_other_ref, out_own_ref, out_other_ref):
    turn_blocks(((corner_own_ref, 0),), out_own_ref)
    turn_blocks(((corner_other_ref, 0),), out_other_ref)


def joined_columns(x_ref, corner_ref, span):
    return jnp.concatenate([x_ref[span], corner_ref[span]], axis=1)


def joined(gp_refs):
    return jnp.concatenate([gp_ref[...].astype(jnp.bfloat16) for gp_ref in gp_refs], axis=0)


def other_kernel(x_ref, corner_ref, *refs):
    gp_refs, out_ref = refs[:SIDE], refs[-1]
    columns = joined_columns(x_ref, corner_ref, slice(None))
    out_ref[...] = jnp.dot(columns, joined(gp_refs), preferred_element_type=jnp.float32)


def own_kernel(x_ref, corner_ref, *refs):
    gp_refs, add_ref, out_refs = refs[:SIDE], refs[SIDE], refs[SIDE + 1 :]
    gp = joined(gp_refs)
    part = out_refs[0].shape[0]
    for which, out_ref in enumerate(out_refs):
        span = slice(which * part, (which + 1) * part)
        columns = joined_columns(x_ref, corner_ref, span)
        product = jnp.dot(columns, gp, preferred_element_type=jnp.float32)
        out_ref[...] = product + add_ref[span]


def sum_kernel(scaling, groups, *refs):
    *in_refs, out_ref = refs
    terms = len(in_refs) // groups
    first = 0
    for group in range(groups):
        total = in_refs[group * terms][...]
        for in_ref in in_refs[group * terms + 1 : (group + 1) * terms]:
            total = total + in_ref[...]
        out_ref[:, first : first + total.shape[1]] = total * scaling
        first += total.shape[1]


def per_device(inputs, in_weight, filter_taps, grad_out):
    rows, depth = inputs.shape
    channels = filter_taps.shape[1]
    columns = in_weight.shape[1]
    blocks = lax.axis_size("seq")
    width = channels // blocks
    part = depth // blocks
    far = blocks // (2 * SIDE)
    chunk = min(1024, depth)
    steps = depth // chunk
    scaling = 1.0 / math.sqrt(rows * blocks)
    f32, bf16 = jnp.float32, jnp.bfloat16
    params = pltpu.CompilerParams(vmem_limit_bytes=VMEM_LIMIT)

    def shaped(*shape, dtype=f32):
        return jax.ShapeDtypeStruct(shape, dtype)

    def exchange(value, flip):
        return lax.ppermute(value, "seq", [(i, i ^ flip) for i in range(blocks)])

    anywhere = pl.BlockSpec(memory_space=pl.ANY)
    inside = pl.BlockSpec(memory_space=pltpu.VMEM)
    own, to_y, to_z = pl.pallas_call(
        layout_kernel,
        out_shape=[shaped(2, far, rows, part)] + [shaped(3, far, rows, part)] * 2,
        compiler_params=params,
    )(inputs)
    from_y, from_z = exchange(to_y, 2), exchange(to_z, 4)
    *turned, relay_z, relay_y = pl.pallas_call(
        turn_kernel,
        out_shape=[shaped(far * part, (SIDE - 1) * rows, dtype=bf16)] * 2
        + [shaped(1, far, rows, part)] * 2,
        compiler_params=params,
        cost_estimate=pl.CostEstimate(
            flops=0, bytes_accessed=200 * SIDE * far * rows * part, transcendentals=0
        ),
    )(own, from_y, from_z)
    corners = exchange(relay_z, 4), exchange(relay_y, 2)
    signals, gates = pl.pallas_call(
        functools.partial(project_kernel, scaling),
        grid=(steps,),
        in_specs=[
            pl.BlockSpec((rows, chunk), lambda i: (0, i)),
            pl.BlockSpec((chunk, columns), lambda i: (i, 0)),
            pl.BlockSpec((rows, channels), lambda i: (0, 0)),
            pl.BlockSpec((rows, channels), lambda i: (0, 0)),
        ],
        out_specs=[
            pl.BlockSpec((blocks, 3, width, rows), lambda i: (0, 0, 0, 0)),
            ]
        + [pl.BlockSpec((3, channels, rows), lambda i: (0, 0, 0))],
        out_shape=[shaped(blocks, 3, width, rows), shaped(3, channels, rows, dtype=bf16)],
        scratch_shapes=[pltpu.VMEM((rows, columns), f32)],
        compiler_params=params,
        cost_estimate=pl.CostEstimate(
            flops=2 * rows * depth * columns,
            bytes_accessed=2 * depth * (rows + columns),
            transcendentals=0,
        ),
    )(inputs, in_weight, filter_taps, grad_out)

    signals = lax.all_to_all(signals, "seq", split_axis=0, concat_axis=0, tiled=True)
    pairs, turn = transform_tables(blocks, width, rows)
    table, places = packed(pairs)
    results = pl.pallas_call(
        functools.partial(conv_kernel, places),
        in_specs=[inside] * 3 + [anywhere] * 3,
        out_shape=shaped(blocks, 3, width, rows),
        scratch_shapes=[pltpu.VMEM((blocks * width, 3 * rows), f32)],
        compiler_params=params,
    )(signals, jnp.asarray(table), jnp.asarray(turn), *turned, corners[0])
    results = lax.all_to_all(results, "seq", split_axis=0, concat_axis=0, tiled=True)
    turned_corners = pl.pallas_call(
        corner_kernel,
        out_shape=[shaped(far * part, rows, dtype=bf16)] * 2,
        compiler_params=params,
        cost_estimate=pl.CostEstimate(
            flops=0, bytes_accessed=800 * SIDE * far * rows * part, transcendentals=0
        ),
    )(*corners)
    grad_proj, sent_first, sent_rest, grad_taps = pl.pallas_call(
        functools.partial(gate_kernel, scaling),
        in_specs=[inside] * 2 + [anywhere] * 2,
        out_shape=[
            shaped(rows, columns, dtype=bf16),
            shaped(rows, channels),
            shaped(rows, columns - channels),
            shaped(rows, channels),
        ],
        scratch_shapes=[pltpu.VMEM((3, channels, rows), f32)],
        compiler_params=params,
    )(results, gates, *turned_corners)
    grad_inputs = lax.dot_general(
        grad_proj, in_weight, (((1,), (1,)), ((), ())), preferred_element_type=f32
    ).astype(bf16)
    terms = []
    for block in (sent_first, sent_rest):
        cols = block.shape[1]
        gathered = [block] + [exchange(block, 2 * k) for k in range(1, SIDE)]
        cost = pl.CostEstimate(
            flops=2 * far * part * SIDE * rows * cols,
            bytes_accessed=4 * far * part * cols,
            transcendentals=0,
        )
        other = pl.pallas_call(
            other_kernel,
            in_specs=[inside] * (2 + SIDE) + [anywhere] * len(terms[1:]),
            out_shape=shaped(far * part, cols),
            compiler_params=params,
            cost_estimate=cost,
        )(turned[1], turned_corners[1], *gathered, *terms[1:])
        kept, *leaving = pl.pallas_call(
            own_kernel,
            out_shape=[shaped(part, cols)] * far,
            compiler_params=params,
            cost_estimate=cost,
        )(turned[0], turned_corners[0], *gathered, exchange(other, 1))
        terms += [kept] + [exchange(v, 2 * SIDE * (k + 1)) for k, v in enumerate(leaving)]
    grad_weight = pl.pallas_call(
        functools.partial(sum_kernel, scaling, 2),
        out_shape=shaped(part, columns),
        compiler_params=params,
    )(*terms)
    return grad_inputs, grad_weight, grad_taps


def solution(mesh):
    in_specs = (P(("grp", "seq"), None), P(), P("seq", None), P(("grp", "seq"), None))
    out_specs = (P(("grp", "seq"), None), P(("grp", "seq"), None), P(("grp", "seq"), None))
    return jax.shard_map(
        per_device, mesh=mesh, in_specs=in_specs, out_specs=out_specs, check_vma=False
    )
```
